32 devices in a mesh: frame: 4 (over y, x), space: 8 (over z, core).
Axes of the slice: x: 2, y: 2, z: 4, core: 2. Of those that a mesh axis runs over, the one named last changes fastest.
Arguments:
- queries: bfloat16 [4096, 3072], P(('frame', 'space')), as said below
- keys: bfloat16 [4096, 3072], P(('frame', 'space')), as said below
- values: bfloat16 [4096, 3072], P(('frame', 'space')), may hold values from -5 to 5
- level_weight: float32 [3, 24, 4096], P(None, None, ('frame', 'space')), may hold values from 0.2 to 2
- frame_len: int32 [32, 4], P(('frame', 'space')), may hold values from 1 to 53, 128 in all within a row
- window_back: int32 [32, 4], P(('frame', 'space')), may hold values from 2 to 63
Outputs:
- mixed: bfloat16 [4096, 3072], P(('frame', 'space'))
The draws below stay inside these ranges and needn't reach their ends.
Inputs may be any that keep to these rules, and one draw needn't show every extreme that they name: `queries`: entries up to 60 in magnitude. `keys`: entries up to 4 in magnitude. `frame_len`: each row is the frame lengths of one device's 128 tokens, summing to 128; the longest frame of each row has exactly 53 tokens.
All inputs are finite; a program needn't handle non-finite values.
Results may differ from the reference program's by a relative error of at most 0.0085.
Values may be sent and summed in bfloat16 or wider, within the bound.
No kernel may reach another device: no remote copies, remote signals or barrier semaphores. Data moves between devices by JAX's collectives and lax.ppermute only.
A program may use at most 64 MiB of HBM per device.

```python
import math
import jax
import jax.numpy as jnp
import numpy as np
from jax import lax

HEADS = 24
HEAD_DIM = 128
TOK_DEV = 128
FRAMES = 4
LEV = 3
MAXF = 53
SHARDS = 32
TOKENS = 4096
N_FRAME = 4
N_SPACE = 8


def query_key_pair(key):
    base = jax.random.fold_in(key, 7301)
    query_key, key_key = jax.random.split(base, 2)
    shape = (TOKENS, HEADS * HEAD_DIM)
    queries = jnp.clip(jax.random.normal(query_key, shape, jnp.float32), -4.0, 4.0)
    keys = jnp.clip(jax.random.normal(key_key, shape, jnp.float32), -4.0, 4.0)
    return (queries, keys)


def draw_queries(key, part):
    return query_key_pair(key)[0].astype(jnp.bfloat16)


def draw_keys(key, part):
    return query_key_pair(key)[1].astype(jnp.bfloat16)


def with_ends(drawn, rng, least, largest):
    longest = drawn.shape.index(max(drawn.shape))
    spots = []
    for shift in (0, 1):
        where = [jax.random.randint(jax.random.fold_in(rng, axis), (), 0, length) for axis, length in enumerate(drawn.shape)]
        where[longest] = (where[longest] + shift) % drawn.shape[longest]
        spots.append(tuple(where))
    return drawn.at[spots[0]].set(least).at[spots[1]].set(largest)


def block_levels(own_key, shape, shards, low, top_value):
    gain, own = 1.0, jax.random.fold_in(own_key, 6)
    for dim, shards_of in shards:
        heights = jnp.exp(jax.random.uniform(jax.random.fold_in(own, dim), (shards_of,), jnp.float32, low / len(shards), top_value / len(shards)))
        gain = gain * jnp.repeat(heights, shape[dim] // shards_of).reshape([-1 if axis == dim else 1 for axis in range(len(shape))])
    return gain


def split_up(amount, total, limit, slope):
    loads = [(1 << 20) // math.isqrt(grade ** slope) + 1 for grade in range(2, amount + 1)]
    surplus, counts = total - limit - (amount - 1), [1] * (amount - 1)
    while surplus > 0:
        candidates = [i for i in range(amount - 1) if counts[i] < limit]
        mass, budget = sum([loads[i] for i in candidates]), surplus
        for i in candidates:
            addition = min(limit - counts[i], max(1, budget * loads[i] // mass), surplus)
            counts[i] = counts[i] + addition
            surplus = surplus - addition
    return np.array([limit] + counts)


def uneven_parts(stream_key, count, total, bound, slope):
    if count == 2:
        one = jax.random.randint(stream_key, (), max(1, total - bound), min(bound, total - 1) + 1)
        return jnp.stack([one, total - one])
    tallies = jnp.asarray(split_up(count, total, bound, slope), jnp.int32)
    couples = (count - 1) // 2
    giver, taker = tallies[1:1 + 2 * couples:2], tallies[2:2 + 2 * couples:2]
    margin = jnp.minimum(giver - 1, bound - taker)
    passed = jax.random.randint(jax.random.fold_in(stream_key, 1), (couples,), 0, 1 << 20) % (margin + 1)
    tallies = tallies.at[1:1 + 2 * couples:2].set(giver - passed).at[2:2 + 2 * couples:2].set(taker + passed)
    return tallies[jax.random.permutation(jax.random.fold_in(stream_key, 2), count)]


def bell_draw(key, shape, spread, most, cuts=(), kind=jnp.bfloat16):
    array = spread * jax.random.normal(key, shape, jnp.float32)
    if cuts:
        array = array * block_levels(key, shape, cuts, -0.22, 0.18)
    return jnp.clip(array, -most, most).astype(kind)


def setup_inputs(seed: int = 0) -> dict:
    splits = jax.random.split(jax.random.key(seed), 7)
    return {
        "queries": draw_queries(jax.random.fold_in(splits[6], 71), 0),
        "keys": draw_keys(jax.random.fold_in(splits[6], 71), 0),
        "values": bell_draw(splits[2], (TOKENS, HEADS * HEAD_DIM), 1.0, 5.0, ((0, 32),)),
        "level_weight": jnp.clip(jnp.exp(math.log(2.0) - 2.3025851 * jax.random.uniform(splits[3], (LEV, HEADS, TOKENS), jnp.float32) ** block_levels(splits[3], (LEV, HEADS, TOKENS), ((2, 32),), -0.2, 0.2)), 0.2, 2.0),
        "frame_len": jax.vmap(lambda own: uneven_parts(own, FRAMES, TOK_DEV, MAXF, 0))(jax.random.split(splits[4], SHARDS)).reshape((SHARDS, FRAMES)).astype(jnp.int32),
        "window_back": with_ends(jax.random.randint(splits[5], (SHARDS, FRAMES), 2, TOK_DEV // 2), jax.random.fold_in(splits[5], 1), 2, (TOK_DEV // 2) - 1).astype(jnp.int32),
    }


EPSILON = 1e-06

def unit_rows(matrix):
    return (matrix * lax.rsqrt(lax.optimization_barrier(jnp.mean(matrix * matrix, -1, keepdims=True)) + EPSILON)).astype(jnp.bfloat16)

def visible_mask(lengths, backward, count):
    lengths = lengths.astype(jnp.int32)
    backward = backward.astype(jnp.int32)
    starts = jnp.cumsum(lengths) - lengths
    lowest = jnp.maximum(starts - backward, 0)
    position = jnp.arange(count, dtype=jnp.int32)
    inside = (position[:, None] >= starts[None, :]).astype(jnp.int32)
    frame_of = lax.optimization_barrier(jnp.sum(inside, 1)) - 1
    onehot = frame_of[:, None] == jnp.arange(lengths.shape[0], dtype=jnp.int32)[None, :]
    floor_row = lax.optimization_barrier(jnp.sum(jnp.where(onehot, lowest[None, :], 0), 1))
    return (position[None, :] <= position[:, None]) & (position[None, :] >= floor_row[:, None])

def causal_mix(query_heads, key_heads, value_heads, visible, heads, head_dim):
    pieces = []
    for first_head in range(0, heads, 4):
        query_part = query_heads[:, first_head:first_head + 4].astype(jnp.float32)
        key_part = key_heads[:, first_head:first_head + 4].astype(jnp.float32)
        value_part = value_heads[:, first_head:first_head + 4].astype(jnp.float32)
        scores = jnp.einsum('thd,shd->hts', query_part, key_part) / math.sqrt(head_dim)
        scores = jnp.where(visible[None], scores, -jnp.inf)
        row_max = lax.optimization_barrier(jnp.max(scores, -1, keepdims=True))
        weights = jnp.exp(scores - row_max)
        totals = lax.optimization_barrier(jnp.sum(weights, -1))
        rounded = lax.optimization_barrier(weights.astype(jnp.bfloat16)).astype(jnp.float32)
        mixed_part = jnp.einsum('hts,shd->thd', rounded, value_part)
        pieces.append(mixed_part / jnp.transpose(totals)[:, :, None])
    return jnp.concatenate(pieces, 1)

def reference(queries, keys, values, level_weight, frame_len, window_back):
    block_tokens = TOK_DEV * N_SPACE
    key_blocks = keys.reshape(N_FRAME, block_tokens, HEADS, HEAD_DIM)
    value_blocks = values.reshape(N_FRAME, block_tokens, HEADS, HEAD_DIM)

    def block_state(pair):
        key_block, value_block = pair
        normal_k = unit_rows(key_block.astype(jnp.float32)).astype(jnp.float32)
        return jnp.einsum('thd,the->hde', normal_k, value_block.astype(jnp.float32))
    states = lax.map(block_state, (key_blocks, value_blocks))
    tree_depth = N_FRAME.bit_length() - 1
    per_block = []
    for frame_index in range(N_FRAME):
        per_level = []
        for level_index in range(tree_depth):
            lowest_block = frame_index >> level_index + 1 << level_index + 1
            if frame_index >> level_index & 1:
                per_level.append(lax.optimization_barrier(jnp.sum(states[lowest_block:lowest_block + 2 ** level_index], 0)))
            else:
                per_level.append(jnp.zeros_like(states[0]))
        per_block.append(jnp.stack(per_level))
    level_states = jnp.stack(per_block).astype(jnp.bfloat16)
    shard_ids = jnp.arange(SHARDS, dtype=jnp.int32)
    weights_by_shard = jnp.moveaxis(level_weight.reshape(LEV, HEADS, SHARDS, TOK_DEV), 2, 0)

    def one_shard(inputs):
        query_rows, key_rows, value_rows, weight_rows, lengths, backward, shard = inputs
        visible = visible_mask(lengths, backward, TOK_DEV)
        local_mix = causal_mix(query_rows, key_rows, value_rows, visible, HEADS, HEAD_DIM)
        result = local_mix * jnp.transpose(weight_rows[0])[:, :, None]
        normal_q = unit_rows(query_rows.astype(jnp.float32)).astype(jnp.float32)
        own_levels = lax.dynamic_index_in_dim(level_states, (shard // N_SPACE).astype(jnp.int32), 0, keepdims=False)
        for level_index in range(tree_depth):
            level_read = jnp.einsum('thd,hde->the', normal_q, own_levels[level_index].astype(jnp.float32))
            level_scale = 1.0 / math.sqrt(HEAD_DIM * 2 ** level_index * block_tokens)
            result = result + jnp.transpose(weight_rows[1 + level_index])[:, :, None] * (level_scale * level_read)
        return result.reshape(TOK_DEV, HEADS * HEAD_DIM).astype(jnp.bfloat16)
    outputs = lax.map(one_shard, (queries.reshape(SHARDS, TOK_DEV, HEADS, HEAD_DIM), keys.reshape(SHARDS, TOK_DEV, HEADS, HEAD_DIM), values.reshape(SHARDS, TOK_DEV, HEADS, HEAD_DIM), weights_by_shard, frame_len, window_back, shard_ids))
    return outputs.reshape(TOKENS, HEADS * HEAD_DIM)
```

```python
import functools
import math

import jax
import jax.numpy as jnp
from jax import lax
from jax.experimental import pallas as pl
from jax.experimental.pallas import tpu as pltpu
from jax.sharding import PartitionSpec as P

HEADS = 24
HEAD_DIM = 128
EPSILON = 1e-06
VMEM_LIMIT = 40 * 1024 * 1024

F32, BF16 = jnp.float32, jnp.bfloat16
WHOLE = pl.BlockSpec(memory_space=pltpu.VMEM)
SCALARS = pl.BlockSpec(memory_space=pltpu.SMEM)
PARAMS = pltpu.CompilerParams(vmem_limit_bytes=VMEM_LIMIT)


def inverse_rms(rows):
    return lax.rsqrt(jnp.mean(rows * rows, -1, keepdims=True) + EPSILON)


def columns(head):
    return pl.ds(pl.multiple_of(head * HEAD_DIM, HEAD_DIM), HEAD_DIM)


def state_kernel(first_ref, key_ref, value_ref, out_ref):
    for h in range(out_ref.shape[0] // HEAD_DIM):
        at = columns(first_ref[0] + h)
        key_rows = key_ref[:, at].astype(F32)
        normal = (key_rows * inverse_rms(key_rows)).astype(BF16)
        state = lax.dot_general(
            normal, value_ref[:, at], (((0,), (0,)), ((), ())), preferred_element_type=F32
        )
        out_ref[h * HEAD_DIM : (h + 1) * HEAD_DIM, :] = state.astype(out_ref.dtype)


def local_state(first_head, keys, values, heads, dtype):
    dim = HEAD_DIM
    rows = keys.shape[0]
    return pl.pallas_call(
        state_kernel,
        out_shape=jax.ShapeDtypeStruct((heads * dim, dim), dtype),
        in_specs=[SCALARS, WHOLE, WHOLE],
        out_specs=WHOLE,
        compiler_params=PARAMS,
        cost_estimate=pl.CostEstimate(
            flops=2 * heads * rows * dim * dim,
            bytes_accessed=6 * heads * rows * dim,
            transcendentals=heads * rows,
        ),
    )(first_head, keys, values)


def split_kernel(order_ref, mine_ref, other_ref, own_ref, *piece_refs):
    rows = own_ref.shape[0]
    for d, ref in enumerate((own_ref,) + piece_refs):
        at = pl.ds(pl.multiple_of(order_ref[d] * rows, rows), rows)
        ref[...] = (mine_ref[at, :] + other_ref[at, :].astype(F32)).astype(ref.dtype)


def split_pieces(order, mine, other, chips):
    rows = mine.shape[0] // chips
    shape = (rows, HEAD_DIM)
    return pl.pallas_call(
        split_kernel,
        out_shape=[jax.ShapeDtypeStruct(shape, F32)]
        + [jax.ShapeDtypeStruct(shape, BF16)] * (chips - 1),
        in_specs=[SCALARS, WHOLE, WHOLE],
        out_specs=[WHOLE] * chips,
        compiler_params=PARAMS,
    )(order, mine, other)


def local_kernel(
    length_ref, back_ref, scale_ref, query_ref, key_ref, value_ref, weight_ref, local_ref, read_ref
):
    tokens = query_ref.shape[0]
    levels = read_ref.shape[0]
    row = lax.broadcasted_iota(jnp.int32, (tokens, tokens), 0)
    col = lax.broadcasted_iota(jnp.int32, (tokens, tokens), 1)
    start = jnp.int32(0)
    floor = jnp.zeros((tokens, tokens), jnp.int32)
    for k in range(length_ref.shape[1]):
        lowest = jnp.maximum(start - back_ref[0, k], 0)
        floor = jnp.where(row >= start, lowest, floor)
        start = start + length_ref[0, k]
    visible = (col <= row) & (col >= floor)
    for h in range(HEADS):
        at = slice(h * HEAD_DIM, (h + 1) * HEAD_DIM)
        query = query_ref[:, at]
        scores = lax.dot_general(
            query, key_ref[:, at], (((1,), (1,)), ((), ())), preferred_element_type=F32
        ) * (1.0 / math.sqrt(HEAD_DIM))
        scores = jnp.where(visible, scores, -jnp.inf)
        weights = jnp.exp(scores - jnp.max(scores, -1, keepdims=True))
        total = jnp.sum(weights, -1, keepdims=True)
        mixed = jnp.dot(weights.astype(BF16), value_ref[:, at], preferred_element_type=F32)
        local_ref[:, at] = mixed * (weight_ref[:, h : h + 1] / total)
        query = query.astype(F32)
        inverse = inverse_rms(query)
        for level in range(levels):
            which = (1 + level) * HEADS + h
            gain = inverse * (weight_ref[:, which : which + 1] * scale_ref[level])
            read_ref[level, :, at] = (query * gain).astype(BF16)


def local_part(frame_len, window_back, scales, queries, keys, values, weights):
    tokens, width = queries.shape
    levels = scales.shape[0]
    return pl.pallas_call(
        local_kernel,
        out_shape=[
            jax.ShapeDtypeStruct((tokens, width), F32),
            jax.ShapeDtypeStruct((levels, tokens, width), BF16),
        ],
        in_specs=[SCALARS] * 3 + [WHOLE] * 4,
        out_specs=[WHOLE] * 2,
        compiler_params=PARAMS,
        cost_estimate=pl.CostEstimate(
            flops=4 * tokens * tokens * width,
            bytes_accessed=14 * tokens * width,
            transcendentals=tokens * tokens * HEADS,
        ),
    )(frame_len, window_back, scales, queries, keys, values, weights)


def read_kernel(levels, first_ref, local_ref, read_ref, *refs):
    out_ref, piece_refs = refs[-1], refs[:-1]
    count = len(piece_refs) // levels
    for piece in range(count):
        heads = piece_refs[piece * levels].shape[0] // HEAD_DIM
        for h in range(heads):
            at = columns(first_ref[piece] + h)
            rows = slice(h * HEAD_DIM, (h + 1) * HEAD_DIM)
            result = local_ref[:, at]
            for level in range(levels):
                result = result + jnp.dot(
                    read_ref[level, :, at],
                    piece_refs[piece * levels + level][rows, :],
                    preferred_element_type=F32,
                )
            out_ref[:, at] = result.astype(BF16)


def read_levels(first, local, reads, pieces, levels):
    tokens, width = local.shape
    return pl.pallas_call(
        functools.partial(read_kernel, levels),
        out_shape=jax.ShapeDtypeStruct((tokens, width), BF16),
        in_specs=[SCALARS] + [WHOLE] * (2 + len(pieces)),
        out_specs=WHOLE,
        compiler_params=PARAMS,
    )(first, local, reads, *pieces)


def body(frames, space, queries, keys, values, level_weight, frame_len, window_back):
    tokens = queries.shape[0]
    frame_pos = lax.axis_index("frame")
    space_pos = lax.axis_index("space")
    depth = frames.bit_length() - 1
    group = math.gcd(space, HEADS)
    group = group & -group
    chips = group // 2
    core = space_pos % 2
    chip = space_pos // 2 % chips
    half_heads = HEADS // 2
    piece_heads = half_heads // chips

    def across_space(array, mask):
        return lax.ppermute(array, "space", [(s, s ^ mask) for s in range(space)])

    def across(array, mask, keep):
        pairs = [
            (f * space + s, f * space + (s ^ mask))
            for f in range(frames)
            if keep(f)
            for s in range(space)
        ]
        return lax.ppermute(array, ("frame", "space"), pairs)

    mine_at = (core * half_heads).astype(jnp.int32).reshape(1)
    other_at = ((1 - core) * half_heads).astype(jnp.int32).reshape(1)
    useful = lambda f: f < frames - 1
    outgoing = local_state(other_at, keys, values, half_heads, BF16)
    incoming = across(outgoing, 1, useful)
    mine = local_state(mine_at, keys, values, half_heads, F32)
    order = jnp.stack([chip ^ d for d in range(chips)]).astype(jnp.int32)
    own, *sends = split_pieces(order, mine, incoming, chips)
    got = [across(sends[d - 1], 2 * d, useful) for d in range(1, chips)]
    total = own
    for piece in got:
        total = total + piece.astype(F32)
    mask = group
    while mask < space:
        total = total + across_space(total.astype(BF16), mask).astype(F32)
        mask *= 2

    pieces = []
    for level in range(depth):
        last = level == depth - 1
        step = 1 << level
        wanted = lambda f: f & step or (not last and f >> level + 1 != frames - 1 >> level + 1)
        pairs = [(f ^ step, f) for f in range(frames) if wanted(f)]
        received = lax.ppermute(total.astype(BF16), "frame", pairs)
        if not last:
            total = total + received.astype(F32)
        has = lambda f, step=step: bool(f & step)
        by_chip = [received] + [across(received, 2 * d, has) for d in range(1, chips)]
        pieces.append([(piece, across(piece, 1, has)) for piece in by_chip])

    scales = jnp.stack(
        [
            ((frame_pos >> level) & 1).astype(F32)
            / math.sqrt(HEAD_DIM * 2**level * tokens * space)
            for level in range(depth)
        ]
    )
    weights = level_weight.reshape(-1, tokens).T
    local, reads = local_part(frame_len, window_back, scales, queries, keys, values, weights)

    flat, first = [], []
    for d in range(chips):
        for c in range(2):
            first.append((core ^ c) * half_heads + (chip ^ d) * piece_heads)
            flat.extend(pieces[level][d][c] for level in range(depth))
    return read_levels(jnp.stack(first).astype(jnp.int32), local, reads, flat, depth)


def solution(mesh):
    rows = P(("frame", "space"), None)
    return jax.shard_map(
        functools.partial(body, mesh.shape["frame"], mesh.shape["space"]),
        mesh=mesh,
        in_specs=(rows, rows, rows, P(None, None, ("frame", "space")), rows, rows),
        out_specs=rows,
        check_vma=False,
    )
```

```python
import functools
import math

import jax
import jax.numpy as jnp
from jax import lax
from jax.experimental import pallas as pl
from jax.experimental.pallas import tpu as pltpu
from jax.sharding import Mesh, PartitionSpec as P

HEADS = 24
HEAD_DIM = 128
EPSILON = 1e-06
VMEM_LIMIT = 40 * 1024 * 1024

F32, BF16 = jnp.float32, jnp.bfloat16
WHOLE = pl.BlockSpec(memory_space=pltpu.VMEM)
SCALARS = pl.BlockSpec(memory_space=pltpu.SMEM)
IN_HBM = pl.BlockSpec(memory_space=pltpu.HBM)
PARAMS = pltpu.CompilerParams(vmem_limit_bytes=VMEM_LIMIT)


def inverse_rms(rows):
    return lax.rsqrt(jnp.mean(rows * rows, -1, keepdims=True) + EPSILON)


def columns(head, width=HEAD_DIM):
    return pl.ds(pl.multiple_of(head * width, width), width)


def state_kernel(chunk, first_ref, key_ref, value_ref, out_ref, keys, values, sems):
    heads = out_ref.shape[0] // HEAD_DIM
    copies = []
    for n, h in enumerate(range(0, heads, chunk)):
        width = chunk * HEAD_DIM
        source = pl.ds(pl.multiple_of((first_ref[0] + h) * HEAD_DIM, HEAD_DIM), width)
        target = pl.ds(h * HEAD_DIM, width)
        for s, (ref, held) in enumerate(((key_ref, keys), (value_ref, values))):
            copy = pltpu.make_async_copy(ref.at[:, source], held.at[:, target], sems.at[n, s])
            copy.start()
            copies.append(copy)
    for h in range(heads):
        if h % chunk == 0:
            copies[h // chunk * 2].wait()
            copies[h // chunk * 2 + 1].wait()
        at = slice(h * HEAD_DIM, (h + 1) * HEAD_DIM)
        key_rows = keys[:, at].astype(F32)
        normal = (key_rows * inverse_rms(key_rows)).astype(BF16)
        state = lax.dot_general(
            normal, values[:, at], (((0,), (0,)), ((), ())), preferred_element_type=F32
        )
        out_ref[at, :] = state.astype(out_ref.dtype)


def local_state(first_head, keys, values, heads, dtype):
    dim, rows = HEAD_DIM, keys.shape[0]
    chunk = math.gcd(heads, 3)
    held = pltpu.VMEM((rows, heads * dim), BF16)
    return pl.pallas_call(
        functools.partial(state_kernel, chunk),
        out_shape=jax.ShapeDtypeStruct((heads * dim, dim), dtype),
        in_specs=[SCALARS, IN_HBM, IN_HBM],
        out_specs=WHOLE,
        scratch_shapes=[held, held, pltpu.SemaphoreType.DMA((heads // chunk, 2))],
        compiler_params=pltpu.CompilerParams(vmem_limit_bytes=56 * 1024 * 1024),
        cost_estimate=pl.CostEstimate(
            flops=2 * heads * rows * dim * dim,
            bytes_accessed=6 * heads * rows * dim,
            transcendentals=heads * rows,
        ),
    )(first_head, keys, values)


def level_kernel(frames, sources, targets, part_ref, out_ref):
    depth = frames.bit_length() - 1
    rows = part_ref.shape[0] // (frames * sources)
    states = []
    for f in range(frames - 1):
        total = None
        for s in range(sources):
            start = (f * sources + s) * rows
            part = part_ref[start : start + rows, :].astype(F32)
            total = part if total is None else total + part
        states.append(total)
    zero = jnp.zeros((rows, HEAD_DIM), BF16)
    for f in range(frames):
        for level in range(depth):
            value = zero
            if f >> level & 1:
                first = f >> level + 1 << level + 1
                value = sum(states[first + 1 : first + 2**level], states[first]).astype(BF16)
            for t in range(targets):
                start = ((f * targets + t) * depth + level) * rows
                out_ref[start : start + rows, :] = value


def level_blocks(parts, frames, sources, targets):
    depth = frames.bit_length() - 1
    rows = parts.shape[0] // (frames * sources)
    return pl.pallas_call(
        functools.partial(level_kernel, frames, sources, targets),
        out_shape=jax.ShapeDtypeStruct((frames * targets * depth * rows, HEAD_DIM), BF16),
        in_specs=[WHOLE],
        out_specs=WHOLE,
        compiler_params=PARAMS,
    )(parts)


def local_kernel(
    length_ref, back_ref, scale_ref, query_ref, key_ref, value_ref, weight_ref, local_ref, read_ref
):
    tokens = query_ref.shape[0]
    levels = weight_ref.shape[0] - 1
    key_at = lax.broadcasted_iota(jnp.int32, (tokens, tokens), 0)
    query_at = lax.broadcasted_iota(jnp.int32, (tokens, tokens), 1)
    start = jnp.int32(0)
    floor = jnp.zeros((tokens, tokens), jnp.int32)
    for k in range(length_ref.shape[1]):
        lowest = jnp.maximum(start - back_ref[0, k], 0)
        floor = jnp.where(query_at >= start, lowest, floor)
        start = start + length_ref[0, k]
    hidden = jnp.where((key_at <= query_at) & (key_at >= floor), 0.0, -jnp.inf).astype(F32)
    scale = math.log2(math.e) / math.sqrt(HEAD_DIM)
    for h in range(HEADS):
        at = slice(h * HEAD_DIM, (h + 1) * HEAD_DIM)
        query = query_ref[:, at]
        scores = lax.dot_general(
            key_ref[:, at], query, (((1,), (1,)), ((), ())), preferred_element_type=F32
        )
        scores = scores * scale + hidden
        weights = jnp.exp2(scores - jnp.max(scores, 0, keepdims=True))
        total = jnp.sum(weights, 0, keepdims=True)
        weights = weights * (weight_ref[0, h : h + 1, :] / total)
        local_ref[:, at] = lax.dot_general(
            weights.astype(BF16), value_ref[:, at], (((0,), (0,)), ((), ())), preferred_element_type=F32
        )
        query = query.astype(F32).T
        inverse = lax.rsqrt(jnp.mean(query * query, 0, keepdims=True) + EPSILON)
        for level in range(levels):
            gain = inverse * (weight_ref[1 + level, h : h + 1, :] * scale_ref[level])
            first = (h * levels + level) * HEAD_DIM
            read_ref[:, first : first + HEAD_DIM] = (query * gain).T.astype(BF16)


def local_part(frame_len, window_back, scales, queries, keys, values, weights):
    tokens, width = queries.shape
    levels = scales.shape[0]
    return pl.pallas_call(
        local_kernel,
        out_shape=[
            jax.ShapeDtypeStruct((tokens, width), F32),
            jax.ShapeDtypeStruct((tokens, levels * width), BF16),
        ],
        in_specs=[SCALARS] * 3 + [WHOLE] * 4,
        out_specs=[WHOLE] * 2,
        compiler_params=PARAMS,
        cost_estimate=pl.CostEstimate(
            flops=4 * tokens * tokens * width,
            bytes_accessed=14 * tokens * width,
            transcendentals=tokens * tokens * HEADS,
        ),
    )(frame_len, window_back, scales, queries, keys, values, weights)


def read_kernel(levels, block, first_ref, local_ref, read_ref, *refs):
    out_ref, state_refs = refs[-1], refs[:-1]
    heads = HEADS // len(state_refs)
    for n, state_ref in enumerate(state_refs):
        for h in range(heads):
            rows = []
            for level in range(levels):
                row, end = h * HEAD_DIM, (h + 1) * HEAD_DIM
                while row < end:
                    stop = min(end, (row // block + 1) * block)
                    start = (row // block * levels + level) * block + row % block
                    rows.append(state_ref[start : start + stop - row, :])
                    row = stop
            head = first_ref[n] + h
            result = local_ref[:, columns(head)] + jnp.dot(
                read_ref[:, columns(head, levels * HEAD_DIM)],
                jnp.concatenate(rows, 0),
                preferred_element_type=F32,
            )
            out_ref[:, columns(head)] = result.astype(BF16)


def read_levels(first, local, reads, states, levels, block):
    tokens, width = local.shape
    return pl.pallas_call(
        functools.partial(read_kernel, levels, block),
        out_shape=jax.ShapeDtypeStruct((tokens, width), BF16),
        in_specs=[SCALARS] + [WHOLE] * (2 + len(states)),
        out_specs=WHOLE,
        compiler_params=PARAMS,
    )(first, local, reads, *states)


def body(sizes, queries, keys, values, level_weight, frame_len, window_back):
    frames, outer, chips = sizes
    tokens = queries.shape[0]
    frame_pos = lax.axis_index("frame")
    core = lax.axis_index("core").astype(jnp.int32)
    depth = frames.bit_length() - 1
    half = HEADS // 2
    first = jnp.stack([core * half, (1 - core) * half])

    outgoing = local_state(first[1:], keys, values, half, BF16)
    incoming = lax.ppermute(outgoing, "core", [(0, 1), (1, 0)])
    mine = local_state(first[:1], keys, values, half, F32)
    chip_sum = (mine + incoming.astype(F32)).astype(BF16)
    parts = lax.all_to_all(chip_sum, ("frame", "chip"), 0, 0, tiled=True)
    block = parts.shape[0] // (frames * chips)
    sources = chips
    if outer > 1:
        parts = parts.astype(F32).reshape(frames, chips, block, HEAD_DIM).sum(1)
        parts = lax.psum(parts, "outer").reshape(frames * block, HEAD_DIM)
        sources = 1
    blocks = level_blocks(parts, frames, sources, chips)
    own = lax.all_to_all(blocks, ("frame", "chip"), 0, 0, tiled=True)
    other = lax.ppermute(own, "core", [(0, 1), (1, 0)])

    scales = jnp.stack(
        [
            (frame_pos >> level & 1).astype(F32)
            / math.sqrt(HEAD_DIM * 2**level * tokens * outer * chips * 2)
            for level in range(depth)
        ]
    )
    local, reads = local_part(frame_len, window_back, scales, queries, keys, values, level_weight)
    return read_levels(first, local, reads, (own, other), depth, block)


def solution(mesh):
    frames, space = mesh.shape["frame"], mesh.shape["space"]
    chips = 1
    while HEADS * HEAD_DIM // 2 % (frames * chips * 2 * 32) == 0 and space % (chips * 4) == 0 and chips < 4:
        chips *= 2
    sizes = (frames, space // (2 * chips), chips)
    names = ("frame", "outer", "chip", "core")
    fine = Mesh(mesh.devices.reshape(sizes + (2,)), names)
    rows = P(names, None)
    return jax.shard_map(
        functools.partial(body, sizes),
        mesh=fine,
        in_specs=(rows, rows, rows, P(None, None, names), rows, rows),
        out_specs=rows,
        check_vma=False,
    )
```

```python
import functools
import math

import jax
import jax.numpy as jnp
from jax import lax
from jax.experimental import pallas as pl
from jax.experimental.pallas import tpu as pltpu
from jax.sharding import Mesh, PartitionSpec as P

HEADS = 24
HEAD_DIM = 128
EPSILON = 1e-06
VMEM_LIMIT = 40 * 1024 * 1024

F32, BF16 = jnp.float32, jnp.bfloat16
WHOLE = pl.BlockSpec(memory_space=pltpu.VMEM)
SCALARS = pl.BlockSpec(memory_space=pltpu.SMEM)
IN_HBM = pl.BlockSpec(memory_space=pltpu.HBM)
PARAMS = pltpu.CompilerParams(vmem_limit_bytes=VMEM_LIMIT)


def inverse_rms(rows):
    return lax.rsqrt(jnp.mean(rows * rows, -1, keepdims=True) + EPSILON)


def columns(head, width=HEAD_DIM):
    return pl.ds(pl.multiple_of(head * width, width), width)


def state_kernel(chunk, first_ref, key_ref, value_ref, out_ref, keys, values, sems):
    heads = out_ref.shape[0] // HEAD_DIM
    copies = []
    for n, h in enumerate(range(0, heads, chunk)):
        width = chunk * HEAD_DIM
        source = pl.ds(pl.multiple_of((first_ref[0] + h) * HEAD_DIM, HEAD_DIM), width)
        target = pl.ds(h * HEAD_DIM, width)
        for s, (ref, held) in enumerate(((key_ref, keys), (value_ref, values))):
            copy = pltpu.make_async_copy(ref.at[:, source], held.at[:, target], sems.at[n, s])
            copy.start()
            copies.append(copy)
    for h in range(heads):
        if h % chunk == 0:
            copies[h // chunk * 2].wait()
            copies[h // chunk * 2 + 1].wait()
        at = slice(h * HEAD_DIM, (h + 1) * HEAD_DIM)
        key_rows = keys[:, at].astype(F32)
        normal = (key_rows * inverse_rms(key_rows)).astype(BF16)
        state = lax.dot_general(
            normal, values[:, at], (((0,), (0,)), ((), ())), preferred_element_type=F32
        )
        out_ref[at, :] = state.astype(out_ref.dtype)


def local_state(first_head, keys, values, heads, dtype):
    dim, rows = HEAD_DIM, keys.shape[0]
    chunk = math.gcd(heads, 3)
    held = pltpu.VMEM((rows, heads * dim), BF16)
    keys, values = (pltpu.with_memory_space_constraint(x, pltpu.HBM) for x in (keys, values))
    return pl.pallas_call(
        functools.partial(state_kernel, chunk),
        out_shape=pltpu.VMEM((heads * dim, dim), dtype),
        in_specs=[SCALARS, IN_HBM, IN_HBM],
        out_specs=WHOLE,
        scratch_shapes=[held, held, pltpu.SemaphoreType.DMA((heads // chunk, 2))],
        compiler_params=PARAMS,
        cost_estimate=pl.CostEstimate(
            flops=2 * heads * rows * dim * dim,
            bytes_accessed=6 * heads * rows * dim,
            transcendentals=heads * rows,
        ),
    )(first_head, keys, values)


def piece_kernel(order_ref, mine_ref, other_ref, own_ref, *piece_refs):
    rows = own_ref.shape[0]
    for d, ref in enumerate((own_ref,) + piece_refs):
        at = pl.ds(pl.multiple_of(order_ref[d] * rows, rows), rows)
        ref[...] = (mine_ref[at, :] + other_ref[at, :].astype(F32)).astype(ref.dtype)


def chip_pieces(order, mine, other, chips):
    shape = (mine.shape[0] // chips, HEAD_DIM)
    return pl.pallas_call(
        piece_kernel,
        out_shape=[jax.ShapeDtypeStruct(shape, F32)]
        + [jax.ShapeDtypeStruct(shape, BF16)] * (chips - 1),
        in_specs=[SCALARS, WHOLE, WHOLE],
        out_specs=[WHOLE] * chips,
        compiler_params=PARAMS,
    )(order, mine, other)


def sum_kernel(after_ref, own_ref, *refs):
    total = own_ref[...]
    for ref in refs[:-1]:
        total = total + ref[...].astype(F32)
    refs[-1][...] = total.astype(refs[-1].dtype)


def sum_pieces(after, own, parts, dtype):
    return pl.pallas_call(
        sum_kernel,
        out_shape=jax.ShapeDtypeStruct(own.shape, dtype),
        in_specs=[pl.BlockSpec(memory_space=pl.ANY)] + [WHOLE] * (1 + len(parts)),
        out_specs=WHOLE,
        compiler_params=PARAMS,
    )(after, own, *parts)


def local_kernel(
    length_ref, back_ref, coef_ref, query_ref, key_ref, value_ref, weight_ref, after_ref, local_ref, *read_refs
):
    tokens = query_ref.shape[0]
    levels = weight_ref.shape[0] - 1
    key_at = lax.broadcasted_iota(jnp.int32, (tokens, tokens), 0)
    query_at = lax.broadcasted_iota(jnp.int32, (tokens, tokens), 1)
    start = jnp.int32(0)
    floor = jnp.zeros((tokens, tokens), jnp.int32)
    for k in range(length_ref.shape[1]):
        lowest = jnp.maximum(start - back_ref[0, k], 0)
        floor = jnp.where(query_at >= start, lowest, floor)
        start = start + length_ref[0, k]
    hidden = jnp.where((key_at <= query_at) & (key_at >= floor), 0.0, -jnp.inf).astype(F32)
    scale = math.log2(math.e) / math.sqrt(HEAD_DIM)
    for h in range(HEADS):
        at = slice(h * HEAD_DIM, (h + 1) * HEAD_DIM)
        query = query_ref[:, at]
        scores = lax.dot_general(
            key_ref[:, at], query, (((1,), (1,)), ((), ())), preferred_element_type=F32
        )
        scores = scores * scale + hidden
        weights = jnp.exp2(scores - jnp.max(scores, 0, keepdims=True))
        total = jnp.sum(weights, 0, keepdims=True)
        weights = weights * (weight_ref[0, h : h + 1, :] / total)
        local_ref[:, at] = lax.dot_general(
            weights.astype(BF16), value_ref[:, at], (((0,), (0,)), ((), ())), preferred_element_type=F32
        )
        query = query.astype(F32).T
        inverse = lax.rsqrt(jnp.mean(query * query, 0, keepdims=True) + EPSILON)
        for slot, read_ref in enumerate(read_refs):
            gain = sum(
                weight_ref[1 + level, h : h + 1, :] * coef_ref[slot, level] for level in range(levels)
            )
            read_ref[:, at] = (query * (inverse * gain)).T.astype(BF16)


def local_part(frame_len, window_back, coefs, queries, keys, values, weights, after):
    tokens, width = queries.shape
    slots = coefs.shape[0]
    return pl.pallas_call(
        local_kernel,
        out_shape=[jax.ShapeDtypeStruct((tokens, width), F32)]
        + [jax.ShapeDtypeStruct((tokens, width), BF16)] * slots,
        in_specs=[SCALARS] * 3 + [WHOLE] * 4 + [pl.BlockSpec(memory_space=pl.ANY)],
        out_specs=[WHOLE] * (1 + slots),
        compiler_params=PARAMS,
        cost_estimate=pl.CostEstimate(
            flops=4 * tokens * tokens * width,
            bytes_accessed=14 * tokens * width,
            transcendentals=tokens * tokens * HEADS,
        ),
    )(frame_len, window_back, coefs, queries, keys, values, weights, after)


def read_kernel(first_ref, base_ref, read_ref, *refs):
    out_ref, state_refs = refs[-1], refs[:-1]
    for n, state_ref in enumerate(state_refs):
        for h in range(state_ref.shape[0] // HEAD_DIM):
            at = columns(first_ref[n] + h)
            result = base_ref[:, at] + jnp.dot(
                read_ref[:, at],
                state_ref[h * HEAD_DIM : (h + 1) * HEAD_DIM, :],
                preferred_element_type=F32,
            )
            out_ref[:, at] = result.astype(out_ref.dtype)


def read_states(first, base, reads, states, dtype):
    return pl.pallas_call(
        read_kernel,
        out_shape=jax.ShapeDtypeStruct(base.shape, dtype),
        in_specs=[SCALARS] + [WHOLE] * (2 + len(states)),
        out_specs=WHOLE,
        compiler_params=PARAMS,
        cost_estimate=pl.CostEstimate(
            flops=2 * base.shape[0] * base.shape[1] * HEAD_DIM,
            bytes_accessed=8 * base.shape[0] * base.shape[1],
            transcendentals=0,
        ),
    )(first, base, reads, *states)


def swap(array, axis, mask, size):
    return lax.ppermute(array, axis, [(n, n ^ mask) for n in range(size)])


def level_scale(level, tokens):
    return 1.0 / math.sqrt(HEAD_DIM * 2**level * tokens)


def plain_body(sizes, queries, keys, values, level_weight, frame_len, window_back):
    frames, outer, chips = sizes
    frame = lax.axis_index("frame")
    space = ("outer", "chip", "core")
    zero = jnp.zeros((1,), jnp.int32)
    state = lax.psum(local_state(zero, keys, values, HEADS, F32), space)
    states = lax.all_gather(state.astype(BF16), "frame").astype(F32)
    ids = jnp.arange(frames)[:, None, None]
    depth = frames.bit_length() - 1
    tokens = queries.shape[0] * outer * chips * 2
    coefs = jnp.diag(jnp.array([level_scale(level, tokens) for level in range(depth)], F32))
    result, *reads = local_part(
        frame_len, window_back, coefs, queries, keys, values, level_weight, states
    )
    for level in range(depth):
        first = (frame >> level + 1) << level + 1
        inside = (ids >= first) & (ids < first + 2**level) & ((frame >> level) % 2 == 1)
        total = jnp.sum(jnp.where(inside, states, 0.0), 0).astype(BF16)
        result = read_states(zero, result, reads[level], [total], F32)
    return result.astype(BF16)


def body(sizes, queries, keys, values, level_weight, frame_len, window_back):
    frames, outer, chips = sizes
    tokens = queries.shape[0]
    frame = lax.axis_index("frame")
    chip = lax.axis_index("chip").astype(jnp.int32)
    core = lax.axis_index("core").astype(jnp.int32)
    half = HEADS // 2
    mine_at, other_at = (core * half).reshape(1), ((1 - core) * half).reshape(1)

    outgoing = local_state(other_at, keys, values, half, BF16)
    incoming = swap(outgoing, "core", 1, 2)
    mine = local_state(mine_at, keys, values, half, F32)
    order = jnp.stack([chip ^ d for d in range(chips)])
    own, *sends = chip_pieces(order, mine, incoming, chips)
    got = [swap(sends[d - 1], "chip", d, chips) for d in range(1, chips)]

    all_tokens = tokens * outer * chips * 2
    low, high = level_scale(0, all_tokens), level_scale(1, all_tokens)
    coefs = jnp.stack(
        [
            jnp.stack([jnp.where(frame % 2 == 1, low, 0.0), jnp.where(frame == 2, high, 0.0)]),
            jnp.stack([jnp.float32(0.0), jnp.where(frame == 3, high, 0.0)]),
        ]
    ).astype(F32)
    local, read_x, read_y = local_part(
        frame_len, window_back, coefs, queries, keys, values, level_weight, own
    )

    state = sum_pieces(local, own, got, F32 if outer > 1 else BF16)
    if outer > 1:
        state = lax.psum(state, "outer").astype(BF16)
    near, across, diagonal = (swap(state, "frame", mask, frames) for mask in (1, 2, 3))
    both = (across.astype(F32) + diagonal.astype(F32)).astype(BF16)
    slot = jnp.where(frame == 2, both, near)

    x_own = [slot] + [swap(slot, "chip", d, chips) for d in range(1, chips)]
    y_own = [swap(piece, "frame", 1, frames) for piece in x_own]
    x_all = [(piece, swap(piece, "core", 1, 2)) for piece in x_own]
    y_all = [(piece, swap(piece, "core", 1, 2)) for piece in y_own]
    first = jnp.stack(
        [(core ^ c) * half + (chip ^ d) * (half // chips) for d in range(chips) for c in range(2)]
    )
    result = read_states(first, local, read_x, [x for pair in x_all for x in pair], F32)
    return read_states(first, result, read_y, [y for pair in y_all for y in pair], BF16)


def solution(mesh):
    frames, space = mesh.shape["frame"], mesh.shape["space"]
    chips = 1
    while HEADS % (chips * 4) == 0 and space % (chips * 4) == 0 and chips < 4:
        chips *= 2
    sizes = (frames, space // (2 * chips), chips)
    names = ("frame", "outer", "chip", "core")
    fine = Mesh(mesh.devices.reshape(sizes + (2,)), names)
    rows = P(names, None)
    return jax.shard_map(
        functools.partial(body if frames == 4 else plain_body, sizes),
        mesh=fine,
        in_specs=(rows, rows, rows, P(None, None, names), rows, rows),
        out_specs=rows,
        check_vma=False,
    )
```

```python
import functools
import math

import jax
import jax.numpy as jnp
from jax import lax
from jax.experimental import pallas as pl
from jax.experimental.pallas import tpu as pltpu
from jax.sharding import Mesh, PartitionSpec as P

HEADS = 24
HEAD_DIM = 128
EPSILON = 1e-06
VMEM_LIMIT = 40 * 1024 * 1024

F32, BF16 = jnp.float32, jnp.bfloat16
WHOLE = pl.BlockSpec(memory_space=pltpu.VMEM)
SCALARS = pl.BlockSpec(memory_space=pltpu.SMEM)
IN_HBM = pl.BlockSpec(memory_space=pltpu.HBM)
PARAMS = pltpu.CompilerParams(vmem_limit_bytes=VMEM_LIMIT)


def inverse_rms(rows):
    return lax.rsqrt(jnp.mean(rows * rows, -1, keepdims=True) + EPSILON)


def columns(head, count=1):
    return pl.ds(pl.multiple_of(head * HEAD_DIM, HEAD_DIM), count * HEAD_DIM)


def core_heads():
    core = lax.axis_index("core")
    return core * (HEADS // 2), (1 - core) * (HEADS // 2)


def in_vmem(*arrays):
    return [pltpu.with_memory_space_constraint(array, pltpu.VMEM) for array in arrays]


def states_of(first, keys, values, out_ref):
    for h in range(out_ref.shape[0] // HEAD_DIM):
        at = columns(first + h)
        key_rows = keys[:, at].astype(F32)
        normal = (key_rows * inverse_rms(key_rows)).astype(BF16)
        state = lax.dot_general(
            normal, values[:, at], (((0,), (0,)), ((), ())), preferred_element_type=F32
        )
        out_ref[h * HEAD_DIM : (h + 1) * HEAD_DIM, :] = state.astype(out_ref.dtype)


def first_kernel(key_ref, value_ref, out_ref, keys, values, sems):
    mine, other = core_heads()
    copies = []
    for n, first in enumerate((other, mine)):
        at = columns(first, HEADS // 2)
        for s, (ref, held) in enumerate(((key_ref, keys), (value_ref, values))):
            copies.append(pltpu.make_async_copy(ref.at[:, at], held.at[:, at], sems.at[n, s]))
            copies[-1].start()
    copies[0].wait()
    copies[1].wait()
    states_of(other, keys, values, out_ref)
    copies[2].wait()
    copies[3].wait()


def outgoing_state(keys, values):
    dim, half = HEAD_DIM, HEADS // 2
    rows = keys.shape[0]
    keys, values = (pltpu.with_memory_space_constraint(x, pltpu.HBM) for x in (keys, values))
    return pl.pallas_call(
        first_kernel,
        out_shape=[pltpu.VMEM((half * dim, dim), BF16)] + [pltpu.VMEM(keys.shape, BF16)] * 2,
        in_specs=[IN_HBM, IN_HBM],
        out_specs=[WHOLE] * 3,
        scratch_shapes=[pltpu.SemaphoreType.DMA((2, 2))],
        compiler_params=PARAMS,
        cost_estimate=pl.CostEstimate(
            flops=2 * half * rows * dim * dim, bytes_accessed=8 * half * rows * dim, transcendentals=0
        ),
    )(keys, values)


def own_kernel(key_ref, value_ref, out_ref):
    states_of(core_heads()[0], key_ref, value_ref, out_ref)


def own_state(keys, values):
    dim, half = HEAD_DIM, HEADS // 2
    rows = keys.shape[0]
    return pl.pallas_call(
        own_kernel,
        out_shape=pltpu.VMEM((half * dim, dim), F32),
        in_specs=[WHOLE, WHOLE],
        out_specs=WHOLE,
        compiler_params=PARAMS,
        cost_estimate=pl.CostEstimate(
            flops=2 * half * rows * dim * dim, bytes_accessed=8 * half * rows * dim, transcendentals=0
        ),
    )(*in_vmem(keys, values))


def piece_kernel(mine_ref, other_ref, own_ref, *piece_refs):
    chip = lax.axis_index("chip")
    rows = own_ref.shape[0]
    for d, ref in enumerate((own_ref,) + piece_refs):
        at = pl.ds(pl.multiple_of((chip ^ d) * rows, rows), rows)
        ref[...] = (mine_ref[at, :] + other_ref[at, :].astype(F32)).astype(ref.dtype)


def chip_pieces(mine, other, chips):
    shape = (mine.shape[0] // chips, HEAD_DIM)
    return pl.pallas_call(
        piece_kernel,
        out_shape=[pltpu.VMEM(shape, F32)] + [pltpu.VMEM(shape, BF16)] * (chips - 1),
        in_specs=[WHOLE, WHOLE],
        out_specs=[WHOLE] * chips,
        compiler_params=PARAMS,
    )(mine, other)


def sum_kernel(after_ref, own_ref, *refs):
    total = own_ref[...]
    for ref in refs[:-1]:
        total = total + ref[...].astype(F32)
    refs[-1][...] = total.astype(refs[-1].dtype)


def sum_pieces(after, own, parts, dtype):
    return pl.pallas_call(
        sum_kernel,
        out_shape=pltpu.VMEM(own.shape, dtype),
        in_specs=[pl.BlockSpec(memory_space=pl.ANY)] + [WHOLE] * (1 + len(parts)),
        out_specs=WHOLE,
        compiler_params=PARAMS,
    )(after, own, *parts)


def pack_kernel(groups, after, *refs):
    inputs, outputs = refs[after : len(refs) - len(groups)], refs[len(refs) - len(groups) :]
    for group, out_ref in zip(groups, outputs):
        rows = out_ref.shape[0] // len(group)
        for n, which in enumerate(group):
            out_ref[n * rows : (n + 1) * rows, :] = inputs[which][...]


def pack(groups, pieces, after):
    rows = pieces[0].shape[0]
    return pl.pallas_call(
        functools.partial(pack_kernel, groups, len(after)),
        out_shape=[pltpu.VMEM((rows * len(group), HEAD_DIM), BF16) for group in groups],
        in_specs=[pl.BlockSpec(memory_space=pl.ANY)] * len(after) + [WHOLE] * len(pieces),
        out_specs=[WHOLE] * len(groups),
        compiler_params=PARAMS,
    )(*after, *in_vmem(*pieces))


def local_kernel(
    coefs, turn, length_ref, back_ref, query_ref, key_ref, value_ref, weight_ref, after_ref, local_ref, *read_refs
):
    tokens = query_ref.shape[0]
    first = core_heads()[turn]
    heads = local_ref.shape[1] // HEAD_DIM
    key_at = lax.broadcasted_iota(jnp.int32, (tokens, tokens), 0)
    query_at = lax.broadcasted_iota(jnp.int32, (tokens, tokens), 1)
    start = jnp.int32(0)
    floor = jnp.zeros((tokens, tokens), jnp.int32)
    for k in range(length_ref.shape[1]):
        lowest = jnp.maximum(start - back_ref[0, k], 0)
        floor = jnp.where(query_at >= start, lowest, floor)
        start = start + length_ref[0, k]
    hidden = jnp.where((key_at <= query_at) & (key_at >= floor), 0.0, -jnp.inf).astype(F32)
    scale = math.log2(math.e) / math.sqrt(HEAD_DIM)
    ones = jnp.full((HEAD_DIM, HEAD_DIM), 1.0 / HEAD_DIM, BF16)
    half = HEADS // 2
    by_slot = []
    for slot_coefs in coefs(lax.axis_index("frame")):
        total = None
        for level, coef in slot_coefs:
            term = weight_ref[1 + level, pl.ds(first, heads), :] * coef
            total = term if total is None else total + term
        by_slot.append(total)
    pad = -len(by_slot) * heads % HEAD_DIM
    gains = jnp.concatenate(by_slot + [jnp.zeros((pad, tokens), F32)], 0).T

    def scores_of(h):
        at = columns(first + h)
        return lax.dot_general(
            key_ref[:, at], query_ref[:, at], (((1,), (1,)), ((), ())), preferred_element_type=F32
        )

    upcoming = scores_of(0)
    for h in range(heads):
        scores = upcoming * scale + hidden
        if h + 1 < heads:
            upcoming = scores_of(h + 1)
        weights = jnp.exp2(scores - jnp.max(scores, 0, keepdims=True))
        total = jnp.sum(weights, 0, keepdims=True)
        weights = weights * (weight_ref[0, pl.ds(first + h, 1), :] / total)
        at = slice(h * HEAD_DIM, (h + 1) * HEAD_DIM)
        local_ref[:, at] = lax.dot_general(
            weights.astype(BF16),
            value_ref[:, columns(first + h)],
            (((0,), (0,)), ((), ())),
            preferred_element_type=F32,
        )
        query = query_ref[:, columns(first + h)].astype(F32)
        mean = jnp.dot((query * query).astype(BF16), ones, preferred_element_type=F32)
        query = query * lax.rsqrt(mean + EPSILON)
        for slot, read_ref in enumerate(read_refs):
            which = slot * heads + h
            read_ref[:, at] = (query * gains[:, which : which + 1]).astype(BF16)


def local_part(coefs, slots, turn, frame_len, window_back, queries, keys, values, weights, after):
    tokens, width = queries.shape
    width //= 2
    return pl.pallas_call(
        functools.partial(local_kernel, coefs, turn),
        out_shape=[pltpu.VMEM((tokens, width), F32)] + [pltpu.VMEM((tokens, width), BF16)] * slots,
        in_specs=[SCALARS] * 2 + [WHOLE] * 4 + [pl.BlockSpec(memory_space=pl.ANY)],
        out_specs=[WHOLE] * (1 + slots),
        compiler_params=PARAMS,
        cost_estimate=pl.CostEstimate(
            flops=4 * tokens * tokens * width,
            bytes_accessed=14 * tokens * width,
            transcendentals=tokens * width,
        ),
    )(frame_len, window_back, queries, *in_vmem(keys, values), weights, after)


def read_heads(d, chips, base_ref, states):
    count = HEADS // 2 // chips
    first = (lax.axis_index("chip") ^ d) * count
    for h in range(count):
        at = columns(first + h)
        result = base_ref[:, at]
        for read_ref, state_ref, row in states:
            result = result + jnp.dot(
                read_ref[:, at],
                state_ref[row + h * HEAD_DIM : row + (h + 1) * HEAD_DIM, :],
                preferred_element_type=F32,
            )
        yield at, result


def middle_kernel(chips, early, local_ref, x_ref, y_ref, state_ref, out_ref):
    rows = state_ref.shape[0] // (chips + early)
    for d in range(chips):
        states = [(x_ref, state_ref, d * rows)]
        if d < early:
            states.append((y_ref, state_ref, (chips + d) * rows))
        for at, result in read_heads(d, chips, local_ref, states):
            out_ref[:, at] = result


def read_middle(chips, early, local, x, y, states):
    return pl.pallas_call(
        functools.partial(middle_kernel, chips, early),
        out_shape=pltpu.VMEM(local.shape, F32),
        in_specs=[WHOLE] * 4,
        out_specs=WHOLE,
        compiler_params=PARAMS,
        cost_estimate=pl.CostEstimate(
            flops=2 * local.size * HEAD_DIM, bytes_accessed=8 * local.size, transcendentals=0
        ),
    )(*in_vmem(local, x, y, states))


def late_half(chips, early, base_ref, y_ref, state_ref, out_ref):
    rows = state_ref.shape[0] // max(chips - early, 1)
    for d in range(chips):
        states = [(y_ref, state_ref, (d - early) * rows)] if d >= early else []
        for at, result in read_heads(d, chips, base_ref, states):
            out_ref[:, at] = result.astype(BF16)


def read_late(chips, early, base, y, states):
    return pl.pallas_call(
        functools.partial(late_half, chips, early),
        out_shape=pltpu.VMEM(base.shape, BF16),
        in_specs=[WHOLE] * 3,
        out_specs=WHOLE,
        compiler_params=PARAMS,
        cost_estimate=pl.CostEstimate(
            flops=base.size * HEAD_DIM, bytes_accessed=6 * base.size, transcendentals=0
        ),
    )(*in_vmem(base, y, states))


def last_kernel(chips, early, done_ref, base_ref, y_ref, state_ref, out_ref, held, sems):
    mine, other = core_heads()
    first = pltpu.make_async_copy(done_ref, out_ref.at[:, columns(mine, HEADS // 2)], sems.at[0])
    first.start()
    late_half(chips, early, base_ref, y_ref, state_ref, held)
    second = pltpu.make_async_copy(held, out_ref.at[:, columns(other, HEADS // 2)], sems.at[1])
    second.start()
    first.wait()
    second.wait()


def read_last(chips, early, done, base, y, states):
    tokens, width = base.shape
    return pl.pallas_call(
        functools.partial(last_kernel, chips, early),
        out_shape=jax.ShapeDtypeStruct((tokens, 2 * width), BF16),
        in_specs=[WHOLE] * 4,
        out_specs=pl.BlockSpec(memory_space=pl.ANY),
        scratch_shapes=[pltpu.VMEM((tokens, width), BF16), pltpu.SemaphoreType.DMA((2,))],
        compiler_params=PARAMS,
        cost_estimate=pl.CostEstimate(
            flops=base.size * HEAD_DIM, bytes_accessed=10 * base.size, transcendentals=0
        ),
    )(*in_vmem(done, base, y, states))


def swap(array, axis, mask, size):
    return lax.ppermute(array, axis, [(n, n ^ mask) for n in range(size)])


def body(sizes, queries, keys, values, level_weight, frame_len, window_back):
    frames, outer, chips = sizes
    frame = lax.axis_index("frame")
    low, high = (
        1.0 / math.sqrt(HEAD_DIM * 2**level * queries.shape[0] * outer * chips * 2) for level in (0, 1)
    )

    def coefs(f):
        x_low = jnp.where(f % 2 == 1, low, 0.0)
        x_high = jnp.where(f == 2, high, 0.0)
        return [[(0, x_low), (1, x_high)], [(1, jnp.where(f == 3, high, 0.0))]]

    local = functools.partial(local_part, coefs, 2)
    rest = (frame_len, window_back, queries)

    outgoing, keys, values = outgoing_state(keys, values)
    incoming = swap(outgoing, "core", 1, 2)
    mine = own_state(keys, values)
    own, *sends = chip_pieces(mine, incoming, chips)
    got = {d: swap(sends[d - 1], "chip", d, chips) for d in reversed(range(1, chips))}

    local_0, x_0, y_0 = local(0, *rest, keys, values, level_weight, own)
    state = sum_pieces(local_0, own, list(got.values()), F32 if outer > 1 else BF16)
    if outer > 1:
        state = lax.psum(state, "outer").astype(BF16)
    near, across, diagonal = (swap(state, "frame", mask, frames) for mask in (1, 2, 3))
    both = (across.astype(F32) + diagonal.astype(F32)).astype(BF16)
    slot = jnp.where(frame == 2, both, near)

    early = min(2, chips)
    x = [swap(slot, "chip", d, chips) for d in range(1, chips)]
    near_pairs = [
        (f * chips + c, (f ^ 1) * chips + (c ^ 1)) for f in range(frames) for c in range(chips)
    ]
    y = [swap(slot, "frame", 1, frames), lax.ppermute(slot, ("frame", "chip"), near_pairs)][:early]
    local_1, x_1, y_1 = local(1, *rest, keys, values, level_weight, slot)
    pieces = [slot] + x + y
    own_states, late = pack(
        [list(range(chips + early)), list(range(early, chips)) or [0]], pieces, [local_1]
    )
    late_own = swap(late, "frame", 1, frames)
    other_states = swap(own_states, "core", 1, 2)
    base_0 = read_middle(chips, early, local_0, x_0, y_0, own_states)
    base_1 = read_middle(chips, early, local_1, x_1, y_1, other_states)
    late_own, base_0, base_1 = lax.optimization_barrier((late_own, base_0, base_1))
    late_other = swap(late_own, "core", 1, 2)
    done = read_late(chips, early, base_0, y_0, late_own)
    return read_last(chips, early, done, base_1, y_1, late_other)


def solution(mesh):
    frames, space = mesh.shape["frame"], mesh.shape["space"]
    chips = 1
    while HEADS % (chips * 4) == 0 and space % (chips * 4) == 0 and chips < 4:
        chips *= 2
    sizes = (frames, space // (2 * chips), chips)
    names = ("frame", "outer", "chip", "core")
    fine = Mesh(mesh.devices.reshape(sizes + (2,)), names)
    rows = P(names, None)
    return jax.shard_map(
        functools.partial(body, sizes),
        mesh=fine,
        in_specs=(rows, rows, rows, P(None, None, names), rows, rows),
        out_specs=rows,
        check_vma=False,
    )
```

```python
import functools
import math

import jax
import jax.numpy as jnp
from jax import lax
from jax.experimental import pallas as pl
from jax.experimental.pallas import tpu as pltpu
from jax.sharding import Mesh, PartitionSpec as P

HEADS = 24
HEAD_DIM = 128
EPSILON = 1e-06
VMEM_LIMIT = 40 * 1024 * 1024

F32, BF16 = jnp.float32, jnp.bfloat16
WHOLE = pl.BlockSpec(memory_space=pltpu.VMEM)
SCALARS = pl.BlockSpec(memory_space=pltpu.SMEM)
ANYWHERE = pl.BlockSpec(memory_space=pl.ANY)
IN_HBM = pl.BlockSpec(memory_space=pltpu.HBM)
PARAMS = pltpu.CompilerParams(vmem_limit_bytes=VMEM_LIMIT)


def inverse_rms(rows):
    return lax.rsqrt(jnp.mean(rows * rows, -1, keepdims=True) + EPSILON)


def columns(head, count=1):
    return pl.ds(pl.multiple_of(head * HEAD_DIM, HEAD_DIM), count * HEAD_DIM)


def core_heads():
    core = lax.axis_index("core")
    return core * (HEADS // 2), (1 - core) * (HEADS // 2)


def in_vmem(*arrays):
    return [pltpu.with_memory_space_constraint(array, pltpu.VMEM) for array in arrays]


def states_of(first, keys, values, out_ref):
    for h in range(out_ref.shape[0] // HEAD_DIM):
        at = columns(first + h)
        key_rows = keys[:, at].astype(F32)
        normal = (key_rows * inverse_rms(key_rows)).astype(BF16)
        state = lax.dot_general(
            normal, values[:, at], (((0,), (0,)), ((), ())), preferred_element_type=F32
        )
        out_ref[h * HEAD_DIM : (h + 1) * HEAD_DIM, :] = state.astype(out_ref.dtype)


def first_kernel(key_ref, value_ref, out_ref, keys, values, sems):
    mine, other = core_heads()
    copies = []
    for n, first in enumerate((other, mine)):
        at = columns(first, HEADS // 2)
        for s, (ref, held) in enumerate(((key_ref, keys), (value_ref, values))):
            copies.append(pltpu.make_async_copy(ref.at[:, at], held.at[:, at], sems.at[n, s]))
            copies[-1].start()
    copies[0].wait()
    copies[1].wait()
    states_of(other, keys, values, out_ref)
    copies[2].wait()
    copies[3].wait()


def outgoing_state(keys, values):
    dim, half = HEAD_DIM, HEADS // 2
    rows = keys.shape[0]
    keys, values = (pltpu.with_memory_space_constraint(x, pltpu.HBM) for x in (keys, values))
    return pl.pallas_call(
        first_kernel,
        out_shape=[pltpu.VMEM((half * dim, dim), BF16)] + [pltpu.VMEM(keys.shape, BF16)] * 2,
        in_specs=[IN_HBM, IN_HBM],
        out_specs=[WHOLE] * 3,
        scratch_shapes=[pltpu.SemaphoreType.DMA((2, 2))],
        compiler_params=PARAMS,
        cost_estimate=pl.CostEstimate(
            flops=2 * half * rows * dim * dim, bytes_accessed=8 * half * rows * dim, transcendentals=0
        ),
    )(keys, values)


def own_kernel(key_ref, value_ref, out_ref):
    states_of(core_heads()[0], key_ref, value_ref, out_ref)


def own_state(keys, values):
    dim, half = HEAD_DIM, HEADS // 2
    rows = keys.shape[0]
    return pl.pallas_call(
        own_kernel,
        out_shape=pltpu.VMEM((half * dim, dim), F32),
        in_specs=[WHOLE, WHOLE],
        out_specs=WHOLE,
        compiler_params=PARAMS,
        cost_estimate=pl.CostEstimate(
            flops=2 * half * rows * dim * dim, bytes_accessed=8 * half * rows * dim, transcendentals=0
        ),
    )(*in_vmem(keys, values))


def piece_kernel(chunks, chips, mine_ref, other_ref, *refs):
    chip = lax.axis_index("chip")
    shard = mine_ref.shape[0] // chips
    refs = iter(refs)
    for d in range(chips):
        offset = 0
        for chunk in chunks:
            rows = chunk * HEAD_DIM
            at = pl.ds(pl.multiple_of((chip ^ d) * shard + offset, HEAD_DIM), rows)
            ref = next(refs)
            ref[...] = (mine_ref[at, :] + other_ref[at, :].astype(F32)).astype(ref.dtype)
            offset += rows


def chip_pieces(chunks, chips, mine, other):
    shapes = [
        pltpu.VMEM((chunk * HEAD_DIM, HEAD_DIM), BF16 if d else F32) for d in range(chips) for chunk in chunks
    ]
    pieces = pl.pallas_call(
        functools.partial(piece_kernel, chunks, chips),
        out_shape=shapes,
        in_specs=[WHOLE, WHOLE],
        out_specs=[WHOLE] * len(shapes),
        compiler_params=PARAMS,
    )(*in_vmem(mine, other))
    return [pieces[n :: len(chunks)] for n in range(len(chunks))]


def sum_kernel(after_ref, own_ref, *refs):
    total = own_ref[...]
    for ref in refs[:-1]:
        total = total + ref[...].astype(F32)
    refs[-1][...] = total.astype(refs[-1].dtype)


def sum_pieces(after, own, parts, dtype):
    return pl.pallas_call(
        sum_kernel,
        out_shape=pltpu.VMEM(own.shape, dtype),
        in_specs=[ANYWHERE] + [WHOLE] * (1 + len(parts)),
        out_specs=WHOLE,
        compiler_params=PARAMS,
    )(after, *in_vmem(own, *parts))


def slot_kernel(after_ref, near_ref, across_ref, diagonal_ref, out_ref):
    both = across_ref[...].astype(F32) + diagonal_ref[...].astype(F32)
    near = near_ref[...].astype(F32)
    out_ref[...] = jnp.where(lax.axis_index("frame") == 2, both, near).astype(BF16)


def choose_slot(after, near, across, diagonal):
    return pl.pallas_call(
        slot_kernel,
        out_shape=pltpu.VMEM(near.shape, BF16),
        in_specs=[ANYWHERE] + [WHOLE] * 3,
        out_specs=WHOLE,
        compiler_params=PARAMS,
    )(after, *in_vmem(near, across, diagonal))


def pack_kernel(groups, after, *refs):
    inputs, outputs = refs[after : len(refs) - len(groups)], refs[len(refs) - len(groups) :]
    for group, out_ref in zip(groups, outputs):
        rows = out_ref.shape[0] // len(group)
        for n, which in enumerate(group):
            out_ref[n * rows : (n + 1) * rows, :] = inputs[which][...]


def pack(groups, pieces, after):
    rows = pieces[0].shape[0]
    return pl.pallas_call(
        functools.partial(pack_kernel, groups, len(after)),
        out_shape=[pltpu.VMEM((rows * len(group), HEAD_DIM), BF16) for group in groups],
        in_specs=[ANYWHERE] * len(after) + [WHOLE] * len(pieces),
        out_specs=[WHOLE] * len(groups),
        compiler_params=PARAMS,
    )(*after, *in_vmem(*pieces))


def local_kernel(
    coefs, turn, length_ref, back_ref, query_ref, key_ref, value_ref, weight_ref, after_ref, local_ref, *read_refs
):
    tokens = query_ref.shape[0]
    first = core_heads()[turn]
    heads = local_ref.shape[1] // HEAD_DIM
    key_at = lax.broadcasted_iota(jnp.int32, (tokens, tokens), 0)
    query_at = lax.broadcasted_iota(jnp.int32, (tokens, tokens), 1)
    start = jnp.int32(0)
    floor = jnp.zeros((tokens, tokens), jnp.int32)
    for k in range(length_ref.shape[1]):
        lowest = jnp.maximum(start - back_ref[0, k], 0)
        floor = jnp.where(query_at >= start, lowest, floor)
        start = start + length_ref[0, k]
    hidden = jnp.where((key_at <= query_at) & (key_at >= floor), 0.0, -jnp.inf).astype(F32)
    scale = math.log2(math.e) / math.sqrt(HEAD_DIM)
    ones = jnp.full((HEAD_DIM, HEAD_DIM), 1.0 / HEAD_DIM, BF16)
    half = HEADS // 2
    by_slot = []
    for slot_coefs in coefs(lax.axis_index("frame")):
        total = None
        for level, coef in slot_coefs:
            term = weight_ref[1 + level, pl.ds(first, heads), :] * coef
            total = term if total is None else total + term
        by_slot.append(total)
    pad = -len(by_slot) * heads % HEAD_DIM
    gains = jnp.concatenate(by_slot + [jnp.zeros((pad, tokens), F32)], 0).T

    def scores_of(h):
        at = columns(first + h)
        return lax.dot_general(
            key_ref[:, at], query_ref[:, at], (((1,), (1,)), ((), ())), preferred_element_type=F32
        )

    upcoming = scores_of(0)
    for h in range(heads):
        scores = upcoming * scale + hidden
        if h + 1 < heads:
            upcoming = scores_of(h + 1)
        weights = jnp.exp2(scores - jnp.max(scores, 0, keepdims=True))
        total = jnp.sum(weights, 0, keepdims=True)
        weights = weights * (weight_ref[0, pl.ds(first + h, 1), :] / total)
        at = slice(h * HEAD_DIM, (h + 1) * HEAD_DIM)
        local_ref[:, at] = lax.dot_general(
            weights.astype(BF16),
            value_ref[:, columns(first + h)],
            (((0,), (0,)), ((), ())),
            preferred_element_type=F32,
        )
        query = query_ref[:, columns(first + h)].astype(F32)
        mean = jnp.dot((query * query).astype(BF16), ones, preferred_element_type=F32)
        query = query * lax.rsqrt(mean + EPSILON)
        for slot, read_ref in enumerate(read_refs):
            which = slot * heads + h
            read_ref[:, at] = (query * gains[:, which : which + 1]).astype(BF16)


def local_part(coefs, slots, turn, frame_len, window_back, queries, keys, values, weights, after):
    tokens, width = queries.shape
    width //= 2
    return pl.pallas_call(
        functools.partial(local_kernel, coefs, turn),
        out_shape=[pltpu.VMEM((tokens, width), F32)] + [pltpu.VMEM((tokens, width), BF16)] * slots,
        in_specs=[SCALARS] * 2 + [WHOLE] * 4 + [ANYWHERE],
        out_specs=[WHOLE] * (1 + slots),
        compiler_params=PARAMS,
        cost_estimate=pl.CostEstimate(
            flops=4 * tokens * tokens * width,
            bytes_accessed=14 * tokens * width,
            transcendentals=tokens * width,
        ),
    )(frame_len, window_back, queries, *in_vmem(keys, values), weights, after)


def read_heads(d, chips, heads, base_ref, states):
    first = (lax.axis_index("chip") ^ d) * (HEADS // 2 // chips)
    for n, h in enumerate(heads):
        at = columns(first + h)
        result = base_ref[:, at]
        for read_ref, state_ref, row in states:
            result = result + jnp.dot(
                read_ref[:, at],
                state_ref[row + n * HEAD_DIM : row + (n + 1) * HEAD_DIM, :],
                preferred_element_type=F32,
            )
        yield at, result


def heads_of(chunks):
    return [range(sum(chunks[:n]), sum(chunks[: n + 1])) for n in range(len(chunks))]


def middle_kernel(chunks, chips, early, local_ref, x_ref, y_ref, *refs):
    out_ref = refs[-1]
    for heads, state_ref in zip(heads_of(chunks), refs):
        rows = len(heads) * HEAD_DIM
        for d in range(chips):
            states = [(x_ref, state_ref, d * rows)]
            if d < early:
                states.append((y_ref, state_ref, (chips + d) * rows))
            for at, result in read_heads(d, chips, heads, local_ref, states):
                out_ref[:, at] = result


def read_middle(chunks, chips, early, local, x, y, states):
    return pl.pallas_call(
        functools.partial(middle_kernel, chunks, chips, early),
        out_shape=pltpu.VMEM(local.shape, F32),
        in_specs=[WHOLE] * (3 + len(states)),
        out_specs=WHOLE,
        compiler_params=PARAMS,
        cost_estimate=pl.CostEstimate(
            flops=2 * local.size * HEAD_DIM, bytes_accessed=8 * local.size, transcendentals=0
        ),
    )(*in_vmem(local, x, y, *states))


def late_half(chunks, chips, early, base_ref, y_ref, *refs):
    out_ref = refs[-1]
    for heads, state_ref in zip(heads_of(chunks), refs):
        rows = len(heads) * HEAD_DIM
        for d in range(chips):
            states = [(y_ref, state_ref, (d - early) * rows)] if d >= early else []
            for at, result in read_heads(d, chips, heads, base_ref, states):
                out_ref[:, at] = result.astype(BF16)


def read_late(chunks, chips, early, base, y, states):
    return pl.pallas_call(
        functools.partial(late_half, chunks, chips, early),
        out_shape=pltpu.VMEM(base.shape, BF16),
        in_specs=[WHOLE] * (2 + len(states)),
        out_specs=WHOLE,
        compiler_params=PARAMS,
        cost_estimate=pl.CostEstimate(
            flops=base.size * HEAD_DIM, bytes_accessed=6 * base.size, transcendentals=0
        ),
    )(*in_vmem(base, y, *states))


def last_kernel(chunks, chips, early, done_ref, base_ref, y_ref, *refs):
    *state_refs, out_ref, held, sems = refs
    mine, other = core_heads()
    first = pltpu.make_async_copy(done_ref, out_ref.at[:, columns(mine, HEADS // 2)], sems.at[0])
    first.start()
    late_half(chunks, chips, early, base_ref, y_ref, *state_refs, held)
    second = pltpu.make_async_copy(held, out_ref.at[:, columns(other, HEADS // 2)], sems.at[1])
    second.start()
    first.wait()
    second.wait()


def read_last(chunks, chips, early, done, base, y, states):
    tokens, width = base.shape
    return pl.pallas_call(
        functools.partial(last_kernel, chunks, chips, early),
        out_shape=jax.ShapeDtypeStruct((tokens, 2 * width), BF16),
        in_specs=[WHOLE] * (3 + len(states)),
        out_specs=ANYWHERE,
        scratch_shapes=[pltpu.VMEM((tokens, width), BF16), pltpu.SemaphoreType.DMA((2,))],
        compiler_params=PARAMS,
        cost_estimate=pl.CostEstimate(
            flops=base.size * HEAD_DIM, bytes_accessed=10 * base.size, transcendentals=0
        ),
    )(*in_vmem(done, base, y, *states))


def swap(array, axis, mask, size):
    return lax.ppermute(array, axis, [(n, n ^ mask) for n in range(size)])


def body(sizes, queries, keys, values, level_weight, frame_len, window_back):
    frames, outer, chips = sizes
    frame = lax.axis_index("frame")
    low, high = (
        1.0 / math.sqrt(HEAD_DIM * 2**level * queries.shape[0] * outer * chips * 2) for level in (0, 1)
    )

    def coefs(f):
        x_low = jnp.where(f % 2 == 1, low, 0.0)
        x_high = jnp.where(f == 2, high, 0.0)
        return [[(0, x_low), (1, x_high)], [(1, jnp.where(f == 3, high, 0.0))]]

    local = functools.partial(local_part, coefs, 2)
    rest = (frame_len, window_back, queries)

    count = HEADS // 2 // chips
    chunks = tuple(n for n in (count - count // 3, count // 3) if n)
    early = min(2, chips)
    near_pairs = [
        (f * chips + c, (f ^ 1) * chips + (c ^ 1)) for f in range(frames) for c in range(chips)
    ]
    shape = (chunks, chips, early)

    outgoing, keys, values = outgoing_state(keys, values)
    incoming = swap(outgoing, "core", 1, 2)
    mine = own_state(keys, values)
    cut = chip_pieces(chunks, chips, mine, incoming)
    got = [[swap(pieces[d], "chip", d, chips) for d in reversed(range(1, chips))] for pieces in cut]

    local_0, x_0, y_0 = local(0, *rest, keys, values, level_weight, cut[0][0])
    after, parts = local_0, []
    for pieces, arrived in zip(cut, got):
        after = sum_pieces(after, pieces[0], arrived, F32 if outer > 1 else BF16)
        state = lax.psum(after, "outer").astype(BF16) if outer > 1 else after
        parts.append([swap(state, "frame", mask, frames) for mask in (3, 2, 1)])

    gathered = []
    for diagonal, across, near in parts:
        slot = after = choose_slot(after, near, across, diagonal)
        x = [swap(slot, "chip", d, chips) for d in reversed(range(1, chips))][::-1]
        y = [swap(slot, "frame", 1, frames), lax.ppermute(slot, ("frame", "chip"), near_pairs)][:early]
        gathered.append([slot] + x + y)
    local_1, x_1, y_1 = local(1, *rest, keys, values, level_weight, after)

    after = local_1
    own, other, late_own = [], [], []
    for pieces in gathered:
        states, late = pack(
            [list(range(chips + early)), list(range(early, chips)) or [0]], pieces, [after]
        )
        after = states
        late_own.append(swap(late, "frame", 1, frames))
        own.append(states)
        other.append(swap(states, "core", 1, 2))
    base_0 = read_middle(*shape, local_0, x_0, y_0, own)
    base_1 = read_middle(*shape, local_1, x_1, y_1, other)
    late_own, base_0, base_1 = lax.optimization_barrier((late_own, base_0, base_1))
    late_other = [swap(late, "core", 1, 2) for late in late_own]
    done = read_late(*shape, base_0, y_0, late_own)
    return read_last(*shape, done, base_1, y_1, late_other)


def solution(mesh):
    frames, space = mesh.shape["frame"], mesh.shape["space"]
    chips = 1
    while HEADS % (chips * 4) == 0 and space % (chips * 4) == 0 and chips < 4:
        chips *= 2
    sizes = (frames, space // (2 * chips), chips)
    names = ("frame", "outer", "chip", "core")
    fine = Mesh(mesh.devices.reshape(sizes + (2,)), names)
    rows = P(names, None)
    return jax.shard_map(
        functools.partial(body, sizes),
        mesh=fine,
        in_specs=(rows, rows, rows, P(None, None, names), rows, rows),
        out_specs=rows,
        check_vma=False,
    )
```

```python
import functools
import math

import jax
import jax.numpy as jnp
from jax import lax
from jax.experimental import pallas as pl
from jax.experimental.pallas import tpu as pltpu
from jax.sharding import Mesh, PartitionSpec as P

HEADS = 24
HEAD_DIM = 128
EPSILON = 1e-06
VMEM_LIMIT = 40 * 1024 * 1024

F32, BF16 = jnp.float32, jnp.bfloat16
WHOLE = pl.BlockSpec(memory_space=pltpu.VMEM)
SCALARS = pl.BlockSpec(memory_space=pltpu.SMEM)
ANYWHERE = pl.BlockSpec(memory_space=pl.ANY)
IN_HBM = pl.BlockSpec(memory_space=pltpu.HBM)
SMALL = pl.CostEstimate(flops=1024, bytes_accessed=1024, transcendentals=0)
PARAMS = pltpu.CompilerParams(vmem_limit_bytes=VMEM_LIMIT)


def inverse_rms(rows):
    return lax.rsqrt(jnp.mean(rows * rows, -1, keepdims=True) + EPSILON)


def columns(head, count=1):
    return pl.ds(pl.multiple_of(head * HEAD_DIM, HEAD_DIM), count * HEAD_DIM)


def core_heads():
    core = lax.axis_index("core")
    return core * (HEADS // 2), (1 - core) * (HEADS // 2)


def in_vmem(*arrays):
    return [pltpu.with_memory_space_constraint(array, pltpu.VMEM) for array in arrays]


def states_of(first, keys, values, out_ref):
    for h in range(out_ref.shape[0] // HEAD_DIM):
        at = columns(first + h)
        key_rows = keys[:, at].astype(F32)
        normal = (key_rows * inverse_rms(key_rows)).astype(BF16)
        state = lax.dot_general(
            normal, values[:, at], (((0,), (0,)), ((), ())), preferred_element_type=F32
        )
        out_ref[h * HEAD_DIM : (h + 1) * HEAD_DIM, :] = state.astype(out_ref.dtype)


def first_kernel(key_ref, value_ref, out_ref, keys, values, sems):
    mine, other = core_heads()
    copies = []
    for n, first in enumerate((other, mine)):
        at = columns(first, HEADS // 2)
        for s, (ref, held) in enumerate(((key_ref, keys), (value_ref, values))):
            copies.append(pltpu.make_async_copy(ref.at[:, at], held.at[:, at], sems.at[n, s]))
            copies[-1].start()
    copies[0].wait()
    copies[1].wait()
    states_of(other, keys, values, out_ref)
    copies[2].wait()
    copies[3].wait()


def outgoing_state(keys, values):
    dim, half = HEAD_DIM, HEADS // 2
    rows = keys.shape[0]
    keys, values = (pltpu.with_memory_space_constraint(x, pltpu.HBM) for x in (keys, values))
    return pl.pallas_call(
        first_kernel,
        out_shape=[pltpu.VMEM((half * dim, dim), BF16)] + [pltpu.VMEM(keys.shape, BF16)] * 2,
        in_specs=[IN_HBM, IN_HBM],
        out_specs=[WHOLE] * 3,
        scratch_shapes=[pltpu.SemaphoreType.DMA((2, 2))],
        compiler_params=PARAMS,
        cost_estimate=pl.CostEstimate(
            flops=2 * half * rows * dim * dim, bytes_accessed=8 * half * rows * dim, transcendentals=0
        ),
    )(keys, values)


def own_kernel(key_ref, value_ref, out_ref):
    states_of(core_heads()[0], key_ref, value_ref, out_ref)


def own_state(keys, values):
    dim, half = HEAD_DIM, HEADS // 2
    rows = keys.shape[0]
    return pl.pallas_call(
        own_kernel,
        out_shape=pltpu.VMEM((half * dim, dim), F32),
        in_specs=[WHOLE, WHOLE],
        out_specs=WHOLE,
        compiler_params=PARAMS,
        cost_estimate=pl.CostEstimate(
            flops=2 * half * rows * dim * dim, bytes_accessed=8 * half * rows * dim, transcendentals=0
        ),
    )(*in_vmem(keys, values))


def piece_kernel(mine_ref, other_ref, own_ref, *piece_refs):
    chip = lax.axis_index("chip")
    rows = own_ref.shape[0]
    for d, ref in enumerate((own_ref,) + piece_refs):
        at = pl.ds(pl.multiple_of((chip ^ d) * rows, rows), rows)
        ref[...] = (mine_ref[at, :] + other_ref[at, :].astype(F32)).astype(ref.dtype)


def chip_pieces(mine, other, chips):
    shape = (mine.shape[0] // chips, HEAD_DIM)
    return pl.pallas_call(
        piece_kernel,
        out_shape=[pltpu.VMEM(shape, F32)] + [pltpu.VMEM(shape, BF16)] * (chips - 1),
        in_specs=[WHOLE, WHOLE],
        out_specs=[WHOLE] * chips,
        compiler_params=PARAMS,
        cost_estimate=SMALL,
    )(*in_vmem(mine, other))


def sum_kernel(after_ref, own_ref, *refs):
    total = own_ref[...]
    for ref in refs[:-1]:
        total = total + ref[...].astype(F32)
    refs[-1][...] = total.astype(refs[-1].dtype)


def sum_pieces(after, own, parts, dtype):
    return pl.pallas_call(
        sum_kernel,
        out_shape=pltpu.VMEM(own.shape, dtype),
        in_specs=[ANYWHERE] + [WHOLE] * (1 + len(parts)),
        out_specs=WHOLE,
        compiler_params=PARAMS,
        cost_estimate=SMALL,
    )(after, *in_vmem(own, *parts))


def slot_kernel(own_ref, near_ref, out_ref):
    near = near_ref[...].astype(F32)
    both = own_ref[...].astype(F32) + near
    out_ref[...] = jnp.where(lax.axis_index("frame") == 0, both, near).astype(BF16)


def choose_slot(own, near):
    return pl.pallas_call(
        slot_kernel,
        out_shape=pltpu.VMEM(near.shape, BF16),
        in_specs=[WHOLE] * 2,
        out_specs=WHOLE,
        compiler_params=PARAMS,
        cost_estimate=SMALL,
    )(*in_vmem(own, near))


def pack_kernel(after, plain, pairs, *refs):
    out_ref, refs = refs[-1], refs[after:-1]
    row = 0
    for ref in refs[:plain]:
        out_ref[row : row + ref.shape[0], :] = ref[...]
        row += ref.shape[0]
    for n in range(pairs):
        first, second = refs[plain + n], refs[plain + pairs + n]
        chosen = jnp.where(
            lax.axis_index("frame") == 2, first[...].astype(F32), second[...].astype(F32)
        )
        out_ref[row : row + first.shape[0], :] = chosen.astype(BF16)
        row += first.shape[0]


def pack(plain, pairs, after):
    firsts, seconds = [p[0] for p in pairs], [p[1] for p in pairs]
    rows = sum(array.shape[0] for array in plain + firsts)
    return pl.pallas_call(
        functools.partial(pack_kernel, len(after), len(plain), len(pairs)),
        out_shape=pltpu.VMEM((rows, HEAD_DIM), BF16),
        in_specs=[ANYWHERE] * len(after) + [WHOLE] * (len(plain) + 2 * len(pairs)),
        out_specs=WHOLE,
        compiler_params=PARAMS,
        cost_estimate=SMALL,
    )(*after, *in_vmem(*plain, *firsts, *seconds))


def local_kernel(
    coefs, turn, length_ref, back_ref, query_ref, key_ref, value_ref, weight_ref, after_ref, local_ref, *read_refs
):
    tokens = query_ref.shape[0]
    first = core_heads()[turn]
    heads = local_ref.shape[1] // HEAD_DIM
    key_at = lax.broadcasted_iota(jnp.int32, (tokens, tokens), 0)
    query_at = lax.broadcasted_iota(jnp.int32, (tokens, tokens), 1)
    start = jnp.int32(0)
    floor = jnp.zeros((tokens, tokens), jnp.int32)
    for k in range(length_ref.shape[1]):
        lowest = jnp.maximum(start - back_ref[0, k], 0)
        floor = jnp.where(query_at >= start, lowest, floor)
        start = start + length_ref[0, k]
    hidden = jnp.where((key_at <= query_at) & (key_at >= floor), 0.0, -jnp.inf).astype(F32)
    scale = math.log2(math.e) / math.sqrt(HEAD_DIM)
    ones = jnp.full((HEAD_DIM, HEAD_DIM), 1.0 / HEAD_DIM, BF16)
    half = HEADS // 2
    by_slot = []
    for slot_coefs in coefs(lax.axis_index("frame")):
        total = None
        for level, coef in slot_coefs:
            term = weight_ref[1 + level, pl.ds(first, heads), :] * coef
            total = term if total is None else total + term
        by_slot.append(total)
    pad = -len(by_slot) * heads % HEAD_DIM
    gains = jnp.concatenate(by_slot + [jnp.zeros((pad, tokens), F32)], 0).T

    def scores_of(h):
        at = columns(first + h)
        return lax.dot_general(
            key_ref[:, at], query_ref[:, at], (((1,), (1,)), ((), ())), preferred_element_type=F32
        )

    upcoming = scores_of(0)
    for h in range(heads):
        scores = upcoming * scale + hidden
        if h + 1 < heads:
            upcoming = scores_of(h + 1)
        weights = jnp.exp2(scores - jnp.max(scores, 0, keepdims=True))
        total = jnp.sum(weights, 0, keepdims=True)
        weights = weights * (weight_ref[0, pl.ds(first + h, 1), :] / total)
        at = slice(h * HEAD_DIM, (h + 1) * HEAD_DIM)
        local_ref[:, at] = lax.dot_general(
            weights.astype(BF16),
            value_ref[:, columns(first + h)],
            (((0,), (0,)), ((), ())),
            preferred_element_type=F32,
        )
        query = query_ref[:, columns(first + h)].astype(F32)
        mean = jnp.dot((query * query).astype(BF16), ones, preferred_element_type=F32)
        query = query * lax.rsqrt(mean + EPSILON)
        for slot, read_ref in enumerate(read_refs):
            which = slot * heads + h
            read_ref[:, at] = (query * gains[:, which : which + 1]).astype(BF16)


def local_part(coefs, slots, turn, frame_len, window_back, queries, keys, values, weights, after):
    tokens, width = queries.shape
    width //= 2
    return pl.pallas_call(
        functools.partial(local_kernel, coefs, turn),
        out_shape=[pltpu.VMEM((tokens, width), F32)] + [pltpu.VMEM((tokens, width), BF16)] * slots,
        in_specs=[SCALARS] * 2 + [WHOLE] * 4 + [ANYWHERE],
        out_specs=[WHOLE] * (1 + slots),
        compiler_params=PARAMS,
        cost_estimate=pl.CostEstimate(
            flops=4 * tokens * tokens * width,
            bytes_accessed=14 * tokens * width,
            transcendentals=tokens * width,
        ),
    )(frame_len, window_back, queries, *in_vmem(keys, values), weights, after)


def read_heads(d, chips, base_ref, states):
    count = HEADS // 2 // chips
    first = (lax.axis_index("chip") ^ d) * count
    for h in range(count):
        at = columns(first + h)
        result = base_ref[:, at]
        for read_ref, state_ref, row in states:
            result = result + jnp.dot(
                read_ref[:, at],
                state_ref[row + h * HEAD_DIM : row + (h + 1) * HEAD_DIM, :],
                preferred_element_type=F32,
            )
        yield at, result


def middle_kernel(chips, early, local_ref, x_ref, y_ref, state_ref, out_ref):
    rows = state_ref.shape[0] // (chips + early)
    for d in range(chips):
        states = [(x_ref, state_ref, d * rows)]
        if d < early:
            states.append((y_ref, state_ref, (chips + d) * rows))
        for at, result in read_heads(d, chips, local_ref, states):
            out_ref[:, at] = result


def read_middle(chips, early, local, x, y, states):
    return pl.pallas_call(
        functools.partial(middle_kernel, chips, early),
        out_shape=pltpu.VMEM(local.shape, F32),
        in_specs=[WHOLE] * 4,
        out_specs=WHOLE,
        compiler_params=PARAMS,
        cost_estimate=pl.CostEstimate(
            flops=2 * local.size * HEAD_DIM, bytes_accessed=8 * local.size, transcendentals=0
        ),
    )(*in_vmem(local, x, y, states))


def late_half(chips, early, base_ref, y_ref, *refs):
    out_ref = refs[-1]
    for d in range(chips):
        states = [(y_ref, refs[0], 0)] if d >= early else []
        for at, result in read_heads(d, chips, base_ref, states):
            out_ref[:, at] = result.astype(BF16)


def read_late(chips, early, base, y, states):
    return pl.pallas_call(
        functools.partial(late_half, chips, early),
        out_shape=pltpu.VMEM(base.shape, BF16),
        in_specs=[WHOLE] * (2 + len(states)),
        out_specs=WHOLE,
        compiler_params=PARAMS,
        cost_estimate=pl.CostEstimate(
            flops=base.size * HEAD_DIM, bytes_accessed=6 * base.size, transcendentals=0
        ),
    )(*in_vmem(base, y, *states))


def last_kernel(chips, early, done_ref, base_ref, y_ref, *refs):
    *state_refs, out_ref, held, sems = refs
    mine, other = core_heads()
    first = pltpu.make_async_copy(done_ref, out_ref.at[:, columns(mine, HEADS // 2)], sems.at[0])
    first.start()
    late_half(chips, early, base_ref, y_ref, *state_refs, held)
    second = pltpu.make_async_copy(held, out_ref.at[:, columns(other, HEADS // 2)], sems.at[1])
    second.start()
    first.wait()
    second.wait()


def read_last(chips, early, done, base, y, states):
    tokens, width = base.shape
    return pl.pallas_call(
        functools.partial(last_kernel, chips, early),
        out_shape=jax.ShapeDtypeStruct((tokens, 2 * width), BF16),
        in_specs=[WHOLE] * (3 + len(states)),
        out_specs=ANYWHERE,
        scratch_shapes=[pltpu.VMEM((tokens, width), BF16), pltpu.SemaphoreType.DMA((2,))],
        compiler_params=PARAMS,
        cost_estimate=pl.CostEstimate(
            flops=base.size * HEAD_DIM, bytes_accessed=10 * base.size, transcendentals=0
        ),
    )(*in_vmem(done, base, y, *states))


def swap(array, axis, mask, size):
    return lax.ppermute(array, axis, [(n, n ^ mask) for n in range(size)])


def from_first(array, target, frames):
    places = {0: target, target: 0}
    return lax.ppermute(array, "frame", [(f, places.get(f, f)) for f in range(frames)])


def body(sizes, queries, keys, values, level_weight, frame_len, window_back):
    frames, outer, chips = sizes
    low, high = (
        1.0 / math.sqrt(HEAD_DIM * 2**level * queries.shape[0] * outer * chips * 2) for level in (0, 1)
    )

    def coefs(f):
        return [[(0, jnp.where(f % 2 == 1, low, 0.0))], [(1, jnp.where(f >= 2, high, 0.0))]]

    local = functools.partial(local_part, coefs, 2)
    rest = (frame_len, window_back, queries)
    early = chips - 1 if chips > 1 else 1

    outgoing, keys, values = outgoing_state(keys, values)
    incoming = swap(outgoing, "core", 1, 2)
    mine = own_state(keys, values)
    own, *sends = chip_pieces(mine, incoming, chips)
    got = [swap(sends[d - 1], "chip", d, chips) for d in reversed(range(1, chips))]
    local_0, x_0, y_0 = local(0, *rest, keys, values, level_weight, own)
    state = sum_pieces(local_0, own, got, F32 if outer > 1 else BF16)
    if outer > 1:
        state = lax.psum(state, "outer").astype(BF16)
    slot = choose_slot(state, swap(state, "frame", 1, frames))

    x = [slot] + [swap(slot, "chip", d, chips) for d in range(1, chips)]
    local_1, x_1, y_1 = local(1, *rest, keys, values, level_weight, slot)
    fan = [pack(x[:2], [], [local_1])] + x[2:]
    pairs = [(from_first(piece, 2, frames), from_first(piece, 3, frames)) for piece in fan]
    late = pairs[1:][-1:]
    own_states = pack(x, pairs[: len(pairs) - len(late)], [])
    other_states = swap(own_states, "core", 1, 2)
    base_0 = read_middle(chips, early, local_0, x_0, y_0, own_states)
    base_1 = read_middle(chips, early, local_1, x_1, y_1, other_states)
    late, base_0, base_1 = lax.optimization_barrier((late, base_0, base_1))
    late_own = [pack([], late, [])] if late else []
    late_other = [swap(piece, "core", 1, 2) for piece in late_own]
    done = read_late(chips, early, base_0, y_0, late_own)
    return read_last(chips, early, done, base_1, y_1, late_other)


def solution(mesh):
    frames, space = mesh.shape["frame"], mesh.shape["space"]
    chips = 1
    while HEADS % (chips * 4) == 0 and space % (chips * 4) == 0 and chips < 4:
        chips *= 2
    sizes = (frames, space // (2 * chips), chips)
    names = ("frame", "outer", "chip", "core")
    fine = Mesh(mesh.devices.reshape(sizes + (2,)), names)
    rows = P(names, None)
    return jax.shard_map(
        functools.partial(body, sizes),
        mesh=fine,
        in_specs=(rows, rows, rows, P(None, None, names), rows, rows),
        out_specs=rows,
        check_vma=False,
    )
```

```python
import functools
import math

import jax
import jax.numpy as jnp
from jax import lax
from jax.experimental import pallas as pl
from jax.experimental.pallas import tpu as pltpu
from jax.sharding import Mesh, PartitionSpec as P

HEADS = 24
HEAD_DIM = 128
EPSILON = 1e-06
VMEM_LIMIT = 40 * 1024 * 1024

F32, BF16 = jnp.float32, jnp.bfloat16
WHOLE = pl.BlockSpec(memory_space=pltpu.VMEM)
SCALARS = pl.BlockSpec(memory_space=pltpu.SMEM)
ANYWHERE = pl.BlockSpec(memory_space=pl.ANY)
IN_HBM = pl.BlockSpec(memory_space=pltpu.HBM)
SMALL = pl.CostEstimate(flops=1024, bytes_accessed=1024, transcendentals=0)
PARAMS = pltpu.CompilerParams(vmem_limit_bytes=VMEM_LIMIT)


def inverse_rms(rows):
    return lax.rsqrt(jnp.mean(rows * rows, -1, keepdims=True) + EPSILON)


def columns(head, count=1):
    return pl.ds(pl.multiple_of(head * HEAD_DIM, HEAD_DIM), count * HEAD_DIM)


def core_heads():
    core = lax.axis_index("core")
    return core * (HEADS // 2), (1 - core) * (HEADS // 2)


def in_vmem(*arrays):
    return [pltpu.with_memory_space_constraint(array, pltpu.VMEM) for array in arrays]


def states_of(first, keys, values, out_ref):
    for h in range(out_ref.shape[0] // HEAD_DIM):
        at = columns(first + h)
        key_rows = keys[:, at].astype(F32)
        normal = (key_rows * inverse_rms(key_rows)).astype(BF16)
        state = lax.dot_general(
            normal, values[:, at], (((0,), (0,)), ((), ())), preferred_element_type=F32
        )
        out_ref[h * HEAD_DIM : (h + 1) * HEAD_DIM, :] = state.astype(out_ref.dtype)


def first_kernel(key_ref, value_ref, out_ref, keys, values, sems):
    mine, other = core_heads()
    copies = []
    for n, first in enumerate((other, mine)):
        at = columns(first, HEADS // 2)
        for s, (ref, held) in enumerate(((key_ref, keys), (value_ref, values))):
            copies.append(pltpu.make_async_copy(ref.at[:, at], held.at[:, at], sems.at[n, s]))
            copies[-1].start()
    copies[0].wait()
    copies[1].wait()
    states_of(other, keys, values, out_ref)
    copies[2].wait()
    copies[3].wait()


def outgoing_state(keys, values):
    dim, half = HEAD_DIM, HEADS // 2
    rows = keys.shape[0]
    keys, values = (pltpu.with_memory_space_constraint(x, pltpu.HBM) for x in (keys, values))
    return pl.pallas_call(
        first_kernel,
        out_shape=[pltpu.VMEM((half * dim, dim), BF16)] + [pltpu.VMEM(keys.shape, BF16)] * 2,
        in_specs=[IN_HBM, IN_HBM],
        out_specs=[WHOLE] * 3,
        scratch_shapes=[pltpu.SemaphoreType.DMA((2, 2))],
        compiler_params=PARAMS,
        cost_estimate=pl.CostEstimate(
            flops=2 * half * rows * dim * dim, bytes_accessed=8 * half * rows * dim, transcendentals=0
        ),
    )(keys, values)


def own_kernel(key_ref, value_ref, out_ref):
    states_of(core_heads()[0], key_ref, value_ref, out_ref)


def own_state(keys, values):
    dim, half = HEAD_DIM, HEADS // 2
    rows = keys.shape[0]
    return pl.pallas_call(
        own_kernel,
        out_shape=pltpu.VMEM((half * dim, dim), F32),
        in_specs=[WHOLE, WHOLE],
        out_specs=WHOLE,
        compiler_params=PARAMS,
        cost_estimate=pl.CostEstimate(
            flops=2 * half * rows * dim * dim, bytes_accessed=8 * half * rows * dim, transcendentals=0
        ),
    )(*in_vmem(keys, values))


def piece_kernel(mine_ref, other_ref, own_ref, *piece_refs):
    chip = lax.axis_index("chip")
    rows = own_ref.shape[0]
    for d, ref in enumerate((own_ref,) + piece_refs):
        at = pl.ds(pl.multiple_of((chip ^ d) * rows, rows), rows)
        ref[...] = (mine_ref[at, :] + other_ref[at, :].astype(F32)).astype(ref.dtype)


def chip_pieces(mine, other, chips):
    shape = (mine.shape[0] // chips, HEAD_DIM)
    return pl.pallas_call(
        piece_kernel,
        out_shape=[pltpu.VMEM(shape, F32)] + [pltpu.VMEM(shape, BF16)] * (chips - 1),
        in_specs=[WHOLE, WHOLE],
        out_specs=[WHOLE] * chips,
        compiler_params=PARAMS,
        cost_estimate=SMALL,
    )(*in_vmem(mine, other))


def sum_kernel(after_ref, own_ref, *refs):
    total = own_ref[...]
    for ref in refs[:-1]:
        total = total + ref[...].astype(F32)
    refs[-1][...] = total.astype(refs[-1].dtype)


def sum_pieces(after, own, parts, dtype):
    return pl.pallas_call(
        sum_kernel,
        out_shape=pltpu.VMEM(own.shape, dtype),
        in_specs=[ANYWHERE] + [WHOLE] * (1 + len(parts)),
        out_specs=WHOLE,
        compiler_params=PARAMS,
        cost_estimate=SMALL,
    )(after, *in_vmem(own, *parts))


def slot_kernel(near_ref, across_ref, diagonal_ref, out_ref):
    both = across_ref[...].astype(F32) + diagonal_ref[...].astype(F32)
    near = near_ref[...].astype(F32)
    out_ref[...] = jnp.where(lax.axis_index("frame") == 2, both, near).astype(BF16)


def choose_slot(near, across, diagonal):
    return pl.pallas_call(
        slot_kernel,
        out_shape=pltpu.VMEM(near.shape, BF16),
        in_specs=[WHOLE] * 3,
        out_specs=WHOLE,
        compiler_params=PARAMS,
        cost_estimate=SMALL,
    )(*in_vmem(near, across, diagonal))


def pack_kernel(after, order, *refs):
    out_ref, refs = refs[-1], refs[after:-1]
    rows = refs[0].shape[0]
    for place, ref in zip(order, refs):
        out_ref[place * rows : (place + 1) * rows, :] = ref[...]


def pack(pieces, order, after):
    rows = sum(array.shape[0] for array in pieces)
    pieces = [pieces[place] for place in order]
    return pl.pallas_call(
        functools.partial(pack_kernel, len(after), order),
        out_shape=pltpu.VMEM((rows, HEAD_DIM), BF16),
        in_specs=[ANYWHERE] * len(after) + [WHOLE] * len(pieces),
        out_specs=WHOLE,
        compiler_params=PARAMS,
        cost_estimate=SMALL,
    )(*after, *in_vmem(*pieces))


def local_kernel(
    coefs, turn, length_ref, back_ref, query_ref, key_ref, value_ref, weight_ref, after_ref, local_ref, *read_refs
):
    tokens = query_ref.shape[0]
    first = core_heads()[turn]
    heads = local_ref.shape[1] // HEAD_DIM
    key_at = lax.broadcasted_iota(jnp.int32, (tokens, tokens), 0)
    query_at = lax.broadcasted_iota(jnp.int32, (tokens, tokens), 1)
    start = jnp.int32(0)
    floor = jnp.zeros((tokens, tokens), jnp.int32)
    for k in range(length_ref.shape[1]):
        lowest = jnp.maximum(start - back_ref[0, k], 0)
        floor = jnp.where(query_at >= start, lowest, floor)
        start = start + length_ref[0, k]
    hidden = jnp.where((key_at <= query_at) & (key_at >= floor), 0.0, -jnp.inf).astype(F32)
    scale = math.log2(math.e) / math.sqrt(HEAD_DIM)
    ones = jnp.full((HEAD_DIM, HEAD_DIM), 1.0 / HEAD_DIM, BF16)
    half = HEADS // 2
    by_slot = []
    for slot_coefs in coefs(lax.axis_index("frame")):
        total = None
        for level, coef in slot_coefs:
            term = weight_ref[1 + level, pl.ds(first, heads), :] * coef
            total = term if total is None else total + term
        by_slot.append(total)
    pad = -len(by_slot) * heads % HEAD_DIM
    gains = jnp.concatenate(by_slot + [jnp.zeros((pad, tokens), F32)], 0).T

    def scores_of(h):
        at = columns(first + h)
        return lax.dot_general(
            key_ref[:, at], query_ref[:, at], (((1,), (1,)), ((), ())), preferred_element_type=F32
        )

    upcoming = scores_of(0)
    for h in range(heads):
        scores = upcoming * scale + hidden
        if h + 1 < heads:
            upcoming = scores_of(h + 1)
        weights = jnp.exp2(scores - jnp.max(scores, 0, keepdims=True))
        total = jnp.sum(weights, 0, keepdims=True)
        weights = weights * (weight_ref[0, pl.ds(first + h, 1), :] / total)
        at = slice(h * HEAD_DIM, (h + 1) * HEAD_DIM)
        local_ref[:, at] = lax.dot_general(
            weights.astype(BF16),
            value_ref[:, columns(first + h)],
            (((0,), (0,)), ((), ())),
            preferred_element_type=F32,
        )
        query = query_ref[:, columns(first + h)].astype(F32)
        mean = jnp.dot((query * query).astype(BF16), ones, preferred_element_type=F32)
        query = query * lax.rsqrt(mean + EPSILON)
        for slot, read_ref in enumerate(read_refs):
            which = slot * heads + h
            read_ref[:, at] = (query * gains[:, which : which + 1]).astype(BF16)


def local_part(coefs, slots, turn, frame_len, window_back, queries, keys, values, weights, after):
    tokens, width = queries.shape
    width //= 2
    return pl.pallas_call(
        functools.partial(local_kernel, coefs, turn),
        out_shape=[pltpu.VMEM((tokens, width), F32)] + [pltpu.VMEM((tokens, width), BF16)] * slots,
        in_specs=[SCALARS] * 2 + [WHOLE] * 4 + [ANYWHERE],
        out_specs=[WHOLE] * (1 + slots),
        compiler_params=PARAMS,
        cost_estimate=pl.CostEstimate(
            flops=4 * tokens * tokens * width,
            bytes_accessed=14 * tokens * width,
            transcendentals=tokens * width,
        ),
    )(frame_len, window_back, queries, *in_vmem(keys, values), weights, after)


def read_heads(d, chips, base_ref, states):
    count = HEADS // 2 // chips
    first = (lax.axis_index("chip") ^ d) * count
    for h in range(count):
        at = columns(first + h)
        result = base_ref[:, at]
        for read_ref, state_ref, row in states:
            result = result + jnp.dot(
                read_ref[:, at],
                state_ref[row + h * HEAD_DIM : row + (h + 1) * HEAD_DIM, :],
                preferred_element_type=F32,
            )
        yield at, result


def middle_kernel(chips, early, local_ref, x_ref, y_ref, state_ref, out_ref):
    rows = state_ref.shape[0] // (chips + early)
    for d in range(chips):
        states = [(x_ref, state_ref, d * rows)]
        if d < early:
            states.append((y_ref, state_ref, (chips + d) * rows))
        for at, result in read_heads(d, chips, local_ref, states):
            out_ref[:, at] = result


def read_middle(chips, early, local, x, y, states):
    return pl.pallas_call(
        functools.partial(middle_kernel, chips, early),
        out_shape=pltpu.VMEM(local.shape, F32),
        in_specs=[WHOLE] * 4,
        out_specs=WHOLE,
        compiler_params=PARAMS,
        cost_estimate=pl.CostEstimate(
            flops=2 * local.size * HEAD_DIM, bytes_accessed=8 * local.size, transcendentals=0
        ),
    )(*in_vmem(local, x, y, states))


def late_half(chips, early, base_ref, y_ref, *refs):
    out_ref = refs[-1]
    for d in range(chips):
        states = [(y_ref, refs[0], 0)] if d >= early else []
        for at, result in read_heads(d, chips, base_ref, states):
            out_ref[:, at] = result.astype(BF16)


def read_late(chips, early, base, y, states):
    return pl.pallas_call(
        functools.partial(late_half, chips, early),
        out_shape=pltpu.VMEM(base.shape, BF16),
        in_specs=[WHOLE] * (2 + len(states)),
        out_specs=WHOLE,
        compiler_params=PARAMS,
        cost_estimate=pl.CostEstimate(
            flops=base.size * HEAD_DIM, bytes_accessed=6 * base.size, transcendentals=0
        ),
    )(*in_vmem(base, y, *states))


def last_kernel(chips, early, done_ref, base_ref, y_ref, *refs):
    *state_refs, out_ref, held, sems = refs
    mine, other = core_heads()
    first = pltpu.make_async_copy(done_ref, out_ref.at[:, columns(mine, HEADS // 2)], sems.at[0])
    first.start()
    late_half(chips, early, base_ref, y_ref, *state_refs, held)
    second = pltpu.make_async_copy(held, out_ref.at[:, columns(other, HEADS // 2)], sems.at[1])
    second.start()
    first.wait()
    second.wait()


def read_last(chips, early, done, base, y, states):
    tokens, width = base.shape
    return pl.pallas_call(
        functools.partial(last_kernel, chips, early),
        out_shape=jax.ShapeDtypeStruct((tokens, 2 * width), BF16),
        in_specs=[WHOLE] * (3 + len(states)),
        out_specs=ANYWHERE,
        scratch_shapes=[pltpu.VMEM((tokens, width), BF16), pltpu.SemaphoreType.DMA((2,))],
        compiler_params=PARAMS,
        cost_estimate=pl.CostEstimate(
            flops=base.size * HEAD_DIM, bytes_accessed=10 * base.size, transcendentals=0
        ),
    )(*in_vmem(done, base, y, *states))


def swap(array, axis, mask, size):
    return lax.ppermute(array, axis, [(n, n ^ mask) for n in range(size)])


def body(sizes, queries, keys, values, level_weight, frame_len, window_back):
    frames, outer, chips = sizes
    low, high = (
        1.0 / math.sqrt(HEAD_DIM * 2**level * queries.shape[0] * outer * chips * 2) for level in (0, 1)
    )

    def coefs(f):
        x_low = jnp.where(f % 2 == 1, low, 0.0)
        x_high = jnp.where(f == 2, high, 0.0)
        return [[(0, x_low), (1, x_high)], [(1, jnp.where(f == 3, high, 0.0))]]

    local = functools.partial(local_part, coefs, 2)
    rest = (frame_len, window_back, queries)
    early = max(chips - 1, 1)

    outgoing, keys, values = outgoing_state(keys, values)
    incoming = swap(outgoing, "core", 1, 2)
    mine = own_state(keys, values)
    own, *sends = chip_pieces(mine, incoming, chips)
    got = [swap(sends[d - 1], "chip", d, chips) for d in reversed(range(1, chips))]
    local_0, x_0, y_0 = local(0, *rest, keys, values, level_weight, own)
    state = sum_pieces(local_0, own, got, F32 if outer > 1 else BF16)
    if outer > 1:
        state = lax.psum(state, "outer").astype(BF16)
    slot = choose_slot(*(swap(state, "frame", mask, frames) for mask in (1, 2, 3)))

    x = [slot] + [swap(slot, "chip", d, chips) for d in range(1, chips)]
    y = [swap(slot, "frame", 1, frames)]
    local_1, x_1, y_1 = local(1, *rest, keys, values, level_weight, slot)
    for piece in x[1:]:
        piece, _ = lax.optimization_barrier((piece, local_1))
        y.append(swap(piece, "frame", 1, frames))
    late_own = y[1:][early - 1 :]
    places = [0, *range(chips + early - 1, chips - 1, -1), *range(1, chips)]
    own_states = pack(x + y[:early], places, [local_1])
    other_states = swap(own_states, "core", 1, 2)
    base_0 = read_middle(chips, early, local_0, x_0, y_0, own_states)
    base_1 = read_middle(chips, early, local_1, x_1, y_1, other_states)
    late_own, base_0, base_1 = lax.optimization_barrier((late_own, base_0, base_1))
    late_other = [swap(piece, "core", 1, 2) for piece in late_own]
    done = read_late(chips, early, base_0, y_0, late_own)
    return read_last(chips, early, done, base_1, y_1, late_other)


def solution(mesh):
    frames, space = mesh.shape["frame"], mesh.shape["space"]
    chips = 1
    while HEADS % (chips * 4) == 0 and space % (chips * 4) == 0 and chips < 4:
        chips *= 2
    sizes = (frames, space // (2 * chips), chips)
    names = ("frame", "outer", "chip", "core")
    fine = Mesh(mesh.devices.reshape(sizes + (2,)), names)
    rows = P(names, None)
    return jax.shard_map(
        functools.partial(body, sizes),
        mesh=fine,
        in_specs=(rows, rows, rows, P(None, None, names), rows, rows),
        out_specs=rows,
        check_vma=False,
    )
```

```python
import functools
import math

import jax
import jax.numpy as jnp
from jax import lax
from jax.experimental import pallas as pl
from jax.experimental.pallas import tpu as pltpu
from jax.sharding import Mesh, PartitionSpec as P

HEADS = 24
HEAD_DIM = 128
EPSILON = 1e-06
VMEM_LIMIT = 40 * 1024 * 1024

F32, BF16 = jnp.float32, jnp.bfloat16
WHOLE = pl.BlockSpec(memory_space=pltpu.VMEM)
SCALARS = pl.BlockSpec(memory_space=pltpu.SMEM)
ANYWHERE = pl.BlockSpec(memory_space=pl.ANY)
IN_HBM = pl.BlockSpec(memory_space=pltpu.HBM)
SMALL = pl.CostEstimate(flops=1024, bytes_accessed=1024, transcendentals=0)
LARGE = pl.CostEstimate(flops=2 * 10**10, bytes_accessed=1024, transcendentals=0)
PARAMS = pltpu.CompilerParams(vmem_limit_bytes=VMEM_LIMIT)


def inverse_rms(rows):
    return lax.rsqrt(jnp.mean(rows * rows, -1, keepdims=True) + EPSILON)


def columns(head, count=1):
    return pl.ds(pl.multiple_of(head * HEAD_DIM, HEAD_DIM), count * HEAD_DIM)


def core_heads():
    core = lax.axis_index("core")
    return core * (HEADS // 2), (1 - core) * (HEADS // 2)


def in_vmem(*arrays):
    return [pltpu.with_memory_space_constraint(array, pltpu.VMEM) for array in arrays]


def states_of(first, keys, values, out_ref):
    for h in range(out_ref.shape[0] // HEAD_DIM):
        at = columns(first + h)
        key_rows = keys[:, at].astype(F32)
        normal = (key_rows * inverse_rms(key_rows)).astype(BF16)
        state = lax.dot_general(
            normal, values[:, at], (((0,), (0,)), ((), ())), preferred_element_type=F32
        )
        out_ref[h * HEAD_DIM : (h + 1) * HEAD_DIM, :] = state.astype(out_ref.dtype)


def first_kernel(key_ref, value_ref, out_ref, keys, values, sems):
    mine, other = core_heads()
    copies = []
    for n, first in enumerate((other, mine)):
        at = columns(first, HEADS // 2)
        for s, (ref, held) in enumerate(((key_ref, keys), (value_ref, values))):
            copies.append(pltpu.make_async_copy(ref.at[:, at], held.at[:, at], sems.at[n, s]))
            copies[-1].start()
    copies[0].wait()
    copies[1].wait()
    states_of(other, keys, values, out_ref)
    copies[2].wait()
    copies[3].wait()


def outgoing_state(keys, values):
    dim, half = HEAD_DIM, HEADS // 2
    rows = keys.shape[0]
    keys, values = (pltpu.with_memory_space_constraint(x, pltpu.HBM) for x in (keys, values))
    return pl.pallas_call(
        first_kernel,
        out_shape=[pltpu.VMEM((half * dim, dim), BF16)] + [pltpu.VMEM(keys.shape, BF16)] * 2,
        in_specs=[IN_HBM, IN_HBM],
        out_specs=[WHOLE] * 3,
        scratch_shapes=[pltpu.SemaphoreType.DMA((2, 2))],
        compiler_params=PARAMS,
        cost_estimate=pl.CostEstimate(
            flops=2 * half * rows * dim * dim, bytes_accessed=8 * half * rows * dim, transcendentals=0
        ),
    )(keys, values)


def own_kernel(key_ref, value_ref, out_ref):
    states_of(core_heads()[0], key_ref, value_ref, out_ref)


def own_state(keys, values):
    dim, half = HEAD_DIM, HEADS // 2
    rows = keys.shape[0]
    return pl.pallas_call(
        own_kernel,
        out_shape=pltpu.VMEM((half * dim, dim), F32),
        in_specs=[WHOLE, WHOLE],
        out_specs=WHOLE,
        compiler_params=PARAMS,
        cost_estimate=pl.CostEstimate(
            flops=2 * half * rows * dim * dim, bytes_accessed=8 * half * rows * dim, transcendentals=0
        ),
    )(*in_vmem(keys, values))


def piece_kernel(mine_ref, other_ref, own_ref, *piece_refs):
    chip = lax.axis_index("chip")
    rows = own_ref.shape[0]
    for d, ref in enumerate((own_ref,) + piece_refs):
        at = pl.ds(pl.multiple_of((chip ^ d) * rows, rows), rows)
        ref[...] = (mine_ref[at, :] + other_ref[at, :].astype(F32)).astype(ref.dtype)


def chip_pieces(mine, other, chips):
    shape = (mine.shape[0] // chips, HEAD_DIM)
    return pl.pallas_call(
        piece_kernel,
        out_shape=[pltpu.VMEM(shape, F32)] + [pltpu.VMEM(shape, BF16)] * (chips - 1),
        in_specs=[WHOLE, WHOLE],
        out_specs=[WHOLE] * chips,
        compiler_params=PARAMS,
        cost_estimate=SMALL,
    )(*in_vmem(mine, other))


def sum_kernel(after_ref, own_ref, *refs):
    total = own_ref[...]
    for ref in refs[:-1]:
        total = total + ref[...].astype(F32)
    refs[-1][...] = total.astype(refs[-1].dtype)


def sum_pieces(after, own, parts, dtype):
    return pl.pallas_call(
        sum_kernel,
        out_shape=pltpu.VMEM(own.shape, dtype),
        in_specs=[ANYWHERE] + [WHOLE] * (1 + len(parts)),
        out_specs=WHOLE,
        compiler_params=PARAMS,
        cost_estimate=SMALL,
    )(after, *in_vmem(own, *parts))


def slot_kernel(near_ref, across_ref, diagonal_ref, out_ref):
    both = across_ref[...].astype(F32) + diagonal_ref[...].astype(F32)
    near = near_ref[...].astype(F32)
    out_ref[...] = jnp.where(lax.axis_index("frame") == 2, both, near).astype(BF16)


def choose_slot(near, across, diagonal):
    return pl.pallas_call(
        slot_kernel,
        out_shape=pltpu.VMEM(near.shape, BF16),
        in_specs=[WHOLE] * 3,
        out_specs=WHOLE,
        compiler_params=PARAMS,
        cost_estimate=SMALL,
    )(*in_vmem(near, across, diagonal))


def pack_kernel(after, order, *refs):
    out_ref, refs = refs[-1], refs[after:-1]
    rows = refs[0].shape[0]
    for place, ref in zip(order, refs):
        out_ref[place * rows : (place + 1) * rows, :] = ref[...]


def pack(pieces, order, after):
    rows = sum(array.shape[0] for array in pieces)
    pieces = [pieces[place] for place in order]
    return pl.pallas_call(
        functools.partial(pack_kernel, len(after), order),
        out_shape=pltpu.VMEM((rows, HEAD_DIM), BF16),
        in_specs=[ANYWHERE] * len(after) + [WHOLE] * len(pieces),
        out_specs=WHOLE,
        compiler_params=PARAMS,
        cost_estimate=SMALL,
    )(*after, *in_vmem(*pieces))


def local_kernel(
    coefs, turn, length_ref, back_ref, query_ref, key_ref, value_ref, weight_ref, after_ref, local_ref, *read_refs
):
    tokens = query_ref.shape[0]
    first = core_heads()[turn]
    heads = local_ref.shape[1] // HEAD_DIM
    key_at = lax.broadcasted_iota(jnp.int32, (tokens, tokens), 0)
    query_at = lax.broadcasted_iota(jnp.int32, (tokens, tokens), 1)
    start = jnp.int32(0)
    floor = jnp.zeros((tokens, tokens), jnp.int32)
    for k in range(length_ref.shape[1]):
        lowest = jnp.maximum(start - back_ref[0, k], 0)
        floor = jnp.where(query_at >= start, lowest, floor)
        start = start + length_ref[0, k]
    hidden = jnp.where((key_at <= query_at) & (key_at >= floor), 0.0, -jnp.inf).astype(F32)
    scale = math.log2(math.e) / math.sqrt(HEAD_DIM)
    ones = jnp.full((HEAD_DIM, HEAD_DIM), 1.0 / HEAD_DIM, BF16)
    half = HEADS // 2
    by_slot = []
    for slot_coefs in coefs(lax.axis_index("frame")):
        total = None
        for level, coef in slot_coefs:
            term = weight_ref[1 + level, pl.ds(first, heads), :] * coef
            total = term if total is None else total + term
        by_slot.append(total)
    pad = -len(by_slot) * heads % HEAD_DIM
    gains = jnp.concatenate(by_slot + [jnp.zeros((pad, tokens), F32)], 0).T

    def scores_of(h):
        at = columns(first + h)
        return lax.dot_general(
            key_ref[:, at], query_ref[:, at], (((1,), (1,)), ((), ())), preferred_element_type=F32
        )

    upcoming = scores_of(0)
    for h in range(heads):
        scores = upcoming * scale + hidden
        if h + 1 < heads:
            upcoming = scores_of(h + 1)
        weights = jnp.exp2(scores - jnp.max(scores, 0, keepdims=True))
        total = jnp.sum(weights, 0, keepdims=True)
        weights = weights * (weight_ref[0, pl.ds(first + h, 1), :] / total)
        at = slice(h * HEAD_DIM, (h + 1) * HEAD_DIM)
        local_ref[:, at] = lax.dot_general(
            weights.astype(BF16),
            value_ref[:, columns(first + h)],
            (((0,), (0,)), ((), ())),
            preferred_element_type=F32,
        )
        query = query_ref[:, columns(first + h)].astype(F32)
        mean = jnp.dot((query * query).astype(BF16), ones, preferred_element_type=F32)
        query = query * lax.rsqrt(mean + EPSILON)
        for slot, read_ref in enumerate(read_refs):
            which = slot * heads + h
            read_ref[:, at] = (query * gains[:, which : which + 1]).astype(BF16)


def local_part(coefs, slots, turn, frame_len, window_back, queries, keys, values, weights, after):
    tokens, width = queries.shape
    width //= 2
    return pl.pallas_call(
        functools.partial(local_kernel, coefs, turn),
        out_shape=[pltpu.VMEM((tokens, width), F32)] + [pltpu.VMEM((tokens, width), BF16)] * slots,
        in_specs=[SCALARS] * 2 + [WHOLE] * 4 + [ANYWHERE],
        out_specs=[WHOLE] * (1 + slots),
        compiler_params=PARAMS,
        cost_estimate=pl.CostEstimate(
            flops=4 * tokens * tokens * width,
            bytes_accessed=14 * tokens * width,
            transcendentals=tokens * width,
        ),
    )(frame_len, window_back, queries, *in_vmem(keys, values), weights, after)


def read_heads(d, chips, base_ref, states):
    count = HEADS // 2 // chips
    first = (lax.axis_index("chip") ^ d) * count
    for h in range(count):
        at = columns(first + h)
        result = base_ref[:, at]
        for read_ref, state_ref, row in states:
            result = result + jnp.dot(
                read_ref[:, at],
                state_ref[row + h * HEAD_DIM : row + (h + 1) * HEAD_DIM, :],
                preferred_element_type=F32,
            )
        yield at, result


def middle_kernel(chips, early, local_ref, x_ref, y_ref, state_ref, out_ref):
    rows = state_ref.shape[0] // (chips + early)
    for d in range(chips):
        states = [(x_ref, state_ref, d * rows)]
        if d < early:
            states.append((y_ref, state_ref, (chips + d) * rows))
        for at, result in read_heads(d, chips, local_ref, states):
            out_ref[:, at] = result


def read_middle(chips, early, local, x, y, states):
    return pl.pallas_call(
        functools.partial(middle_kernel, chips, early),
        out_shape=pltpu.VMEM(local.shape, F32),
        in_specs=[WHOLE] * 4,
        out_specs=WHOLE,
        compiler_params=PARAMS,
        cost_estimate=LARGE,
    )(*in_vmem(local, x, y, states))


def late_half(chips, early, base_ref, y_ref, *refs):
    out_ref = refs[-1]
    rows = base_ref.shape[1] // chips
    for d in range(chips):
        states = [(y_ref, refs[0], (d - early) * rows)] if d >= early else []
        for at, result in read_heads(d, chips, base_ref, states):
            out_ref[:, at] = result.astype(BF16)


def read_late(chips, early, base, y, states):
    return pl.pallas_call(
        functools.partial(late_half, chips, early),
        out_shape=pltpu.VMEM(base.shape, BF16),
        in_specs=[WHOLE] * (2 + len(states)),
        out_specs=WHOLE,
        compiler_params=PARAMS,
        cost_estimate=pl.CostEstimate(
            flops=base.size * HEAD_DIM, bytes_accessed=6 * base.size, transcendentals=0
        ),
    )(*in_vmem(base, y, *states))


def last_kernel(chips, early, done_ref, base_ref, y_ref, *refs):
    *state_refs, out_ref, held, sems = refs
    mine, other = core_heads()
    first = pltpu.make_async_copy(done_ref, out_ref.at[:, columns(mine, HEADS // 2)], sems.at[0])
    first.start()
    late_half(chips, early, base_ref, y_ref, *state_refs, held)
    second = pltpu.make_async_copy(held, out_ref.at[:, columns(other, HEADS // 2)], sems.at[1])
    second.start()
    first.wait()
    second.wait()


def read_last(chips, early, done, base, y, states):
    tokens, width = base.shape
    return pl.pallas_call(
        functools.partial(last_kernel, chips, early),
        out_shape=jax.ShapeDtypeStruct((tokens, 2 * width), BF16),
        in_specs=[WHOLE] * (3 + len(states)),
        out_specs=ANYWHERE,
        scratch_shapes=[pltpu.VMEM((tokens, width), BF16), pltpu.SemaphoreType.DMA((2,))],
        compiler_params=PARAMS,
        cost_estimate=pl.CostEstimate(
            flops=base.size * HEAD_DIM, bytes_accessed=10 * base.size, transcendentals=0
        ),
    )(*in_vmem(done, base, y, *states))


def swap(array, axis, mask, size):
    return lax.ppermute(array, axis, [(n, n ^ mask) for n in range(size)])


def body(sizes, queries, keys, values, level_weight, frame_len, window_back):
    frames, outer, chips = sizes
    low, high = (
        1.0 / math.sqrt(HEAD_DIM * 2**level * queries.shape[0] * outer * chips * 2) for level in (0, 1)
    )

    def coefs(f):
        x_low = jnp.where(f % 2 == 1, low, 0.0)
        x_high = jnp.where(f == 2, high, 0.0)
        return [[(0, x_low), (1, x_high)], [(1, jnp.where(f == 3, high, 0.0))]]

    local = functools.partial(local_part, coefs, 2)
    rest = (frame_len, window_back, queries)
    early = 1

    outgoing, keys, values = outgoing_state(keys, values)
    incoming = swap(outgoing, "core", 1, 2)
    mine = own_state(keys, values)
    own, *sends = chip_pieces(mine, incoming, chips)
    got = [swap(sends[d - 1], "chip", d, chips) for d in reversed(range(1, chips))]
    local_0, x_0, y_0 = local(0, *rest, keys, values, level_weight, own)
    state = sum_pieces(local_0, own, got, F32 if outer > 1 else BF16)
    if outer > 1:
        state = lax.psum(state, "outer").astype(BF16)
    slot = choose_slot(*(swap(state, "frame", mask, frames) for mask in (1, 2, 3)))

    x = [slot] + [swap(slot, "chip", d, chips) for d in range(1, chips)]
    y = [swap(slot, "frame", 1, frames)]
    local_1, x_1, y_1 = local(1, *rest, keys, values, level_weight, slot)
    for piece in x[1:]:
        piece, _ = lax.optimization_barrier((piece, local_1))
        y.append(swap(piece, "frame", 1, frames))
    places = [0, *reversed(range(1, chips + early))]
    own_states = pack(x + y[:early], places, [local_1])
    other_states = swap(own_states, "core", 1, 2)
    base_0 = read_middle(chips, early, local_0, x_0, y_0, own_states)
    base_1 = read_middle(chips, early, local_1, x_1, y_1, other_states)
    late = y[early:]
    late_own = [pack(late, list(range(len(late))), [])] if late else []
    late_other = [swap(piece, "core", 1, 2) for piece in late_own]
    done = read_late(chips, early, base_0, y_0, late_own)
    return read_last(chips, early, done, base_1, y_1, late_other)


def solution(mesh):
    frames, space = mesh.shape["frame"], mesh.shape["space"]
    chips = 1
    while HEADS % (chips * 4) == 0 and space % (chips * 4) == 0 and chips < 4:
        chips *= 2
    sizes = (frames, space // (2 * chips), chips)
    names = ("frame", "outer", "chip", "core")
    fine = Mesh(mesh.devices.reshape(sizes + (2,)), names)
    rows = P(names, None)
    return jax.shard_map(
        functools.partial(body, sizes),
        mesh=fine,
        in_specs=(rows, rows, rows, P(None, None, names), rows, rows),
        out_specs=rows,
        check_vma=False,
    )
```

```python
import functools
import math

import jax
import jax.numpy as jnp
from jax import lax
from jax.experimental import pallas as pl
from jax.experimental.pallas import tpu as pltpu
from jax.sharding import Mesh, PartitionSpec as P

HEADS = 24
HEAD_DIM = 128
EPSILON = 1e-06
VMEM_LIMIT = 40 * 1024 * 1024

F32, BF16 = jnp.float32, jnp.bfloat16
WHOLE = pl.BlockSpec(memory_space=pltpu.VMEM)
SCALARS = pl.BlockSpec(memory_space=pltpu.SMEM)
ANYWHERE = pl.BlockSpec(memory_space=pl.ANY)
IN_HBM = pl.BlockSpec(memory_space=pltpu.HBM)
SMALL = pl.CostEstimate(flops=1024, bytes_accessed=1024, transcendentals=0)
LARGE = pl.CostEstimate(flops=2 * 10**10, bytes_accessed=1024, transcendentals=0)
PARAMS = pltpu.CompilerParams(vmem_limit_bytes=VMEM_LIMIT)


def inverse_rms(rows):
    return lax.rsqrt(jnp.mean(rows * rows, -1, keepdims=True) + EPSILON)


def columns(head, count=1):
    return pl.ds(pl.multiple_of(head * HEAD_DIM, HEAD_DIM), count * HEAD_DIM)


def core_heads():
    core = lax.axis_index("core")
    return core * (HEADS // 2), (1 - core) * (HEADS // 2)


def in_vmem(*arrays):
    return [pltpu.with_memory_space_constraint(array, pltpu.VMEM) for array in arrays]


def states_of(first, keys, values, out_ref, ready=lambda h: None):
    for h in range(out_ref.shape[0] // HEAD_DIM):
        ready(h)
        at = columns(first + h)
        key_rows = keys[:, at].astype(F32)
        normal = (key_rows * inverse_rms(key_rows)).astype(BF16)
        state = lax.dot_general(
            normal, values[:, at], (((0,), (0,)), ((), ())), preferred_element_type=F32
        )
        out_ref[h * HEAD_DIM : (h + 1) * HEAD_DIM, :] = state.astype(out_ref.dtype)


def first_kernel(parts, key_ref, value_ref, out_ref, keys, values, sems):
    mine, other = core_heads()
    half = HEADS // 2
    starts = [(other + h, half // parts) for h in range(0, half, half // parts)] + [(mine, half)]
    copies = []
    for n, (first, heads) in enumerate(starts):
        at = columns(first, heads)
        pair = [
            pltpu.make_async_copy(ref.at[:, at], held.at[:, at], sems.at[n, s])
            for s, (ref, held) in enumerate(((key_ref, keys), (value_ref, values)))
        ]
        for copy in pair:
            copy.start()
        copies.append(pair)

    def ready(h):
        if h % (half // parts) == 0:
            for copy in copies[h // (half // parts)]:
                copy.wait()

    states_of(other, keys, values, out_ref, ready)
    for copy in copies[-1]:
        copy.wait()


def outgoing_state(keys, values):
    dim, half = HEAD_DIM, HEADS // 2
    rows, parts = keys.shape[0], math.gcd(half, 3)
    keys, values = (pltpu.with_memory_space_constraint(x, pltpu.HBM) for x in (keys, values))
    return pl.pallas_call(
        functools.partial(first_kernel, parts),
        out_shape=[pltpu.VMEM((half * dim, dim), BF16)] + [pltpu.VMEM(keys.shape, BF16)] * 2,
        in_specs=[IN_HBM, IN_HBM],
        out_specs=[WHOLE] * 3,
        scratch_shapes=[pltpu.SemaphoreType.DMA((parts + 1, 2))],
        compiler_params=PARAMS,
        cost_estimate=pl.CostEstimate(
            flops=2 * half * rows * dim * dim, bytes_accessed=8 * half * rows * dim, transcendentals=0
        ),
    )(keys, values)


def own_kernel(key_ref, value_ref, out_ref):
    states_of(core_heads()[0], key_ref, value_ref, out_ref)


def own_state(keys, values):
    dim, half = HEAD_DIM, HEADS // 2
    rows = keys.shape[0]
    return pl.pallas_call(
        own_kernel,
        out_shape=pltpu.VMEM((half * dim, dim), F32),
        in_specs=[WHOLE, WHOLE],
        out_specs=WHOLE,
        compiler_params=PARAMS,
        cost_estimate=pl.CostEstimate(
            flops=2 * half * rows * dim * dim, bytes_accessed=8 * half * rows * dim, transcendentals=0
        ),
    )(*in_vmem(keys, values))


def piece_kernel(mine_ref, other_ref, own_ref, *piece_refs):
    chip = lax.axis_index("chip")
    rows = own_ref.shape[0]
    for d, ref in enumerate((own_ref,) + piece_refs):
        at = pl.ds(pl.multiple_of((chip ^ d) * rows, rows), rows)
        ref[...] = (mine_ref[at, :] + other_ref[at, :].astype(F32)).astype(ref.dtype)


def chip_pieces(mine, other, chips):
    shape = (mine.shape[0] // chips, HEAD_DIM)
    return pl.pallas_call(
        piece_kernel,
        out_shape=[pltpu.VMEM(shape, F32)] + [pltpu.VMEM(shape, BF16)] * (chips - 1),
        in_specs=[WHOLE, WHOLE],
        out_specs=[WHOLE] * chips,
        compiler_params=PARAMS,
        cost_estimate=SMALL,
    )(*in_vmem(mine, other))


def sum_kernel(after_ref, own_ref, *refs):
    total = own_ref[...]
    for ref in refs[:-1]:
        total = total + ref[...].astype(F32)
    refs[-1][...] = total.astype(refs[-1].dtype)


def sum_pieces(after, own, parts, dtype):
    return pl.pallas_call(
        sum_kernel,
        out_shape=pltpu.VMEM(own.shape, dtype),
        in_specs=[ANYWHERE] + [WHOLE] * (1 + len(parts)),
        out_specs=WHOLE,
        compiler_params=PARAMS,
        cost_estimate=SMALL,
    )(after, *in_vmem(own, *parts))


def slot_kernel(after_ref, near_ref, across_ref, diagonal_ref, out_ref):
    both = across_ref[...].astype(F32) + diagonal_ref[...].astype(F32)
    near = near_ref[...].astype(F32)
    out_ref[...] = jnp.where(lax.axis_index("frame") == 2, both, near).astype(BF16)


def choose_slot(after, near, across, diagonal):
    return pl.pallas_call(
        slot_kernel,
        out_shape=pltpu.VMEM(near.shape, BF16),
        in_specs=[ANYWHERE] + [WHOLE] * 3,
        out_specs=WHOLE,
        compiler_params=PARAMS,
        cost_estimate=SMALL,
    )(after, *in_vmem(near, across, diagonal))


def pack_kernel(after, order, *refs):
    out_ref, refs = refs[-1], refs[after:-1]
    rows = refs[0].shape[0]
    for place, ref in zip(order, refs):
        out_ref[place * rows : (place + 1) * rows, :] = ref[...]


def pack(pieces, order, after):
    rows = sum(array.shape[0] for array in pieces)
    pieces = [pieces[place] for place in order]
    return pl.pallas_call(
        functools.partial(pack_kernel, len(after), order),
        out_shape=pltpu.VMEM((rows, HEAD_DIM), BF16),
        in_specs=[ANYWHERE] * len(after) + [WHOLE] * len(pieces),
        out_specs=WHOLE,
        compiler_params=PARAMS,
        cost_estimate=SMALL,
    )(*after, *in_vmem(*pieces))


def local_kernel(
    coefs, turn, length_ref, back_ref, query_ref, key_ref, value_ref, weight_ref, after_ref, local_ref, *read_refs
):
    tokens = query_ref.shape[0]
    first = core_heads()[turn]
    heads = local_ref.shape[1] // HEAD_DIM
    key_at = lax.broadcasted_iota(jnp.int32, (tokens, tokens), 0)
    query_at = lax.broadcasted_iota(jnp.int32, (tokens, tokens), 1)
    start = jnp.int32(0)
    floor = jnp.zeros((tokens, tokens), jnp.int32)
    for k in range(length_ref.shape[1]):
        lowest = jnp.maximum(start - back_ref[0, k], 0)
        floor = jnp.where(query_at >= start, lowest, floor)
        start = start + length_ref[0, k]
    hidden = jnp.where((key_at <= query_at) & (key_at >= floor), 0.0, -jnp.inf).astype(F32)
    scale = math.log2(math.e) / math.sqrt(HEAD_DIM)
    ones = jnp.full((HEAD_DIM, HEAD_DIM), 1.0 / HEAD_DIM, BF16)
    half = HEADS // 2
    by_slot = []
    for slot_coefs in coefs(lax.axis_index("frame")):
        total = None
        for level, coef in slot_coefs:
            term = weight_ref[1 + level, pl.ds(first, heads), :] * coef
            total = term if total is None else total + term
        by_slot.append(total)
    pad = -len(by_slot) * heads % HEAD_DIM
    gains = jnp.concatenate(by_slot + [jnp.zeros((pad, tokens), F32)], 0).T

    def scores_of(h):
        at = columns(first + h)
        return lax.dot_general(
            key_ref[:, at], query_ref[:, at], (((1,), (1,)), ((), ())), preferred_element_type=F32
        )

    upcoming = scores_of(0)
    for h in range(heads):
        scores = upcoming * scale + hidden
        if h + 1 < heads:
            upcoming = scores_of(h + 1)
        weights = jnp.exp2(scores - jnp.max(scores, 0, keepdims=True))
        total = jnp.sum(weights, 0, keepdims=True)
        weights = weights * (weight_ref[0, pl.ds(first + h, 1), :] / total)
        at = slice(h * HEAD_DIM, (h + 1) * HEAD_DIM)
        local_ref[:, at] = lax.dot_general(
            weights.astype(BF16),
            value_ref[:, columns(first + h)],
            (((0,), (0,)), ((), ())),
            preferred_element_type=F32,
        )
        query = query_ref[:, columns(first + h)].astype(F32)
        mean = jnp.dot((query * query).astype(BF16), ones, preferred_element_type=F32)
        query = query * lax.rsqrt(mean + EPSILON)
        for slot, read_ref in enumerate(read_refs):
            which = slot * heads + h
            read_ref[:, at] = (query * gains[:, which : which + 1]).astype(BF16)


def local_part(coefs, slots, turn, frame_len, window_back, queries, keys, values, weights, after):
    tokens, width = queries.shape
    width //= 2
    return pl.pallas_call(
        functools.partial(local_kernel, coefs, turn),
        out_shape=[pltpu.VMEM((tokens, width), F32)] + [pltpu.VMEM((tokens, width), BF16)] * slots,
        in_specs=[SCALARS] * 2 + [WHOLE] * 4 + [ANYWHERE],
        out_specs=[WHOLE] * (1 + slots),
        compiler_params=PARAMS,
        cost_estimate=pl.CostEstimate(
            flops=4 * tokens * tokens * width,
            bytes_accessed=14 * tokens * width,
            transcendentals=tokens * width,
        ),
    )(frame_len, window_back, queries, *in_vmem(keys, values), weights, after)


def read_heads(d, chips, base_ref, states):
    count = HEADS // 2 // chips
    first = (lax.axis_index("chip") ^ d) * count
    for h in range(count):
        at = columns(first + h)
        result = base_ref[:, at]
        for read_ref, state_ref, row in states:
            result = result + jnp.dot(
                read_ref[:, at],
                state_ref[row + h * HEAD_DIM : row + (h + 1) * HEAD_DIM, :],
                preferred_element_type=F32,
            )
        yield at, result


def middle_kernel(chips, early, local_ref, x_ref, y_ref, state_ref, out_ref):
    rows = state_ref.shape[0] // (chips + early)
    for d in range(chips):
        states = [(x_ref, state_ref, d * rows)]
        if d < early:
            states.append((y_ref, state_ref, (chips + d) * rows))
        for at, result in read_heads(d, chips, local_ref, states):
            out_ref[:, at] = result


def read_middle(chips, early, local, x, y, states):
    return pl.pallas_call(
        functools.partial(middle_kernel, chips, early),
        out_shape=pltpu.VMEM(local.shape, F32),
        in_specs=[WHOLE] * 4,
        out_specs=WHOLE,
        compiler_params=PARAMS,
        cost_estimate=SMALL,
    )(*in_vmem(local, x, y, states))


def late_kernel(turn, chips, early, base_ref, y_ref, *refs):
    *state_refs, out_ref, held, sems = refs
    rows = base_ref.shape[1] // chips
    half = core_heads()[turn]
    copies = []
    for d in range(chips):
        states = [(y_ref, state_refs[0], (d - early) * rows)] if d >= early else []
        for at, result in read_heads(d, chips, base_ref, states):
            held[:, at] = result.astype(BF16)
        count = HEADS // 2 // chips
        first = (lax.axis_index("chip") ^ d) * count
        copies.append(
            pltpu.make_async_copy(
                held.at[:, columns(first, count)], out_ref.at[:, columns(half + first, count)], sems.at[d]
            )
        )
        copies[-1].start()
    for copy in copies:
        copy.wait()


def aliased_kernel(turn, chips, early, out_before_ref, *refs):
    late_kernel(turn, chips, early, *refs)


def write_late(turn, chips, early, base, y, states, out=None):
    tokens, width = base.shape
    before = [] if out is None else [out]
    kernel = late_kernel if out is None else aliased_kernel
    return pl.pallas_call(
        functools.partial(kernel, turn, chips, early),
        out_shape=jax.ShapeDtypeStruct((tokens, 2 * width), BF16),
        in_specs=[ANYWHERE] * len(before) + [WHOLE] * (2 + len(states)),
        out_specs=ANYWHERE,
        input_output_aliases={0: 0} if before else {},
        scratch_shapes=[pltpu.VMEM((tokens, width), BF16), pltpu.SemaphoreType.DMA((chips,))],
        compiler_params=PARAMS,
        cost_estimate=SMALL if before else LARGE,
    )(*before, *in_vmem(base, y, *states))


def swap(array, axis, mask, size):
    return lax.ppermute(array, axis, [(n, n ^ mask) for n in range(size)])


def body(sizes, queries, keys, values, level_weight, frame_len, window_back):
    frames, outer, chips = sizes
    low, high = (
        1.0 / math.sqrt(HEAD_DIM * 2**level * queries.shape[0] * outer * chips * 2) for level in (0, 1)
    )

    def coefs(f):
        x_low = jnp.where(f % 2 == 1, low, 0.0)
        x_high = jnp.where(f == 2, high, 0.0)
        return [[(0, x_low), (1, x_high)], [(1, jnp.where(f == 3, high, 0.0))]]

    local = functools.partial(local_part, coefs, 2)
    rest = (frame_len, window_back, queries)
    early = 1

    outgoing, keys, values = outgoing_state(keys, values)
    incoming = swap(outgoing, "core", 1, 2)
    mine = own_state(keys, values)
    own, *sends = chip_pieces(mine, incoming, chips)
    got = [swap(sends[d - 1], "chip", d, chips) for d in reversed(range(1, chips))]
    local_0, x_0, y_0 = local(0, *rest, keys, values, level_weight, own)
    state = sum_pieces(local_0, own, got, F32 if outer > 1 else BF16)
    if outer > 1:
        state = lax.psum(state, "outer").astype(BF16)
    local_1, x_1, y_1 = local(1, *rest, keys, values, level_weight, state)
    slot = choose_slot(local_1, *(swap(state, "frame", mask, frames) for mask in (1, 2, 3)))

    x = [slot] + [swap(slot, "chip", d, chips) for d in range(1, chips)]
    y = [swap(slot, "frame", 1, frames)]
    y += [swap(piece, "frame", 1, frames) for piece in x[1:]]
    places = [0, *reversed(range(1, chips + early))]
    own_states = pack(x + y[:early], places, [local_1])
    other_states = swap(own_states, "core", 1, 2)
    base_0 = read_middle(chips, early, local_0, x_0, y_0, own_states)
    base_1 = read_middle(chips, early, local_1, x_1, y_1, other_states)
    late = y[early:]
    late_own = [pack(late, list(range(len(late))), [])] if late else []
    late_other = [swap(piece, "core", 1, 2) for piece in late_own]
    out = write_late(0, chips, early, base_0, y_0, late_own)
    return write_late(1, chips, early, base_1, y_1, late_other, out)


def solution(mesh):
    frames, space = mesh.shape["frame"], mesh.shape["space"]
    chips = 1
    while HEADS % (chips * 4) == 0 and space % (chips * 4) == 0 and chips < 4:
        chips *= 2
    sizes = (frames, space // (2 * chips), chips)
    names = ("frame", "outer", "chip", "core")
    fine = Mesh(mesh.devices.reshape(sizes + (2,)), names)
    rows = P(names, None)
    return jax.shard_map(
        functools.partial(body, sizes),
        mesh=fine,
        in_specs=(rows, rows, rows, P(None, None, names), rows, rows),
        out_specs=rows,
        check_vma=False,
    )
```

```python
import functools
import math

import jax
import jax.numpy as jnp
from jax import lax
from jax.experimental import pallas as pl
from jax.experimental.pallas import tpu as pltpu
from jax.sharding import Mesh, PartitionSpec as P

HEADS = 24
HEAD_DIM = 128
EPSILON = 1e-06
VMEM_LIMIT = 40 * 1024 * 1024

F32, BF16 = jnp.float32, jnp.bfloat16
WHOLE = pl.BlockSpec(memory_space=pltpu.VMEM)
SCALARS = pl.BlockSpec(memory_space=pltpu.SMEM)
ANYWHERE = pl.BlockSpec(memory_space=pl.ANY)
IN_HBM = pl.BlockSpec(memory_space=pltpu.HBM)
SMALL = pl.CostEstimate(flops=1024, bytes_accessed=1024, transcendentals=0)
LARGE = pl.CostEstimate(flops=2 * 10**10, bytes_accessed=1024, transcendentals=0)
PARAMS = pltpu.CompilerParams(vmem_limit_bytes=VMEM_LIMIT)


def inverse_rms(rows):
    return lax.rsqrt(jnp.mean(rows * rows, -1, keepdims=True) + EPSILON)


def columns(head, count=1):
    return pl.ds(pl.multiple_of(head * HEAD_DIM, HEAD_DIM), count * HEAD_DIM)


def core_heads():
    core = lax.axis_index("core")
    return core * (HEADS // 2), (1 - core) * (HEADS // 2)


def in_vmem(*arrays):
    return [pltpu.with_memory_space_constraint(array, pltpu.VMEM) for array in arrays]


def states_of(first, keys, values, out_ref, ready=lambda h: None):
    for h in range(out_ref.shape[0] // HEAD_DIM):
        ready(h)
        at = columns(first + h)
        key_rows = keys[:, at].astype(F32)
        normal = (key_rows * inverse_rms(key_rows)).astype(BF16)
        state = lax.dot_general(
            normal, values[:, at], (((0,), (0,)), ((), ())), preferred_element_type=F32
        )
        out_ref[h * HEAD_DIM : (h + 1) * HEAD_DIM, :] = state.astype(out_ref.dtype)


def first_kernel(parts, key_ref, value_ref, out_ref, keys, values, sems):
    mine, other = core_heads()
    half = HEADS // 2
    starts = [(other + h, half // parts) for h in range(0, half, half // parts)] + [(mine, half)]
    copies = []
    for n, (first, heads) in enumerate(starts):
        at = columns(first, heads)
        pair = [
            pltpu.make_async_copy(ref.at[:, at], held.at[:, at], sems.at[n, s])
            for s, (ref, held) in enumerate(((key_ref, keys), (value_ref, values)))
        ]
        for copy in pair:
            copy.start()
        copies.append(pair)

    def ready(h):
        if h % (half // parts) == 0:
            for copy in copies[h // (half // parts)]:
                copy.wait()

    states_of(other, keys, values, out_ref, ready)
    for copy in copies[-1]:
        copy.wait()


def outgoing_state(keys, values):
    dim, half = HEAD_DIM, HEADS // 2
    rows, parts = keys.shape[0], 1
    keys, values = (pltpu.with_memory_space_constraint(x, pltpu.HBM) for x in (keys, values))
    return pl.pallas_call(
        functools.partial(first_kernel, parts),
        out_shape=[pltpu.VMEM((half * dim, dim), BF16)] + [pltpu.VMEM(keys.shape, BF16)] * 2,
        in_specs=[IN_HBM, IN_HBM],
        out_specs=[WHOLE] * 3,
        scratch_shapes=[pltpu.SemaphoreType.DMA((parts + 1, 2))],
        compiler_params=PARAMS,
        cost_estimate=pl.CostEstimate(
            flops=2 * half * rows * dim * dim, bytes_accessed=8 * half * rows * dim, transcendentals=0
        ),
    )(keys, values)


def own_kernel(key_ref, value_ref, out_ref):
    states_of(core_heads()[0], key_ref, value_ref, out_ref)


def own_state(keys, values):
    dim, half = HEAD_DIM, HEADS // 2
    rows = keys.shape[0]
    return pl.pallas_call(
        own_kernel,
        out_shape=pltpu.VMEM((half * dim, dim), F32),
        in_specs=[WHOLE, WHOLE],
        out_specs=WHOLE,
        compiler_params=PARAMS,
        cost_estimate=pl.CostEstimate(
            flops=2 * half * rows * dim * dim, bytes_accessed=8 * half * rows * dim, transcendentals=0
        ),
    )(*in_vmem(keys, values))


def piece_kernel(mine_ref, other_ref, own_ref, *piece_refs):
    chip = lax.axis_index("chip")
    rows = own_ref.shape[0]
    for d, ref in enumerate((own_ref,) + piece_refs):
        at = pl.ds(pl.multiple_of((chip ^ d) * rows, rows), rows)
        ref[...] = (mine_ref[at, :] + other_ref[at, :].astype(F32)).astype(ref.dtype)


def chip_pieces(mine, other, chips):
    shape = (mine.shape[0] // chips, HEAD_DIM)
    return pl.pallas_call(
        piece_kernel,
        out_shape=[pltpu.VMEM(shape, F32)] + [pltpu.VMEM(shape, BF16)] * (chips - 1),
        in_specs=[WHOLE, WHOLE],
        out_specs=[WHOLE] * chips,
        compiler_params=PARAMS,
        cost_estimate=SMALL,
    )(*in_vmem(mine, other))


def sum_kernel(after_ref, own_ref, *refs):
    total = own_ref[...]
    for ref in refs[:-1]:
        total = total + ref[...].astype(F32)
    refs[-1][...] = total.astype(refs[-1].dtype)


def sum_pieces(after, own, parts, dtype):
    return pl.pallas_call(
        sum_kernel,
        out_shape=pltpu.VMEM(own.shape, dtype),
        in_specs=[ANYWHERE] + [WHOLE] * (1 + len(parts)),
        out_specs=WHOLE,
        compiler_params=PARAMS,
        cost_estimate=SMALL,
    )(after, *in_vmem(own, *parts))


def slot_kernel(after_ref, before_ref, first_ref, out_ref):
    before = before_ref[...].astype(F32)
    both = first_ref[...].astype(F32) + before
    out_ref[...] = jnp.where(lax.axis_index("frame") == 2, both, before).astype(BF16)


def choose_slot(after, before, first):
    return pl.pallas_call(
        slot_kernel,
        out_shape=pltpu.VMEM(before.shape, BF16),
        in_specs=[ANYWHERE] + [WHOLE] * 2,
        out_specs=WHOLE,
        compiler_params=PARAMS,
        cost_estimate=SMALL,
    )(after, *in_vmem(before, first))


def pack_kernel(after, order, *refs):
    out_ref, refs = refs[-1], refs[after:-1]
    rows = refs[0].shape[0]
    for place, ref in zip(order, refs):
        out_ref[place * rows : (place + 1) * rows, :] = ref[...]


def pack(pieces, order, after):
    rows = sum(array.shape[0] for array in pieces)
    pieces = [pieces[place] for place in order]
    return pl.pallas_call(
        functools.partial(pack_kernel, len(after), order),
        out_shape=pltpu.VMEM((rows, HEAD_DIM), BF16),
        in_specs=[ANYWHERE] * len(after) + [WHOLE] * len(pieces),
        out_specs=WHOLE,
        compiler_params=PARAMS,
        cost_estimate=SMALL,
    )(*after, *in_vmem(*pieces))


def local_kernel(
    coefs, turn, length_ref, back_ref, query_ref, key_ref, value_ref, weight_ref, after_ref, local_ref, *read_refs
):
    tokens = query_ref.shape[0]
    first = core_heads()[turn]
    heads = local_ref.shape[1] // HEAD_DIM
    key_at = lax.broadcasted_iota(jnp.int32, (tokens, tokens), 0)
    query_at = lax.broadcasted_iota(jnp.int32, (tokens, tokens), 1)
    start = jnp.int32(0)
    floor = jnp.zeros((tokens, tokens), jnp.int32)
    for k in range(length_ref.shape[1]):
        lowest = jnp.maximum(start - back_ref[0, k], 0)
        floor = jnp.where(query_at >= start, lowest, floor)
        start = start + length_ref[0, k]
    hidden = jnp.where((key_at <= query_at) & (key_at >= floor), 0.0, -jnp.inf).astype(F32)
    scale = math.log2(math.e) / math.sqrt(HEAD_DIM)
    ones = jnp.full((HEAD_DIM, HEAD_DIM), 1.0 / HEAD_DIM, BF16)
    half = HEADS // 2
    by_slot = []
    for slot_coefs in coefs(lax.axis_index("frame")):
        total = None
        for level, coef in slot_coefs:
            term = weight_ref[1 + level, pl.ds(first, heads), :] * coef
            total = term if total is None else total + term
        by_slot.append(total)
    pad = -len(by_slot) * heads % HEAD_DIM
    gains = jnp.concatenate(by_slot + [jnp.zeros((pad, tokens), F32)], 0).T

    def scores_of(h):
        at = columns(first + h)
        return lax.dot_general(
            key_ref[:, at], query_ref[:, at], (((1,), (1,)), ((), ())), preferred_element_type=F32
        )

    upcoming = scores_of(0)
    for h in range(heads):
        scores = upcoming * scale + hidden
        if h + 1 < heads:
            upcoming = scores_of(h + 1)
        weights = jnp.exp2(scores - jnp.max(scores, 0, keepdims=True))
        total = jnp.sum(weights, 0, keepdims=True)
        weights = weights * (weight_ref[0, pl.ds(first + h, 1), :] / total)
        at = slice(h * HEAD_DIM, (h + 1) * HEAD_DIM)
        local_ref[:, at] = lax.dot_general(
            weights.astype(BF16),
            value_ref[:, columns(first + h)],
            (((0,), (0,)), ((), ())),
            preferred_element_type=F32,
        )
        query = query_ref[:, columns(first + h)].astype(F32)
        mean = jnp.dot((query * query).astype(BF16), ones, preferred_element_type=F32)
        query = query * lax.rsqrt(mean + EPSILON)
        for slot, read_ref in enumerate(read_refs):
            which = slot * heads + h
            read_ref[:, at] = (query * gains[:, which : which + 1]).astype(BF16)


def local_part(coefs, slots, turn, frame_len, window_back, queries, keys, values, weights, after):
    tokens, width = queries.shape
    width //= 2
    return pl.pallas_call(
        functools.partial(local_kernel, coefs, turn),
        out_shape=[pltpu.VMEM((tokens, width), F32)] + [pltpu.VMEM((tokens, width), BF16)] * slots,
        in_specs=[SCALARS] * 2 + [WHOLE] * 4 + [ANYWHERE],
        out_specs=[WHOLE] * (1 + slots),
        compiler_params=PARAMS,
        cost_estimate=pl.CostEstimate(
            flops=4 * tokens * tokens * width,
            bytes_accessed=14 * tokens * width,
            transcendentals=tokens * width,
        ),
    )(frame_len, window_back, queries, *in_vmem(keys, values), weights, after)


def read_heads(d, chips, base_ref, states):
    count = HEADS // 2 // chips
    first = (lax.axis_index("chip") ^ d) * count
    for h in range(count):
        at = columns(first + h)
        result = base_ref[:, at]
        for read_ref, state_ref, row in states:
            result = result + jnp.dot(
                read_ref[:, at],
                state_ref[row + h * HEAD_DIM : row + (h + 1) * HEAD_DIM, :],
                preferred_element_type=F32,
            )
        yield at, result


def middle_kernel(chips, early, local_ref, x_ref, y_ref, state_ref, out_ref):
    rows = state_ref.shape[0] // (chips + early)
    for d in range(chips):
        states = [(x_ref, state_ref, d * rows)]
        if d < early:
            states.append((y_ref, state_ref, (chips + d) * rows))
        for at, result in read_heads(d, chips, local_ref, states):
            out_ref[:, at] = result


def read_middle(chips, early, local, x, y, states):
    return pl.pallas_call(
        functools.partial(middle_kernel, chips, early),
        out_shape=pltpu.VMEM(local.shape, F32),
        in_specs=[WHOLE] * 4,
        out_specs=WHOLE,
        compiler_params=PARAMS,
        cost_estimate=SMALL,
    )(*in_vmem(local, x, y, states))


def late_kernel(turn, chips, early, base_ref, y_ref, *refs):
    *state_refs, out_ref, held, sems = refs
    rows = base_ref.shape[1] // chips
    half = core_heads()[turn]
    copies = []
    for d in range(chips):
        states = [(y_ref, state_refs[0], (d - early) * rows)] if d >= early else []
        for at, result in read_heads(d, chips, base_ref, states):
            held[:, at] = result.astype(BF16)
        count = HEADS // 2 // chips
        first = (lax.axis_index("chip") ^ d) * count
        copies.append(
            pltpu.make_async_copy(
                held.at[:, columns(first, count)], out_ref.at[:, columns(half + first, count)], sems.at[d]
            )
        )
        copies[-1].start()
    for copy in copies:
        copy.wait()


def aliased_kernel(turn, chips, early, out_before_ref, *refs):
    late_kernel(turn, chips, early, *refs)


def write_late(turn, chips, early, base, y, states, out=None):
    tokens, width = base.shape
    before = [] if out is None else [out]
    kernel = late_kernel if out is None else aliased_kernel
    return pl.pallas_call(
        functools.partial(kernel, turn, chips, early),
        out_shape=jax.ShapeDtypeStruct((tokens, 2 * width), BF16),
        in_specs=[ANYWHERE] * len(before) + [WHOLE] * (2 + len(states)),
        out_specs=ANYWHERE,
        input_output_aliases={0: 0} if before else {},
        scratch_shapes=[pltpu.VMEM((tokens, width), BF16), pltpu.SemaphoreType.DMA((chips,))],
        compiler_params=PARAMS,
        cost_estimate=SMALL if before else LARGE,
    )(*before, *in_vmem(base, y, *states))


def swap(array, axis, mask, size):
    return lax.ppermute(array, axis, [(n, n ^ mask) for n in range(size)])


def body(sizes, queries, keys, values, level_weight, frame_len, window_back):
    frames, outer, chips = sizes
    low, high = (
        1.0 / math.sqrt(HEAD_DIM * 2**level * queries.shape[0] * outer * chips * 2) for level in (0, 1)
    )

    def coefs(f):
        x_low = jnp.where(f % 2 == 1, low, 0.0)
        x_high = jnp.where(f == 2, high, 0.0)
        return [[(0, x_low), (1, x_high)], [(1, jnp.where(f == 3, high, 0.0))]]

    local = functools.partial(local_part, coefs, 2)
    rest = (frame_len, window_back, queries)
    early = 1

    outgoing, keys, values = outgoing_state(keys, values)
    incoming = swap(outgoing, "core", 1, 2)
    mine = own_state(keys, values)
    own, *sends = chip_pieces(mine, incoming, chips)
    got = [swap(sends[d - 1], "chip", d, chips) for d in reversed(range(1, chips))]
    local_0, x_0, y_0 = local(0, *rest, keys, values, level_weight, own)
    state = sum_pieces(local_0, own, got, F32 if outer > 1 else BF16)
    if outer > 1:
        state = lax.psum(state, "outer").astype(BF16)
    local_1, x_1, y_1 = local(1, *rest, keys, values, level_weight, state)
    shifted = lax.ppermute(state, "frame", [(f, (f + 1) % frames) for f in range(frames)])
    slot = choose_slot(local_1, shifted, swap(state, "frame", 2, frames))

    x = [slot] + [swap(slot, "chip", d, chips) for d in range(1, chips)]
    y = [swap(slot, "frame", 1, frames)]
    y += [swap(piece, "frame", 1, frames) for piece in x[1:]]
    places = [0, *range(chips + early - 1, 2, -1), *range(1, min(3, chips + early))]
    own_states = pack(x + y[:early], places, [local_1])
    other_states = swap(own_states, "core", 1, 2)
    base_0 = read_middle(chips, early, local_0, x_0, y_0, own_states)
    base_1 = read_middle(chips, early, local_1, x_1, y_1, other_states)
    late = y[early:]
    late_own = [pack(late, list(range(len(late))), [])] if late else []
    late_other = [swap(piece, "core", 1, 2) for piece in late_own]
    out = write_late(0, chips, early, base_0, y_0, late_own)
    return write_late(1, chips, early, base_1, y_1, late_other, out)


def solution(mesh):
    frames, space = mesh.shape["frame"], mesh.shape["space"]
    chips = 1
    while HEADS % (chips * 4) == 0 and space % (chips * 4) == 0 and chips < 4:
        chips *= 2
    sizes = (frames, space // (2 * chips), chips)
    names = ("frame", "outer", "chip", "core")
    fine = Mesh(mesh.devices.reshape(sizes + (2,)), names)
    rows = P(names, None)
    return jax.shard_map(
        functools.partial(body, sizes),
        mesh=fine,
        in_specs=(rows, rows, rows, P(None, None, names), rows, rows),
        out_specs=rows,
        check_vma=False,
    )
```

```python
import functools
import math

import jax
import jax.numpy as jnp
from jax import lax
from jax.experimental import pallas as pl
from jax.experimental.pallas import tpu as pltpu
from jax.sharding import Mesh, PartitionSpec as P

HEADS = 24
HEAD_DIM = 128
EPSILON = 1e-06
VMEM_LIMIT = 40 * 1024 * 1024

F32, BF16 = jnp.float32, jnp.bfloat16
WHOLE = pl.BlockSpec(memory_space=pltpu.VMEM)
SCALARS = pl.BlockSpec(memory_space=pltpu.SMEM)
ANYWHERE = pl.BlockSpec(memory_space=pl.ANY)
IN_HBM = pl.BlockSpec(memory_space=pltpu.HBM)
SMALL = pl.CostEstimate(flops=1024, bytes_accessed=1024, transcendentals=0)
LARGE = pl.CostEstimate(flops=2 * 10**10, bytes_accessed=1024, transcendentals=0)
PARAMS = pltpu.CompilerParams(vmem_limit_bytes=VMEM_LIMIT)


def inverse_rms(rows):
    return lax.rsqrt(jnp.mean(rows * rows, -1, keepdims=True) + EPSILON)


def columns(head, count=1):
    return pl.ds(pl.multiple_of(head * HEAD_DIM, HEAD_DIM), count * HEAD_DIM)


def core_heads():
    core = lax.axis_index("core")
    return core * (HEADS // 2), (1 - core) * (HEADS // 2)


def in_vmem(*arrays):
    return [pltpu.with_memory_space_constraint(array, pltpu.VMEM) for array in arrays]


def states_of(first, keys, values, out_ref, ready=lambda h: None):
    for h in range(out_ref.shape[0] // HEAD_DIM):
        ready(h)
        at = columns(first + h)
        key_rows = keys[:, at].astype(F32)
        normal = (key_rows * inverse_rms(key_rows)).astype(BF16)
        state = lax.dot_general(
            normal, values[:, at], (((0,), (0,)), ((), ())), preferred_element_type=F32
        )
        out_ref[h * HEAD_DIM : (h + 1) * HEAD_DIM, :] = state.astype(out_ref.dtype)


def first_kernel(parts, key_ref, value_ref, out_ref, keys, values, sems):
    mine, other = core_heads()
    half = HEADS // 2
    starts = [(other + h, half // parts) for h in range(0, half, half // parts)] + [(mine, half)]
    copies = []
    for n, (first, heads) in enumerate(starts):
        at = columns(first, heads)
        pair = [
            pltpu.make_async_copy(ref.at[:, at], held.at[:, at], sems.at[n, s])
            for s, (ref, held) in enumerate(((key_ref, keys), (value_ref, values)))
        ]
        for copy in pair:
            copy.start()
        copies.append(pair)

    def ready(h):
        if h % (half // parts) == 0:
            for copy in copies[h // (half // parts)]:
                copy.wait()

    states_of(other, keys, values, out_ref, ready)
    for copy in copies[-1]:
        copy.wait()


def outgoing_state(keys, values):
    dim, half = HEAD_DIM, HEADS // 2
    rows, parts = keys.shape[0], 1
    keys, values = (pltpu.with_memory_space_constraint(x, pltpu.HBM) for x in (keys, values))
    return pl.pallas_call(
        functools.partial(first_kernel, parts),
        out_shape=[pltpu.VMEM((half * dim, dim), BF16)] + [pltpu.VMEM(keys.shape, BF16)] * 2,
        in_specs=[IN_HBM, IN_HBM],
        out_specs=[WHOLE] * 3,
        scratch_shapes=[pltpu.SemaphoreType.DMA((parts + 1, 2))],
        compiler_params=PARAMS,
        cost_estimate=pl.CostEstimate(
            flops=2 * half * rows * dim * dim, bytes_accessed=8 * half * rows * dim, transcendentals=0
        ),
    )(keys, values)


def own_kernel(key_ref, value_ref, out_ref):
    states_of(core_heads()[0], key_ref, value_ref, out_ref)


def own_state(keys, values):
    dim, half = HEAD_DIM, HEADS // 2
    rows = keys.shape[0]
    return pl.pallas_call(
        own_kernel,
        out_shape=pltpu.VMEM((half * dim, dim), F32),
        in_specs=[WHOLE, WHOLE],
        out_specs=WHOLE,
        compiler_params=PARAMS,
        cost_estimate=pl.CostEstimate(
            flops=2 * half * rows * dim * dim, bytes_accessed=8 * half * rows * dim, transcendentals=0
        ),
    )(*in_vmem(keys, values))


def piece_kernel(mine_ref, other_ref, own_ref, *piece_refs):
    chip = lax.axis_index("chip")
    rows = own_ref.shape[0]
    for d, ref in enumerate((own_ref,) + piece_refs):
        at = pl.ds(pl.multiple_of((chip ^ d) * rows, rows), rows)
        ref[...] = (mine_ref[at, :] + other_ref[at, :].astype(F32)).astype(ref.dtype)


def chip_pieces(mine, other, chips):
    shape = (mine.shape[0] // chips, HEAD_DIM)
    return pl.pallas_call(
        piece_kernel,
        out_shape=[pltpu.VMEM(shape, F32)] + [pltpu.VMEM(shape, BF16)] * (chips - 1),
        in_specs=[WHOLE, WHOLE],
        out_specs=[WHOLE] * chips,
        compiler_params=PARAMS,
        cost_estimate=SMALL,
    )(*in_vmem(mine, other))


def sum_kernel(after_ref, own_ref, *refs):
    total = own_ref[...]
    for ref in refs[:-1]:
        total = total + ref[...].astype(F32)
    refs[-1][...] = total.astype(refs[-1].dtype)


def sum_pieces(after, own, parts, dtype):
    return pl.pallas_call(
        sum_kernel,
        out_shape=pltpu.VMEM(own.shape, dtype),
        in_specs=[ANYWHERE] + [WHOLE] * (1 + len(parts)),
        out_specs=WHOLE,
        compiler_params=PARAMS,
        cost_estimate=SMALL,
    )(after, *in_vmem(own, *parts))


def slot_kernel(after_ref, before_ref, first_ref, out_ref):
    before = before_ref[...].astype(F32)
    both = first_ref[...].astype(F32) + before
    out_ref[...] = jnp.where(lax.axis_index("frame") == 2, both, before).astype(BF16)


def choose_slot(after, before, first):
    return pl.pallas_call(
        slot_kernel,
        out_shape=pltpu.VMEM(before.shape, BF16),
        in_specs=[ANYWHERE] + [WHOLE] * 2,
        out_specs=WHOLE,
        compiler_params=PARAMS,
        cost_estimate=SMALL,
    )(after, *in_vmem(before, first))


def pack_kernel(after, order, *refs):
    out_ref, refs = refs[-1], refs[after:-1]
    rows = refs[0].shape[0]
    for place, ref in zip(order, refs):
        out_ref[place * rows : (place + 1) * rows, :] = ref[...]


def pack(pieces, order, after):
    rows = sum(array.shape[0] for array in pieces)
    pieces = [pieces[place] for place in order]
    return pl.pallas_call(
        functools.partial(pack_kernel, len(after), order),
        out_shape=pltpu.VMEM((rows, HEAD_DIM), BF16),
        in_specs=[ANYWHERE] * len(after) + [WHOLE] * len(pieces),
        out_specs=WHOLE,
        compiler_params=PARAMS,
        cost_estimate=SMALL,
    )(*after, *in_vmem(*pieces))


def local_kernel(
    coefs, turn, length_ref, back_ref, query_ref, key_ref, value_ref, weight_ref, after_ref, local_ref, *read_refs
):
    tokens = query_ref.shape[0]
    first = core_heads()[turn]
    heads = local_ref.shape[1] // HEAD_DIM
    key_at = lax.broadcasted_iota(jnp.int32, (tokens, tokens), 0)
    query_at = lax.broadcasted_iota(jnp.int32, (tokens, tokens), 1)
    start = jnp.int32(0)
    floor = jnp.zeros((tokens, tokens), jnp.int32)
    for k in range(length_ref.shape[1]):
        lowest = jnp.maximum(start - back_ref[0, k], 0)
        floor = jnp.where(query_at >= start, lowest, floor)
        start = start + length_ref[0, k]
    hidden = jnp.where((key_at <= query_at) & (key_at >= floor), 0.0, -jnp.inf).astype(F32)
    scale = math.log2(math.e) / math.sqrt(HEAD_DIM)
    ones = jnp.full((HEAD_DIM, HEAD_DIM), 1.0 / HEAD_DIM, BF16)
    half = HEADS // 2
    by_slot = []
    for slot_coefs in coefs(lax.axis_index("frame")):
        total = None
        for level, coef in slot_coefs:
            term = weight_ref[1 + level, pl.ds(first, heads), :] * coef
            total = term if total is None else total + term
        by_slot.append(total)
    pad = -len(by_slot) * heads % HEAD_DIM
    gains = jnp.concatenate(by_slot + [jnp.zeros((pad, tokens), F32)], 0).T

    def scores_of(h):
        at = columns(first + h)
        return lax.dot_general(
            key_ref[:, at], query_ref[:, at], (((1,), (1,)), ((), ())), preferred_element_type=F32
        )

    upcoming = scores_of(0)
    for h in range(heads):
        scores = upcoming * scale + hidden
        if h + 1 < heads:
            upcoming = scores_of(h + 1)
        weights = jnp.exp2(scores - jnp.max(scores, 0, keepdims=True))
        total = jnp.sum(weights, 0, keepdims=True)
        weights = weights * (weight_ref[0, pl.ds(first + h, 1), :] / total)
        at = slice(h * HEAD_DIM, (h + 1) * HEAD_DIM)
        local_ref[:, at] = lax.dot_general(
            weights.astype(BF16),
            value_ref[:, columns(first + h)],
            (((0,), (0,)), ((), ())),
            preferred_element_type=F32,
        )
        query = query_ref[:, columns(first + h)].astype(F32)
        mean = jnp.dot((query * query).astype(BF16), ones, preferred_element_type=F32)
        query = query * lax.rsqrt(mean + EPSILON)
        for slot, read_ref in enumerate(read_refs):
            which = slot * heads + h
            read_ref[:, at] = (query * gains[:, which : which + 1]).astype(BF16)


def local_part(coefs, slots, turn, frame_len, window_back, queries, keys, values, weights, after):
    tokens, width = queries.shape
    width //= 2
    return pl.pallas_call(
        functools.partial(local_kernel, coefs, turn),
        out_shape=[pltpu.VMEM((tokens, width), F32)] + [pltpu.VMEM((tokens, width), BF16)] * slots,
        in_specs=[SCALARS] * 2 + [WHOLE] * 4 + [ANYWHERE],
        out_specs=[WHOLE] * (1 + slots),
        compiler_params=PARAMS,
        cost_estimate=pl.CostEstimate(
            flops=4 * tokens * tokens * width,
            bytes_accessed=14 * tokens * width,
            transcendentals=tokens * width,
        ),
    )(frame_len, window_back, queries, *in_vmem(keys, values), weights, after)


def read_heads(d, chips, base_ref, states):
    count = HEADS // 2 // chips
    first = (lax.axis_index("chip") ^ d) * count
    for h in range(count):
        at = columns(first + h)
        result = base_ref[:, at]
        for read_ref, state_ref, row in states:
            result = result + jnp.dot(
                read_ref[:, at],
                state_ref[row + h * HEAD_DIM : row + (h + 1) * HEAD_DIM, :],
                preferred_element_type=F32,
            )
        yield at, result


def middle_kernel(chips, early, local_ref, x_ref, y_ref, state_ref, out_ref):
    rows = state_ref.shape[0] // (chips + early)
    for d in range(chips):
        states = [(x_ref, state_ref, d * rows)]
        if d < early:
            states.append((y_ref, state_ref, (chips + d) * rows))
        for at, result in read_heads(d, chips, local_ref, states):
            out_ref[:, at] = result


def read_middle(chips, early, local, x, y, states):
    return pl.pallas_call(
        functools.partial(middle_kernel, chips, early),
        out_shape=pltpu.VMEM(local.shape, F32),
        in_specs=[WHOLE] * 4,
        out_specs=WHOLE,
        compiler_params=PARAMS,
        cost_estimate=SMALL,
    )(*in_vmem(local, x, y, states))


def late_kernel(turn, chips, early, base_ref, y_ref, *refs):
    *state_refs, out_ref, held, sems = refs
    rows = base_ref.shape[1] // chips
    half = core_heads()[turn]
    copies = []
    for d in range(chips):
        states = [(y_ref, state_refs[0], (d - early) * rows)] if d >= early else []
        for at, result in read_heads(d, chips, base_ref, states):
            held[:, at] = result.astype(BF16)
        count = HEADS // 2 // chips
        first = (lax.axis_index("chip") ^ d) * count
        copies.append(
            pltpu.make_async_copy(
                held.at[:, columns(first, count)], out_ref.at[:, columns(half + first, count)], sems.at[d]
            )
        )
        copies[-1].start()
    for copy in copies:
        copy.wait()


def aliased_kernel(turn, chips, early, out_before_ref, *refs):
    late_kernel(turn, chips, early, *refs)


def write_late(turn, chips, early, base, y, states, out=None):
    tokens, width = base.shape
    before = [] if out is None else [out]
    kernel = late_kernel if out is None else aliased_kernel
    return pl.pallas_call(
        functools.partial(kernel, turn, chips, early),
        out_shape=jax.ShapeDtypeStruct((tokens, 2 * width), BF16),
        in_specs=[ANYWHERE] * len(before) + [WHOLE] * (2 + len(states)),
        out_specs=ANYWHERE,
        input_output_aliases={0: 0} if before else {},
        scratch_shapes=[pltpu.VMEM((tokens, width), BF16), pltpu.SemaphoreType.DMA((chips,))],
        compiler_params=PARAMS,
        cost_estimate=SMALL if before else LARGE,
    )(*before, *in_vmem(base, y, *states))


def swap(array, axis, mask, size):
    return lax.ppermute(array, axis, [(n, n ^ mask) for n in range(size)])


def body(sizes, queries, keys, values, level_weight, frame_len, window_back):
    frames, outer, chips = sizes
    low, high = (
        1.0 / math.sqrt(HEAD_DIM * 2**level * queries.shape[0] * outer * chips * 2) for level in (0, 1)
    )

    def coefs(f):
        x_low = jnp.where(f % 2 == 1, low, 0.0)
        x_high = jnp.where(f == 2, high, 0.0)
        return [[(0, x_low), (1, x_high)], [(1, jnp.where(f == 3, high, 0.0))]]

    local = functools.partial(local_part, coefs, 2)
    rest = (frame_len, window_back, queries)
    early = 1

    order = [*range(min(2, chips - 1), 0, -1), *range(3, chips)]

    outgoing, keys, values = outgoing_state(keys, values)
    incoming = swap(outgoing, "core", 1, 2)
    mine = own_state(keys, values)
    own, *sends = chip_pieces(mine, incoming, chips)
    got = [swap(sends[d - 1], "chip", d, chips) for d in order]
    local_0, x_0, y_0 = local(0, *rest, keys, values, level_weight, own)
    state = sum_pieces(local_0, own, got, F32 if outer > 1 else BF16)
    if outer > 1:
        state = lax.psum(state, "outer").astype(BF16)
    local_1, x_1, y_1 = local(1, *rest, keys, values, level_weight, state)
    shifted = lax.ppermute(state, "frame", [(f, (f + 1) % frames) for f in range(frames)])
    slot = choose_slot(local_1, shifted, swap(state, "frame", 2, frames))

    x = [slot] + [swap(slot, "chip", d, chips) for d in range(1, chips)]
    y = [swap(slot, "frame", 1, frames)]
    x_sent = list(x)
    if chips > 2:
        x_sent[2], _ = lax.optimization_barrier((x[2], x[1]))
        x_sent[1], y[0] = lax.optimization_barrier((x[1], y[0]))
    y += [swap(piece, "frame", 1, frames) for piece in x_sent[1:]]
    places = [0, *range(3, chips), *range(1, min(3, chips)), *range(chips, chips + early)]
    own_states = pack(x + y[:early], places, [local_1])
    other_states = swap(own_states, "core", 1, 2)
    base_0 = read_middle(chips, early, local_0, x_0, y_0, own_states)
    base_1 = read_middle(chips, early, local_1, x_1, y_1, other_states)
    late = y[early:]
    late_own = [pack(late, list(range(len(late))), [])] if late else []
    late_other = [swap(piece, "core", 1, 2) for piece in late_own]
    out = write_late(0, chips, early, base_0, y_0, late_own)
    return write_late(1, chips, early, base_1, y_1, late_other, out)


def solution(mesh):
    frames, space = mesh.shape["frame"], mesh.shape["space"]
    chips = 1
    while HEADS % (chips * 4) == 0 and space % (chips * 4) == 0 and chips < 4:
        chips *= 2
    sizes = (frames, space // (2 * chips), chips)
    names = ("frame", "outer", "chip", "core")
    fine = Mesh(mesh.devices.reshape(sizes + (2,)), names)
    rows = P(names, None)
    return jax.shard_map(
        functools.partial(body, sizes),
        mesh=fine,
        in_specs=(rows, rows, rows, P(None, None, names), rows, rows),
        out_specs=rows,
        check_vma=False,
    )
```

```python
import functools
import math

import jax
import jax.numpy as jnp
from jax import lax
from jax.experimental import pallas as pl
from jax.experimental.pallas import tpu as pltpu
from jax.sharding import Mesh, PartitionSpec as P

HEADS = 24
HEAD_DIM = 128
EPSILON = 1e-06
VMEM_LIMIT = 40 * 1024 * 1024

F32, BF16 = jnp.float32, jnp.bfloat16
WHOLE = pl.BlockSpec(memory_space=pltpu.VMEM)
SCALARS = pl.BlockSpec(memory_space=pltpu.SMEM)
ANYWHERE = pl.BlockSpec(memory_space=pl.ANY)
IN_HBM = pl.BlockSpec(memory_space=pltpu.HBM)
SMALL = pl.CostEstimate(flops=1024, bytes_accessed=1024, transcendentals=0)
LARGE = pl.CostEstimate(flops=2 * 10**10, bytes_accessed=1024, transcendentals=0)
PARAMS = pltpu.CompilerParams(vmem_limit_bytes=VMEM_LIMIT)


def inverse_rms(rows):
    return lax.rsqrt(jnp.mean(rows * rows, -1, keepdims=True) + EPSILON)


def columns(head, count=1):
    return pl.ds(pl.multiple_of(head * HEAD_DIM, HEAD_DIM), count * HEAD_DIM)


def core_heads():
    core = lax.axis_index("core")
    return core * (HEADS // 2), (1 - core) * (HEADS // 2)


def in_vmem(*arrays):
    return [pltpu.with_memory_space_constraint(array, pltpu.VMEM) for array in arrays]


def states_of(first, keys, values, out_ref, ready=lambda h: None):
    for h in range(out_ref.shape[0] // HEAD_DIM):
        ready(h)
        at = columns(first + h)
        key_rows = keys[:, at].astype(F32)
        normal = (key_rows * inverse_rms(key_rows)).astype(BF16)
        state = lax.dot_general(
            normal, values[:, at], (((0,), (0,)), ((), ())), preferred_element_type=F32
        )
        out_ref[h * HEAD_DIM : (h + 1) * HEAD_DIM, :] = state.astype(out_ref.dtype)


def first_kernel(parts, key_ref, value_ref, out_ref, keys, values, sems):
    mine, other = core_heads()
    half = HEADS // 2
    starts = [(other + h, half // parts) for h in range(0, half, half // parts)] + [(mine, half)]
    copies = []
    for n, (first, heads) in enumerate(starts):
        at = columns(first, heads)
        pair = [
            pltpu.make_async_copy(ref.at[:, at], held.at[:, at], sems.at[n, s])
            for s, (ref, held) in enumerate(((key_ref, keys), (value_ref, values)))
        ]
        for copy in pair:
            copy.start()
        copies.append(pair)

    def ready(h):
        if h % (half // parts) == 0:
            for copy in copies[h // (half // parts)]:
                copy.wait()

    states_of(other, keys, values, out_ref, ready)
    for copy in copies[-1]:
        copy.wait()


def outgoing_state(keys, values):
    dim, half = HEAD_DIM, HEADS // 2
    rows, parts = keys.shape[0], 1
    keys, values = (pltpu.with_memory_space_constraint(x, pltpu.HBM) for x in (keys, values))
    return pl.pallas_call(
        functools.partial(first_kernel, parts),
        out_shape=[pltpu.VMEM((half * dim, dim), BF16)] + [pltpu.VMEM(keys.shape, BF16)] * 2,
        in_specs=[IN_HBM, IN_HBM],
        out_specs=[WHOLE] * 3,
        scratch_shapes=[pltpu.SemaphoreType.DMA((parts + 1, 2))],
        compiler_params=PARAMS,
        cost_estimate=pl.CostEstimate(
            flops=2 * half * rows * dim * dim, bytes_accessed=8 * half * rows * dim, transcendentals=0
        ),
    )(keys, values)


def own_kernel(key_ref, value_ref, out_ref):
    states_of(core_heads()[0], key_ref, value_ref, out_ref)


def own_state(keys, values):
    dim, half = HEAD_DIM, HEADS // 2
    rows = keys.shape[0]
    return pl.pallas_call(
        own_kernel,
        out_shape=pltpu.VMEM((half * dim, dim), F32),
        in_specs=[WHOLE, WHOLE],
        out_specs=WHOLE,
        compiler_params=PARAMS,
        cost_estimate=pl.CostEstimate(
            flops=2 * half * rows * dim * dim, bytes_accessed=8 * half * rows * dim, transcendentals=0
        ),
    )(*in_vmem(keys, values))


def piece_kernel(mine_ref, other_ref, own_ref, *piece_refs):
    chip = lax.axis_index("chip")
    rows = own_ref.shape[0]
    for d, ref in enumerate((own_ref,) + piece_refs):
        at = pl.ds(pl.multiple_of((chip ^ d) * rows, rows), rows)
        ref[...] = (mine_ref[at, :] + other_ref[at, :].astype(F32)).astype(ref.dtype)


def chip_pieces(mine, other, chips):
    shape = (mine.shape[0] // chips, HEAD_DIM)
    return pl.pallas_call(
        piece_kernel,
        out_shape=[pltpu.VMEM(shape, F32)] + [pltpu.VMEM(shape, BF16)] * (chips - 1),
        in_specs=[WHOLE, WHOLE],
        out_specs=[WHOLE] * chips,
        compiler_params=PARAMS,
        cost_estimate=SMALL,
    )(*in_vmem(mine, other))


def sum_kernel(after_ref, own_ref, *refs):
    total = own_ref[...]
    for ref in refs[:-1]:
        total = total + ref[...].astype(F32)
    refs[-1][...] = total.astype(refs[-1].dtype)


def sum_pieces(after, own, parts, dtype):
    return pl.pallas_call(
        sum_kernel,
        out_shape=pltpu.VMEM(own.shape, dtype),
        in_specs=[ANYWHERE] + [WHOLE] * (1 + len(parts)),
        out_specs=WHOLE,
        compiler_params=PARAMS,
        cost_estimate=SMALL,
    )(after, *in_vmem(own, *parts))


def slot_kernel(after_ref, before_ref, first_ref, out_ref):
    before = before_ref[...].astype(F32)
    both = first_ref[...].astype(F32) + before
    out_ref[...] = jnp.where(lax.axis_index("frame") == 2, both, before).astype(BF16)


def choose_slot(after, before, first):
    return pl.pallas_call(
        slot_kernel,
        out_shape=pltpu.VMEM(before.shape, BF16),
        in_specs=[ANYWHERE] + [WHOLE] * 2,
        out_specs=WHOLE,
        compiler_params=PARAMS,
        cost_estimate=SMALL,
    )(after, *in_vmem(before, first))


def pack_kernel(after, order, *refs):
    out_ref, refs = refs[-1], refs[after:-1]
    rows = refs[0].shape[0]
    for place, ref in zip(order, refs):
        out_ref[place * rows : (place + 1) * rows, :] = ref[...]


def pack(pieces, order, after):
    rows = sum(array.shape[0] for array in pieces)
    pieces = [pieces[place] for place in order]
    return pl.pallas_call(
        functools.partial(pack_kernel, len(after), order),
        out_shape=pltpu.VMEM((rows, HEAD_DIM), BF16),
        in_specs=[ANYWHERE] * len(after) + [WHOLE] * len(pieces),
        out_specs=WHOLE,
        compiler_params=PARAMS,
        cost_estimate=SMALL,
    )(*after, *in_vmem(*pieces))


def local_kernel(
    coefs, turn, length_ref, back_ref, query_ref, key_ref, value_ref, weight_ref, after_ref, local_ref, *read_refs
):
    tokens = query_ref.shape[0]
    first = core_heads()[turn]
    heads = local_ref.shape[1] // HEAD_DIM
    key_at = lax.broadcasted_iota(jnp.int32, (tokens, tokens), 0)
    query_at = lax.broadcasted_iota(jnp.int32, (tokens, tokens), 1)
    start = jnp.int32(0)
    floor = jnp.zeros((tokens, tokens), jnp.int32)
    for k in range(length_ref.shape[1]):
        lowest = jnp.maximum(start - back_ref[0, k], 0)
        floor = jnp.where(query_at >= start, lowest, floor)
        start = start + length_ref[0, k]
    hidden = jnp.where((key_at <= query_at) & (key_at >= floor), 0.0, -jnp.inf).astype(F32)
    scale = math.log2(math.e) / math.sqrt(HEAD_DIM)
    ones = jnp.full((HEAD_DIM, HEAD_DIM), 1.0 / HEAD_DIM, BF16)
    half = HEADS // 2
    by_slot = []
    for slot_coefs in coefs(lax.axis_index("frame")):
        total = None
        for level, coef in slot_coefs:
            term = weight_ref[1 + level, pl.ds(first, heads), :] * coef
            total = term if total is None else total + term
        by_slot.append(total)
    pad = -len(by_slot) * heads % HEAD_DIM
    gains = jnp.concatenate(by_slot + [jnp.zeros((pad, tokens), F32)], 0).T

    def scores_of(h):
        at = columns(first + h)
        return lax.dot_general(
            key_ref[:, at], query_ref[:, at], (((1,), (1,)), ((), ())), preferred_element_type=F32
        )

    upcoming = scores_of(0)
    for h in range(heads):
        scores = upcoming * scale + hidden
        if h + 1 < heads:
            upcoming = scores_of(h + 1)
        weights = jnp.exp2(scores - jnp.max(scores, 0, keepdims=True))
        total = jnp.sum(weights, 0, keepdims=True)
        weights = weights * (weight_ref[0, pl.ds(first + h, 1), :] / total)
        at = slice(h * HEAD_DIM, (h + 1) * HEAD_DIM)
        local_ref[:, at] = lax.dot_general(
            weights.astype(BF16),
            value_ref[:, columns(first + h)],
            (((0,), (0,)), ((), ())),
            preferred_element_type=F32,
        )
        query = query_ref[:, columns(first + h)].astype(F32)
        mean = jnp.dot((query * query).astype(BF16), ones, preferred_element_type=F32)
        query = query * lax.rsqrt(mean + EPSILON)
        for slot, read_ref in enumerate(read_refs):
            which = slot * heads + h
            read_ref[:, at] = (query * gains[:, which : which + 1]).astype(BF16)


def local_part(coefs, slots, turn, frame_len, window_back, queries, keys, values, weights, after):
    tokens, width = queries.shape
    width //= 2
    return pl.pallas_call(
        functools.partial(local_kernel, coefs, turn),
        out_shape=[pltpu.VMEM((tokens, width), F32)] + [pltpu.VMEM((tokens, width), BF16)] * slots,
        in_specs=[SCALARS] * 2 + [WHOLE] * 4 + [ANYWHERE],
        out_specs=[WHOLE] * (1 + slots),
        compiler_params=PARAMS,
        cost_estimate=pl.CostEstimate(
            flops=4 * tokens * tokens * width,
            bytes_accessed=14 * tokens * width,
            transcendentals=tokens * width,
        ),
    )(frame_len, window_back, queries, *in_vmem(keys, values), weights, after)


def read_heads(d, chips, base_ref, states):
    count = HEADS // 2 // chips
    first = (lax.axis_index("chip") ^ d) * count
    for h in range(count):
        at = columns(first + h)
        result = base_ref[:, at]
        for read_ref, state_ref, row in states:
            result = result + jnp.dot(
                read_ref[:, at],
                state_ref[row + h * HEAD_DIM : row + (h + 1) * HEAD_DIM, :],
                preferred_element_type=F32,
            )
        yield at, result


def middle_kernel(chips, early, local_ref, x_ref, y_ref, state_ref, out_ref):
    rows = state_ref.shape[0] // (chips + early)
    for d in range(chips):
        states = [(x_ref, state_ref, d * rows)]
        if d < early:
            states.append((y_ref, state_ref, (chips + d) * rows))
        for at, result in read_heads(d, chips, local_ref, states):
            out_ref[:, at] = result


def read_middle(cost, chips, early, local, x, y, states):
    return pl.pallas_call(
        functools.partial(middle_kernel, chips, early),
        out_shape=pltpu.VMEM(local.shape, F32),
        in_specs=[WHOLE] * 4,
        out_specs=WHOLE,
        compiler_params=PARAMS,
        cost_estimate=cost,
    )(*in_vmem(local, x, y, states))


def late_kernel(turn, chips, early, base_ref, y_ref, *refs):
    *state_refs, out_ref, held, sems = refs
    rows = base_ref.shape[1] // chips
    half = core_heads()[turn]
    copies = []
    for d in range(chips):
        states = []
        if d >= early:
            ref = state_refs[0] if d < chips - 1 else state_refs[-1]
            states.append((y_ref, ref, (d - early) * rows if d < chips - 1 else 0))
        for at, result in read_heads(d, chips, base_ref, states):
            held[:, at] = result.astype(BF16)
        count = HEADS // 2 // chips
        first = (lax.axis_index("chip") ^ d) * count
        copies.append(
            pltpu.make_async_copy(
                held.at[:, columns(first, count)], out_ref.at[:, columns(half + first, count)], sems.at[d]
            )
        )
        copies[-1].start()
    for copy in copies:
        copy.wait()


def aliased_kernel(turn, chips, early, out_before_ref, *refs):
    late_kernel(turn, chips, early, *refs)


def write_late(turn, chips, early, base, y, states, out=None):
    tokens, width = base.shape
    before = [] if out is None else [out]
    kernel = late_kernel if out is None else aliased_kernel
    return pl.pallas_call(
        functools.partial(kernel, turn, chips, early),
        out_shape=jax.ShapeDtypeStruct((tokens, 2 * width), BF16),
        in_specs=[ANYWHERE] * len(before) + [WHOLE] * (2 + len(states)),
        out_specs=ANYWHERE,
        input_output_aliases={0: 0} if before else {},
        scratch_shapes=[pltpu.VMEM((tokens, width), BF16), pltpu.SemaphoreType.DMA((chips,))],
        compiler_params=PARAMS,
        cost_estimate=SMALL if before else LARGE,
    )(*before, *in_vmem(base, y, *states))


def swap(array, axis, mask, size):
    return lax.ppermute(array, axis, [(n, n ^ mask) for n in range(size)])


def body(sizes, queries, keys, values, level_weight, frame_len, window_back):
    frames, outer, chips = sizes
    low, high = (
        1.0 / math.sqrt(HEAD_DIM * 2**level * queries.shape[0] * outer * chips * 2) for level in (0, 1)
    )

    def coefs(f):
        x_low = jnp.where(f % 2 == 1, low, 0.0)
        x_high = jnp.where(f == 2, high, 0.0)
        return [[(0, x_low), (1, x_high)], [(1, jnp.where(f == 3, high, 0.0))]]

    local = functools.partial(local_part, coefs, 2)
    rest = (frame_len, window_back, queries)
    early = 1

    order = [*range(min(2, chips - 1), 0, -1), *range(3, chips)]

    outgoing, keys, values = outgoing_state(keys, values)
    incoming = swap(outgoing, "core", 1, 2)
    mine = own_state(keys, values)
    own, *sends = chip_pieces(mine, incoming, chips)
    got = [swap(sends[d - 1], "chip", d, chips) for d in order]
    local_0, x_0, y_0 = local(0, *rest, keys, values, level_weight, own)
    state = sum_pieces(local_0, own, got, F32 if outer > 1 else BF16)
    if outer > 1:
        state = lax.psum(state, "outer").astype(BF16)
    local_1, x_1, y_1 = local(1, *rest, keys, values, level_weight, state)
    shifted = lax.ppermute(state, "frame", [(f, (f + 1) % frames) for f in range(frames)])
    slot = choose_slot(local_1, shifted, swap(state, "frame", 2, frames))

    x = [slot] + [swap(slot, "chip", d, chips) for d in range(1, chips)]
    y = [swap(slot, "frame", 1, frames)]
    y += [swap(piece, "frame", 1, frames) for piece in x[1:]]
    places = [0, *range(chips + early - 1, 2, -1), *range(1, min(3, chips + early))]
    own_states = pack(x + y[:early], places, [local_1])
    other_states = swap(own_states, "core", 1, 2)
    base_0 = read_middle(SMALL, chips, early, local_0, x_0, y_0, own_states)
    base_1 = read_middle(LARGE, chips, early, local_1, x_1, y_1, other_states)
    late_own = [pack(y[early:-1], list(range(chips - 1 - early)), [])] if chips - 1 > early else []
    late_other = [swap(piece, "core", 1, 2) for piece in late_own]
    if chips > early:
        last = y[-1]
        late_own.append(last)
        late_other.append(swap(last, "core", 1, 2))
    out = write_late(0, chips, early, base_0, y_0, late_own)
    return write_late(1, chips, early, base_1, y_1, late_other, out)


def solution(mesh):
    frames, space = mesh.shape["frame"], mesh.shape["space"]
    chips = 1
    while HEADS % (chips * 4) == 0 and space % (chips * 4) == 0 and chips < 4:
        chips *= 2
    sizes = (frames, space // (2 * chips), chips)
    names = ("frame", "outer", "chip", "core")
    fine = Mesh(mesh.devices.reshape(sizes + (2,)), names)
    rows = P(names, None)
    return jax.shard_map(
        functools.partial(body, sizes),
        mesh=fine,
        in_specs=(rows, rows, rows, P(None, None, names), rows, rows),
        out_specs=rows,
        check_vma=False,
    )
```

```python
import functools
import math

import jax
import jax.numpy as jnp
from jax import lax
from jax.experimental import pallas as pl
from jax.experimental.pallas import tpu as pltpu
from jax.sharding import Mesh, PartitionSpec as P

HEADS = 24
HEAD_DIM = 128
EPSILON = 1e-06
VMEM_LIMIT = 40 * 1024 * 1024

F32, BF16 = jnp.float32, jnp.bfloat16
WHOLE = pl.BlockSpec(memory_space=pltpu.VMEM)
SCALARS = pl.BlockSpec(memory_space=pltpu.SMEM)
ANYWHERE = pl.BlockSpec(memory_space=pl.ANY)
IN_HBM = pl.BlockSpec(memory_space=pltpu.HBM)
SMALL = pl.CostEstimate(flops=1024, bytes_accessed=1024, transcendentals=0)
LARGE = pl.CostEstimate(flops=2 * 10**10, bytes_accessed=1024, transcendentals=0)
PARAMS = pltpu.CompilerParams(vmem_limit_bytes=VMEM_LIMIT)


def inverse_rms(rows):
    return lax.rsqrt(jnp.mean(rows * rows, -1, keepdims=True) + EPSILON)


def columns(head, count=1):
    return pl.ds(pl.multiple_of(head * HEAD_DIM, HEAD_DIM), count * HEAD_DIM)


def core_heads():
    core = lax.axis_index("core")
    return core * (HEADS // 2), (1 - core) * (HEADS // 2)


def in_vmem(*arrays):
    return [pltpu.with_memory_space_constraint(array, pltpu.VMEM) for array in arrays]


def states_of(first, keys, values, out_ref, ready=lambda h: None):
    for h in range(out_ref.shape[0] // HEAD_DIM):
        ready(h)
        at = columns(first + h)
        key_rows = keys[:, at].astype(F32)
        normal = (key_rows * inverse_rms(key_rows)).astype(BF16)
        state = lax.dot_general(
            normal, values[:, at], (((0,), (0,)), ((), ())), preferred_element_type=F32
        )
        out_ref[h * HEAD_DIM : (h + 1) * HEAD_DIM, :] = state.astype(out_ref.dtype)


def first_kernel(parts, key_ref, value_ref, out_ref, keys, values, sems):
    mine, other = core_heads()
    half = HEADS // 2
    starts = [(other + h, half // parts) for h in range(0, half, half // parts)] + [(mine, half)]
    copies = []
    for n, (first, heads) in enumerate(starts):
        at = columns(first, heads)
        pair = [
            pltpu.make_async_copy(ref.at[:, at], held.at[:, at], sems.at[n, s])
            for s, (ref, held) in enumerate(((key_ref, keys), (value_ref, values)))
        ]
        for copy in pair:
            copy.start()
        copies.append(pair)

    def ready(h):
        if h % (half // parts) == 0:
            for copy in copies[h // (half // parts)]:
                copy.wait()

    states_of(other, keys, values, out_ref, ready)
    for copy in copies[-1]:
        copy.wait()


def outgoing_state(keys, values):
    dim, half = HEAD_DIM, HEADS // 2
    rows, parts = keys.shape[0], 1
    keys, values = (pltpu.with_memory_space_constraint(x, pltpu.HBM) for x in (keys, values))
    return pl.pallas_call(
        functools.partial(first_kernel, parts),
        out_shape=[pltpu.VMEM((half * dim, dim), BF16)] + [pltpu.VMEM(keys.shape, BF16)] * 2,
        in_specs=[IN_HBM, IN_HBM],
        out_specs=[WHOLE] * 3,
        scratch_shapes=[pltpu.SemaphoreType.DMA((parts + 1, 2))],
        compiler_params=PARAMS,
        cost_estimate=pl.CostEstimate(
            flops=2 * half * rows * dim * dim, bytes_accessed=8 * half * rows * dim, transcendentals=0
        ),
    )(keys, values)


def own_kernel(key_ref, value_ref, out_ref):
    states_of(core_heads()[0], key_ref, value_ref, out_ref)


def own_state(keys, values):
    dim, half = HEAD_DIM, HEADS // 2
    rows = keys.shape[0]
    return pl.pallas_call(
        own_kernel,
        out_shape=pltpu.VMEM((half * dim, dim), F32),
        in_specs=[WHOLE, WHOLE],
        out_specs=WHOLE,
        compiler_params=PARAMS,
        cost_estimate=pl.CostEstimate(
            flops=2 * half * rows * dim * dim, bytes_accessed=8 * half * rows * dim, transcendentals=0
        ),
    )(*in_vmem(keys, values))


def piece_kernel(mine_ref, other_ref, own_ref, *piece_refs):
    chip = lax.axis_index("chip")
    rows = own_ref.shape[0]
    for d, ref in enumerate((own_ref,) + piece_refs):
        at = pl.ds(pl.multiple_of((chip ^ d) * rows, rows), rows)
        ref[...] = (mine_ref[at, :] + other_ref[at, :].astype(F32)).astype(ref.dtype)


def chip_pieces(mine, other, chips):
    shape = (mine.shape[0] // chips, HEAD_DIM)
    return pl.pallas_call(
        piece_kernel,
        out_shape=[pltpu.VMEM(shape, F32)] + [pltpu.VMEM(shape, BF16)] * (chips - 1),
        in_specs=[WHOLE, WHOLE],
        out_specs=[WHOLE] * chips,
        compiler_params=PARAMS,
        cost_estimate=SMALL,
    )(*in_vmem(mine, other))


def sum_kernel(after_ref, own_ref, *refs):
    total = own_ref[...]
    for ref in refs[:-1]:
        total = total + ref[...].astype(F32)
    refs[-1][...] = total.astype(refs[-1].dtype)


def sum_pieces(after, own, parts, dtype):
    return pl.pallas_call(
        sum_kernel,
        out_shape=pltpu.VMEM(own.shape, dtype),
        in_specs=[ANYWHERE] + [WHOLE] * (1 + len(parts)),
        out_specs=WHOLE,
        compiler_params=PARAMS,
        cost_estimate=SMALL,
    )(after, *in_vmem(own, *parts))


def slot_kernel(after_ref, before_ref, first_ref, out_ref):
    before = before_ref[...].astype(F32)
    both = first_ref[...].astype(F32) + before
    out_ref[...] = jnp.where(lax.axis_index("frame") == 2, both, before).astype(BF16)


def choose_slot(after, before, first):
    return pl.pallas_call(
        slot_kernel,
        out_shape=pltpu.VMEM(before.shape, BF16),
        in_specs=[ANYWHERE] + [WHOLE] * 2,
        out_specs=WHOLE,
        compiler_params=PARAMS,
        cost_estimate=SMALL,
    )(after, *in_vmem(before, first))


def pack_kernel(after, order, *refs):
    out_ref, refs = refs[-1], refs[after:-1]
    rows = refs[0].shape[0]
    for place, ref in zip(order, refs):
        out_ref[place * rows : (place + 1) * rows, :] = ref[...]


def pack(pieces, order, after):
    rows = sum(array.shape[0] for array in pieces)
    pieces = [pieces[place] for place in order]
    return pl.pallas_call(
        functools.partial(pack_kernel, len(after), order),
        out_shape=pltpu.VMEM((rows, HEAD_DIM), BF16),
        in_specs=[ANYWHERE] * len(after) + [WHOLE] * len(pieces),
        out_specs=WHOLE,
        compiler_params=PARAMS,
        cost_estimate=SMALL,
    )(*after, *in_vmem(*pieces))


def local_kernel(
    coefs, turn, length_ref, back_ref, query_ref, key_ref, value_ref, weight_ref, after_ref, local_ref, *read_refs
):
    tokens = query_ref.shape[0]
    first = core_heads()[turn]
    heads = local_ref.shape[1] // HEAD_DIM
    key_at = lax.broadcasted_iota(jnp.int32, (tokens, tokens), 0)
    query_at = lax.broadcasted_iota(jnp.int32, (tokens, tokens), 1)
    start = jnp.int32(0)
    floor = jnp.zeros((tokens, tokens), jnp.int32)
    for k in range(length_ref.shape[1]):
        lowest = jnp.maximum(start - back_ref[0, k], 0)
        floor = jnp.where(query_at >= start, lowest, floor)
        start = start + length_ref[0, k]
    hidden = jnp.where((key_at <= query_at) & (key_at >= floor), 0.0, -jnp.inf).astype(F32)
    scale = math.log2(math.e) / math.sqrt(HEAD_DIM)
    ones = jnp.full((HEAD_DIM, HEAD_DIM), 1.0 / HEAD_DIM, BF16)
    half = HEADS // 2
    by_slot = []
    for slot_coefs in coefs(lax.axis_index("frame")):
        total = None
        for level, coef in slot_coefs:
            term = weight_ref[1 + level, pl.ds(first, heads), :] * coef
            total = term if total is None else total + term
        by_slot.append(total)
    pad = -len(by_slot) * heads % HEAD_DIM
    gains = jnp.concatenate(by_slot + [jnp.zeros((pad, tokens), F32)], 0).T

    def scores_of(h):
        at = columns(first + h)
        return lax.dot_general(
            key_ref[:, at], query_ref[:, at], (((1,), (1,)), ((), ())), preferred_element_type=F32
        )

    upcoming = scores_of(0)
    for h in range(heads):
        scores = upcoming * scale + hidden
        if h + 1 < heads:
            upcoming = scores_of(h + 1)
        weights = jnp.exp2(scores - jnp.max(scores, 0, keepdims=True))
        total = jnp.sum(weights, 0, keepdims=True)
        weights = weights * (weight_ref[0, pl.ds(first + h, 1), :] / total)
        at = slice(h * HEAD_DIM, (h + 1) * HEAD_DIM)
        local_ref[:, at] = lax.dot_general(
            weights.astype(BF16),
            value_ref[:, columns(first + h)],
            (((0,), (0,)), ((), ())),
            preferred_element_type=F32,
        )
        query = query_ref[:, columns(first + h)].astype(F32)
        mean = jnp.dot((query * query).astype(BF16), ones, preferred_element_type=F32)
        query = query * lax.rsqrt(mean + EPSILON)
        for slot, read_ref in enumerate(read_refs):
            which = slot * heads + h
            read_ref[:, at] = (query * gains[:, which : which + 1]).astype(BF16)


def local_part(coefs, slots, turn, frame_len, window_back, queries, keys, values, weights, after):
    tokens, width = queries.shape
    width //= 2
    return pl.pallas_call(
        functools.partial(local_kernel, coefs, turn),
        out_shape=[pltpu.VMEM((tokens, width), F32)] + [pltpu.VMEM((tokens, width), BF16)] * slots,
        in_specs=[SCALARS] * 2 + [WHOLE] * 4 + [ANYWHERE],
        out_specs=[WHOLE] * (1 + slots),
        compiler_params=PARAMS,
        cost_estimate=pl.CostEstimate(
            flops=4 * tokens * tokens * width,
            bytes_accessed=14 * tokens * width,
            transcendentals=tokens * width,
        ),
    )(frame_len, window_back, queries, *in_vmem(keys, values), weights, after)


def read_heads(d, chips, base_ref, states):
    count = HEADS // 2 // chips
    first = (lax.axis_index("chip") ^ d) * count
    for h in range(count):
        at = columns(first + h)
        result = base_ref[:, at]
        for read_ref, state_ref, row in states:
            result = result + jnp.dot(
                read_ref[:, at],
                state_ref[row + h * HEAD_DIM : row + (h + 1) * HEAD_DIM, :],
                preferred_element_type=F32,
            )
        yield at, result


def middle_kernel(chips, early, local_ref, x_ref, y_ref, state_ref, out_ref):
    rows = state_ref.shape[0] // (chips + early)
    for d in range(chips):
        states = [(x_ref, state_ref, d * rows)]
        if d < early:
            states.append((y_ref, state_ref, (chips + d) * rows))
        for at, result in read_heads(d, chips, local_ref, states):
            out_ref[:, at] = result


def read_middle(chips, early, local, x, y, states):
    return pl.pallas_call(
        functools.partial(middle_kernel, chips, early),
        out_shape=pltpu.VMEM(local.shape, F32),
        in_specs=[WHOLE] * 4,
        out_specs=WHOLE,
        compiler_params=PARAMS,
        cost_estimate=SMALL,
    )(*in_vmem(local, x, y, states))


def late_kernel(turn, chips, early, base_ref, y_ref, *refs):
    *state_refs, out_ref, held, sems = refs
    rows = base_ref.shape[1] // chips
    half = core_heads()[turn]
    copies = []
    for d in range(chips):
        states = [(y_ref, state_refs[0], (d - early) * rows)] if d >= early else []
        for at, result in read_heads(d, chips, base_ref, states):
            held[:, at] = result.astype(BF16)
        count = HEADS // 2 // chips
        first = (lax.axis_index("chip") ^ d) * count
        copies.append(
            pltpu.make_async_copy(
                held.at[:, columns(first, count)], out_ref.at[:, columns(half + first, count)], sems.at[d]
            )
        )
        copies[-1].start()
    for copy in copies:
        copy.wait()


def aliased_kernel(turn, chips, early, out_before_ref, *refs):
    late_kernel(turn, chips, early, *refs)


def write_late(turn, chips, early, base, y, states, out=None):
    tokens, width = base.shape
    before = [] if out is None else [out]
    kernel = late_kernel if out is None else aliased_kernel
    return pl.pallas_call(
        functools.partial(kernel, turn, chips, early),
        out_shape=jax.ShapeDtypeStruct((tokens, 2 * width), BF16),
        in_specs=[ANYWHERE] * len(before) + [WHOLE] * (2 + len(states)),
        out_specs=ANYWHERE,
        input_output_aliases={0: 0} if before else {},
        scratch_shapes=[pltpu.VMEM((tokens, width), BF16), pltpu.SemaphoreType.DMA((chips,))],
        compiler_params=PARAMS,
        cost_estimate=SMALL if before else LARGE,
    )(*before, *in_vmem(base, y, *states))


def swap(array, axis, mask, size):
    return lax.ppermute(array, axis, [(n, n ^ mask) for n in range(size)])


def body(sizes, queries, keys, values, level_weight, frame_len, window_back):
    frames, outer, chips = sizes
    low, high = (
        1.0 / math.sqrt(HEAD_DIM * 2**level * queries.shape[0] * outer * chips * 2) for level in (0, 1)
    )

    def coefs(f):
        x_low = jnp.where(f % 2 == 1, low, 0.0)
        x_high = jnp.where(f == 2, high, 0.0)
        return [[(0, x_low), (1, x_high)], [(1, jnp.where(f == 3, high, 0.0))]]

    local = functools.partial(local_part, coefs, 2)
    rest = (frame_len, window_back, queries)
    early = 1

    outgoing, keys, values = outgoing_state(keys, values)
    incoming = swap(outgoing, "core", 1, 2)
    mine = own_state(keys, values)
    own, *sends = chip_pieces(mine, incoming, chips)
    got = [swap(sends[d - 1], "chip", d, chips) for d in reversed(range(1, chips))]
    local_0, x_0, y_0 = local(0, *rest, keys, values, level_weight, own)
    state = sum_pieces(local_0, own, got, F32 if outer > 1 else BF16)
    if outer > 1:
        state = lax.psum(state, "outer").astype(BF16)
    local_1, x_1, y_1 = local(1, *rest, keys, values, level_weight, state)
    shifted = lax.ppermute(state, "frame", [(f, (f + 1) % frames) for f in range(frames)])
    slot = choose_slot(local_1, shifted, swap(state, "frame", 2, frames))

    x = [slot] + [swap(slot, "chip", d, chips) for d in range(1, chips)]
    y = [swap(slot, "frame", 1, frames)]
    y += [swap(piece, "frame", 1, frames) for piece in x[1:3]]
    for d in range(3, chips):
        pairs = [(f * chips + c, (f ^ 1) * chips + (c ^ d)) for f in range(frames) for c in range(chips)]
        y.append(lax.ppermute(slot, ("frame", "chip"), pairs))
    places = [0, *range(chips + early - 1, 2, -1), *range(1, min(3, chips + early))]
    own_states = pack(x + y[:early], places, [local_1])
    other_states = swap(own_states, "core", 1, 2)
    base_0 = read_middle(chips, early, local_0, x_0, y_0, own_states)
    base_1 = read_middle(chips, early, local_1, x_1, y_1, other_states)
    late = y[early:]
    late_own = [pack(late, list(range(len(late))), [])] if late else []
    late_other = [swap(piece, "core", 1, 2) for piece in late_own]
    out = write_late(0, chips, early, base_0, y_0, late_own)
    return write_late(1, chips, early, base_1, y_1, late_other, out)


def solution(mesh):
    frames, space = mesh.shape["frame"], mesh.shape["space"]
    chips = 1
    while HEADS % (chips * 4) == 0 and space % (chips * 4) == 0 and chips < 4:
        chips *= 2
    sizes = (frames, space // (2 * chips), chips)
    names = ("frame", "outer", "chip", "core")
    fine = Mesh(mesh.devices.reshape(sizes + (2,)), names)
    rows = P(names, None)
    return jax.shard_map(
        functools.partial(body, sizes),
        mesh=fine,
        in_specs=(rows, rows, rows, P(None, None, names), rows, rows),
        out_specs=rows,
        check_vma=False,
    )
```

```python
import functools
import math

import jax
import jax.numpy as jnp
from jax import lax
from jax.experimental import pallas as pl
from jax.experimental.pallas import tpu as pltpu
from jax.sharding import Mesh, PartitionSpec as P

HEADS = 24
HEAD_DIM = 128
EPSILON = 1e-06
VMEM_LIMIT = 40 * 1024 * 1024

F32, BF16 = jnp.float32, jnp.bfloat16
WHOLE = pl.BlockSpec(memory_space=pltpu.VMEM)
SCALARS = pl.BlockSpec(memory_space=pltpu.SMEM)
ANYWHERE = pl.BlockSpec(memory_space=pl.ANY)
IN_HBM = pl.BlockSpec(memory_space=pltpu.HBM)
SMALL = pl.CostEstimate(flops=1024, bytes_accessed=1024, transcendentals=0)
LARGE = pl.CostEstimate(flops=2 * 10**10, bytes_accessed=1024, transcendentals=0)
PARAMS = pltpu.CompilerParams(vmem_limit_bytes=VMEM_LIMIT)


def inverse_rms(rows):
    return lax.rsqrt(jnp.mean(rows * rows, -1, keepdims=True) + EPSILON)


def columns(head, count=1):
    return pl.ds(pl.multiple_of(head * HEAD_DIM, HEAD_DIM), count * HEAD_DIM)


def core_heads():
    core = lax.axis_index("core")
    return core * (HEADS // 2), (1 - core) * (HEADS // 2)


def in_vmem(*arrays):
    return [pltpu.with_memory_space_constraint(array, pltpu.VMEM) for array in arrays]


def states_of(first, keys, values, out_ref, ready=lambda h: None):
    for h in range(out_ref.shape[0] // HEAD_DIM):
        ready(h)
        at = columns(first + h)
        key_rows = keys[:, at].astype(F32)
        normal = (key_rows * inverse_rms(key_rows)).astype(BF16)
        state = lax.dot_general(
            normal, values[:, at], (((0,), (0,)), ((), ())), preferred_element_type=F32
        )
        out_ref[h * HEAD_DIM : (h + 1) * HEAD_DIM, :] = state.astype(out_ref.dtype)


def first_kernel(parts, key_ref, value_ref, out_ref, keys, values, sems):
    mine, other = core_heads()
    half = HEADS // 2
    starts = [(other + h, half // parts) for h in range(0, half, half // parts)] + [(mine, half)]
    copies = []
    for n, (first, heads) in enumerate(starts):
        at = columns(first, heads)
        pair = [
            pltpu.make_async_copy(ref.at[:, at], held.at[:, at], sems.at[n, s])
            for s, (ref, held) in enumerate(((key_ref, keys), (value_ref, values)))
        ]
        for copy in pair:
            copy.start()
        copies.append(pair)

    def ready(h):
        if h % (half // parts) == 0:
            for copy in copies[h // (half // parts)]:
                copy.wait()

    states_of(other, keys, values, out_ref, ready)
    for copy in copies[-1]:
        copy.wait()


def outgoing_state(keys, values):
    dim, half = HEAD_DIM, HEADS // 2
    rows, parts = keys.shape[0], 1
    keys, values = (pltpu.with_memory_space_constraint(x, pltpu.HBM) for x in (keys, values))
    return pl.pallas_call(
        functools.partial(first_kernel, parts),
        out_shape=[pltpu.VMEM((half * dim, dim), BF16)] + [pltpu.VMEM(keys.shape, BF16)] * 2,
        in_specs=[IN_HBM, IN_HBM],
        out_specs=[WHOLE] * 3,
        scratch_shapes=[pltpu.SemaphoreType.DMA((parts + 1, 2))],
        compiler_params=PARAMS,
        cost_estimate=pl.CostEstimate(
            flops=2 * half * rows * dim * dim, bytes_accessed=8 * half * rows * dim, transcendentals=0
        ),
    )(keys, values)


def own_kernel(key_ref, value_ref, out_ref):
    states_of(core_heads()[0], key_ref, value_ref, out_ref)


def own_state(keys, values):
    dim, half = HEAD_DIM, HEADS // 2
    rows = keys.shape[0]
    return pl.pallas_call(
        own_kernel,
        out_shape=pltpu.VMEM((half * dim, dim), F32),
        in_specs=[WHOLE, WHOLE],
        out_specs=WHOLE,
        compiler_params=PARAMS,
        cost_estimate=pl.CostEstimate(
            flops=2 * half * rows * dim * dim, bytes_accessed=8 * half * rows * dim, transcendentals=0
        ),
    )(*in_vmem(keys, values))


def piece_kernel(orders, mine_ref, other_ref, own_ref, *piece_refs):
    chip = lax.axis_index("chip")
    rows = own_ref.shape[0]
    second = lax.axis_index("core") == 1
    for (d, e), ref in zip(((0, 0), *orders), (own_ref,) + piece_refs):
        at = pl.ds(pl.multiple_of((chip ^ jnp.where(second, e, d)) * rows, rows), rows)
        ref[...] = (mine_ref[at, :] + other_ref[at, :].astype(F32)).astype(ref.dtype)


def chip_pieces(orders, mine, other, chips):
    shape = (mine.shape[0] // chips, HEAD_DIM)
    return pl.pallas_call(
        functools.partial(piece_kernel, orders),
        out_shape=[pltpu.VMEM(shape, F32)] + [pltpu.VMEM(shape, BF16)] * (chips - 1),
        in_specs=[WHOLE, WHOLE],
        out_specs=[WHOLE] * chips,
        compiler_params=PARAMS,
        cost_estimate=SMALL,
    )(*in_vmem(mine, other))


def sum_kernel(after_ref, own_ref, *refs):
    total = own_ref[...]
    for ref in refs[:-1]:
        total = total + ref[...].astype(F32)
    refs[-1][...] = total.astype(refs[-1].dtype)


def sum_pieces(after, own, parts, dtype):
    return pl.pallas_call(
        sum_kernel,
        out_shape=pltpu.VMEM(own.shape, dtype),
        in_specs=[ANYWHERE] + [WHOLE] * (1 + len(parts)),
        out_specs=WHOLE,
        compiler_params=PARAMS,
        cost_estimate=SMALL,
    )(after, *in_vmem(own, *parts))


def slot_kernel(after_ref, one_ref, two_ref, out_ref):
    one, two = one_ref[...].astype(F32), two_ref[...].astype(F32)
    before = jnp.where(lax.axis_index("core") == 0, one, two)
    out_ref[...] = jnp.where(lax.axis_index("frame") == 2, one + two, before).astype(BF16)


def choose_slot(after, one, two):
    return pl.pallas_call(
        slot_kernel,
        out_shape=pltpu.VMEM(one.shape, BF16),
        in_specs=[ANYWHERE] + [WHOLE] * 2,
        out_specs=WHOLE,
        compiler_params=PARAMS,
        cost_estimate=SMALL,
    )(after, *in_vmem(one, two))


def pack_kernel(after, order, *refs):
    out_ref, refs = refs[-1], refs[after:-1]
    rows = refs[0].shape[0]
    for place, ref in zip(order, refs):
        out_ref[place * rows : (place + 1) * rows, :] = ref[...]


def pack(pieces, order, after):
    rows = sum(array.shape[0] for array in pieces)
    pieces = [pieces[place] for place in order]
    return pl.pallas_call(
        functools.partial(pack_kernel, len(after), order),
        out_shape=pltpu.VMEM((rows, HEAD_DIM), BF16),
        in_specs=[ANYWHERE] * len(after) + [WHOLE] * len(pieces),
        out_specs=WHOLE,
        compiler_params=PARAMS,
        cost_estimate=SMALL,
    )(*after, *in_vmem(*pieces))


def local_kernel(
    coefs, turn, length_ref, back_ref, query_ref, key_ref, value_ref, weight_ref, after_ref, local_ref, *read_refs
):
    tokens = query_ref.shape[0]
    first = core_heads()[turn]
    heads = local_ref.shape[1] // HEAD_DIM
    key_at = lax.broadcasted_iota(jnp.int32, (tokens, tokens), 0)
    query_at = lax.broadcasted_iota(jnp.int32, (tokens, tokens), 1)
    start = jnp.int32(0)
    floor = jnp.zeros((tokens, tokens), jnp.int32)
    for k in range(length_ref.shape[1]):
        lowest = jnp.maximum(start - back_ref[0, k], 0)
        floor = jnp.where(query_at >= start, lowest, floor)
        start = start + length_ref[0, k]
    hidden = jnp.where((key_at <= query_at) & (key_at >= floor), 0.0, -jnp.inf).astype(F32)
    scale = math.log2(math.e) / math.sqrt(HEAD_DIM)
    ones = jnp.full((HEAD_DIM, HEAD_DIM), 1.0 / HEAD_DIM, BF16)
    half = HEADS // 2
    by_slot = []
    for slot_coefs in coefs(lax.axis_index("frame")):
        total = None
        for level, coef in slot_coefs:
            term = weight_ref[1 + level, pl.ds(first, heads), :] * coef
            total = term if total is None else total + term
        by_slot.append(total)
    pad = -len(by_slot) * heads % HEAD_DIM
    gains = jnp.concatenate(by_slot + [jnp.zeros((pad, tokens), F32)], 0).T

    def scores_of(h):
        at = columns(first + h)
        return lax.dot_general(
            key_ref[:, at], query_ref[:, at], (((1,), (1,)), ((), ())), preferred_element_type=F32
        )

    upcoming = scores_of(0)
    for h in range(heads):
        scores = upcoming * scale + hidden
        if h + 1 < heads:
            upcoming = scores_of(h + 1)
        weights = jnp.exp2(scores - jnp.max(scores, 0, keepdims=True))
        total = jnp.sum(weights, 0, keepdims=True)
        weights = weights * (weight_ref[0, pl.ds(first + h, 1), :] / total)
        at = slice(h * HEAD_DIM, (h + 1) * HEAD_DIM)
        local_ref[:, at] = lax.dot_general(
            weights.astype(BF16),
            value_ref[:, columns(first + h)],
            (((0,), (0,)), ((), ())),
            preferred_element_type=F32,
        )
        query = query_ref[:, columns(first + h)].astype(F32)
        mean = jnp.dot((query * query).astype(BF16), ones, preferred_element_type=F32)
        query = query * lax.rsqrt(mean + EPSILON)
        for slot, read_ref in enumerate(read_refs):
            which = slot * heads + h
            read_ref[:, at] = (query * gains[:, which : which + 1]).astype(BF16)


def local_part(coefs, slots, turn, frame_len, window_back, queries, keys, values, weights, after):
    tokens, width = queries.shape
    width //= 2
    return pl.pallas_call(
        functools.partial(local_kernel, coefs, turn),
        out_shape=[pltpu.VMEM((tokens, width), F32)] + [pltpu.VMEM((tokens, width), BF16)] * slots,
        in_specs=[SCALARS] * 2 + [WHOLE] * 4 + [ANYWHERE],
        out_specs=[WHOLE] * (1 + slots),
        compiler_params=PARAMS,
        cost_estimate=pl.CostEstimate(
            flops=4 * tokens * tokens * width,
            bytes_accessed=14 * tokens * width,
            transcendentals=tokens * width,
        ),
    )(frame_len, window_back, queries, *in_vmem(keys, values), weights, after)


def read_heads(d, chips, base_ref, states):
    count = HEADS // 2 // chips
    first = (lax.axis_index("chip") ^ d) * count
    for h in range(count):
        at = columns(first + h)
        result = base_ref[:, at]
        for read_ref, state_ref, row in states:
            result = result + jnp.dot(
                read_ref[:, at],
                state_ref[row + h * HEAD_DIM : row + (h + 1) * HEAD_DIM, :],
                preferred_element_type=F32,
            )
        yield at, result


def middle_kernel(chips, early, local_ref, x_ref, y_ref, state_ref, out_ref):
    rows = state_ref.shape[0] // (chips + early)
    for d in range(chips):
        states = [(x_ref, state_ref, d * rows)]
        if d < early:
            states.append((y_ref, state_ref, (chips + d) * rows))
        for at, result in read_heads(d, chips, local_ref, states):
            out_ref[:, at] = result


def read_middle(chips, early, local, x, y, states):
    return pl.pallas_call(
        functools.partial(middle_kernel, chips, early),
        out_shape=pltpu.VMEM(local.shape, F32),
        in_specs=[WHOLE] * 4,
        out_specs=WHOLE,
        compiler_params=PARAMS,
        cost_estimate=SMALL,
    )(*in_vmem(local, x, y, states))


def late_kernel(turn, chips, early, base_ref, y_ref, *refs):
    *state_refs, out_ref, held, sems = refs
    rows = base_ref.shape[1] // chips
    half = core_heads()[turn]
    copies = []
    for d in range(chips):
        states = [(y_ref, state_refs[0], (d - early) * rows)] if d >= early else []
        for at, result in read_heads(d, chips, base_ref, states):
            held[:, at] = result.astype(BF16)
        count = HEADS // 2 // chips
        first = (lax.axis_index("chip") ^ d) * count
        copies.append(
            pltpu.make_async_copy(
                held.at[:, columns(first, count)], out_ref.at[:, columns(half + first, count)], sems.at[d]
            )
        )
        copies[-1].start()
    for copy in copies:
        copy.wait()


def aliased_kernel(turn, chips, early, out_before_ref, *refs):
    late_kernel(turn, chips, early, *refs)


def write_late(turn, chips, early, base, y, states, out=None):
    tokens, width = base.shape
    before = [] if out is None else [out]
    kernel = late_kernel if out is None else aliased_kernel
    return pl.pallas_call(
        functools.partial(kernel, turn, chips, early),
        out_shape=jax.ShapeDtypeStruct((tokens, 2 * width), BF16),
        in_specs=[ANYWHERE] * len(before) + [WHOLE] * (2 + len(states)),
        out_specs=ANYWHERE,
        input_output_aliases={0: 0} if before else {},
        scratch_shapes=[pltpu.VMEM((tokens, width), BF16), pltpu.SemaphoreType.DMA((chips,))],
        compiler_params=PARAMS,
        cost_estimate=SMALL if before else LARGE,
    )(*before, *in_vmem(base, y, *states))


def swap(array, axis, mask, size):
    return lax.ppermute(array, axis, [(n, n ^ mask) for n in range(size)])


def body(sizes, queries, keys, values, level_weight, frame_len, window_back):
    frames, outer, chips = sizes
    low, high = (
        1.0 / math.sqrt(HEAD_DIM * 2**level * queries.shape[0] * outer * chips * 2) for level in (0, 1)
    )

    def coefs(f):
        x_low = jnp.where(f % 2 == 1, low, 0.0)
        x_high = jnp.where(f == 2, high, 0.0)
        return [[(0, x_low), (1, x_high)], [(1, jnp.where(f == 3, high, 0.0))]]

    local = functools.partial(local_part, coefs, 2)
    rest = (frame_len, window_back, queries)
    early = 1

    outgoing, keys, values = outgoing_state(keys, values)
    incoming = swap(outgoing, "core", 1, 2)
    mine = own_state(keys, values)
    order = [*reversed(range(1, chips))]
    orders = [*zip(order, order[-1:] + order[:-1])]
    own, *sends = chip_pieces(orders, mine, incoming, chips)
    got = [
        lax.ppermute(
            piece,
            ("chip", "core"),
            [(z * 2 + c, (z ^ pair[c]) * 2 + c) for z in range(chips) for c in range(2)],
        )
        for piece, pair in zip(sends, orders)
    ]
    local_0, x_0, y_0 = local(0, *rest, keys, values, level_weight, own)
    state = sum_pieces(local_0, own, got, F32 if outer > 1 else BF16)
    if outer > 1:
        state = lax.psum(state, "outer").astype(BF16)
    local_1, x_1, y_1 = local(1, *rest, keys, values, level_weight, state)
    moved = [
        lax.ppermute(
            state,
            ("frame", "core"),
            [(f * 2 + c, ((f + 1) % frames if c == turn else f ^ 2) * 2 + c) for f in range(frames) for c in range(2)],
        )
        for turn in range(2)
    ]
    slot = choose_slot(local_1, *moved)

    x = [slot] + [swap(slot, "chip", d, chips) for d in range(1, chips)]
    y = [swap(slot, "frame", 1, frames)]
    y += [swap(piece, "frame", 1, frames) for piece in x[1:]]
    places = [0, *range(chips + early - 1, 2, -1), *range(1, min(3, chips + early))]
    own_states = pack(x + y[:early], places, [local_1])
    other_states = swap(own_states, "core", 1, 2)
    base_0 = read_middle(chips, early, local_0, x_0, y_0, own_states)
    base_1 = read_middle(chips, early, local_1, x_1, y_1, other_states)
    late = y[early:]
    late_own = [pack(late, list(range(len(late))), [])] if late else []
    late_other = [swap(piece, "core", 1, 2) for piece in late_own]
    out = write_late(0, chips, early, base_0, y_0, late_own)
    return write_late(1, chips, early, base_1, y_1, late_other, out)


def solution(mesh):
    frames, space = mesh.shape["frame"], mesh.shape["space"]
    chips = 1
    while HEADS % (chips * 4) == 0 and space % (chips * 4) == 0 and chips < 4:
        chips *= 2
    sizes = (frames, space // (2 * chips), chips)
    names = ("frame", "outer", "chip", "core")
    fine = Mesh(mesh.devices.reshape(sizes + (2,)), names)
    rows = P(names, None)
    return jax.shard_map(
        functools.partial(body, sizes),
        mesh=fine,
        in_specs=(rows, rows, rows, P(None, None, names), rows, rows),
        out_specs=rows,
        check_vma=False,
    )
```

```python
import functools
import math

import jax
import jax.numpy as jnp
from jax import lax
from jax.experimental import pallas as pl
from jax.experimental.pallas import tpu as pltpu
from jax.sharding import Mesh, PartitionSpec as P

HEADS = 24
HEAD_DIM = 128
EPSILON = 1e-06
VMEM_LIMIT = 40 * 1024 * 1024

F32, BF16 = jnp.float32, jnp.bfloat16
WHOLE = pl.BlockSpec(memory_space=pltpu.VMEM)
SCALARS = pl.BlockSpec(memory_space=pltpu.SMEM)
ANYWHERE = pl.BlockSpec(memory_space=pl.ANY)
IN_HBM = pl.BlockSpec(memory_space=pltpu.HBM)
SMALL = pl.CostEstimate(flops=1024, bytes_accessed=1024, transcendentals=0)
LARGE = pl.CostEstimate(flops=2 * 10**10, bytes_accessed=1024, transcendentals=0)
PARAMS = pltpu.CompilerParams(vmem_limit_bytes=VMEM_LIMIT)


def inverse_rms(rows):
    return lax.rsqrt(jnp.mean(rows * rows, -1, keepdims=True) + EPSILON)


def columns(head, count=1):
    return pl.ds(pl.multiple_of(head * HEAD_DIM, HEAD_DIM), count * HEAD_DIM)


def core_heads():
    core = lax.axis_index("core")
    return core * (HEADS // 2), (1 - core) * (HEADS // 2)


def in_vmem(*arrays):
    return [pltpu.with_memory_space_constraint(array, pltpu.VMEM) for array in arrays]


def states_of(first, keys, values, out_ref, ready=lambda h: None):
    for h in range(out_ref.shape[0] // HEAD_DIM):
        ready(h)
        at = columns(first + h)
        key_rows = keys[:, at].astype(F32)
        normal = (key_rows * inverse_rms(key_rows)).astype(BF16)
        state = lax.dot_general(
            normal, values[:, at], (((0,), (0,)), ((), ())), preferred_element_type=F32
        )
        out_ref[h * HEAD_DIM : (h + 1) * HEAD_DIM, :] = state.astype(out_ref.dtype)


def first_kernel(parts, key_ref, value_ref, out_ref, keys, values, sems):
    mine, other = core_heads()
    half = HEADS // 2
    starts = [(other + h, half // parts) for h in range(0, half, half // parts)] + [(mine, half)]
    copies = []
    for n, (first, heads) in enumerate(starts):
        at = columns(first, heads)
        pair = [
            pltpu.make_async_copy(ref.at[:, at], held.at[:, at], sems.at[n, s])
            for s, (ref, held) in enumerate(((key_ref, keys), (value_ref, values)))
        ]
        for copy in pair:
            copy.start()
        copies.append(pair)

    def ready(h):
        if h % (half // parts) == 0:
            for copy in copies[h // (half // parts)]:
                copy.wait()

    states_of(other, keys, values, out_ref, ready)
    for copy in copies[-1]:
        copy.wait()


def outgoing_state(keys, values):
    dim, half = HEAD_DIM, HEADS // 2
    rows, parts = keys.shape[0], 1
    keys, values = (pltpu.with_memory_space_constraint(x, pltpu.HBM) for x in (keys, values))
    return pl.pallas_call(
        functools.partial(first_kernel, parts),
        out_shape=[pltpu.VMEM((half * dim, dim), BF16)] + [pltpu.VMEM(keys.shape, BF16)] * 2,
        in_specs=[IN_HBM, IN_HBM],
        out_specs=[WHOLE] * 3,
        scratch_shapes=[pltpu.SemaphoreType.DMA((parts + 1, 2))],
        compiler_params=PARAMS,
        cost_estimate=pl.CostEstimate(
            flops=2 * half * rows * dim * dim, bytes_accessed=8 * half * rows * dim, transcendentals=0
        ),
    )(keys, values)


def own_kernel(key_ref, value_ref, out_ref):
    states_of(core_heads()[0], key_ref, value_ref, out_ref)


def own_state(keys, values):
    dim, half = HEAD_DIM, HEADS // 2
    rows = keys.shape[0]
    return pl.pallas_call(
        own_kernel,
        out_shape=pltpu.VMEM((half * dim, dim), F32),
        in_specs=[WHOLE, WHOLE],
        out_specs=WHOLE,
        compiler_params=PARAMS,
        cost_estimate=pl.CostEstimate(
            flops=2 * half * rows * dim * dim, bytes_accessed=8 * half * rows * dim, transcendentals=0
        ),
    )(*in_vmem(keys, values))


def piece_kernel(after, *refs):
    mine_ref, other_ref, own_ref, *piece_refs = refs[after:]
    chip = lax.axis_index("chip")
    rows = own_ref.shape[0]
    for d, ref in enumerate([own_ref] + piece_refs):
        at = pl.ds(pl.multiple_of((chip ^ d) * rows, rows), rows)
        ref[...] = (mine_ref[at, :] + other_ref[at, :].astype(F32)).astype(ref.dtype)


def chip_pieces(after, mine, other, chips):
    shape = (mine.shape[0] // chips, HEAD_DIM)
    return pl.pallas_call(
        functools.partial(piece_kernel, len(after)),
        out_shape=[pltpu.VMEM(shape, F32)] + [pltpu.VMEM(shape, BF16)] * (chips - 1),
        in_specs=[ANYWHERE] * len(after) + [WHOLE, WHOLE],
        out_specs=[WHOLE] * chips,
        compiler_params=PARAMS,
        cost_estimate=SMALL,
    )(*after, *in_vmem(mine, other))


def sum_kernel(after_ref, own_ref, *refs):
    total = own_ref[...]
    for ref in refs[:-1]:
        total = total + ref[...].astype(F32)
    refs[-1][...] = total.astype(refs[-1].dtype)


def sum_pieces(after, own, parts, dtype):
    return pl.pallas_call(
        sum_kernel,
        out_shape=pltpu.VMEM(own.shape, dtype),
        in_specs=[ANYWHERE] + [WHOLE] * (1 + len(parts)),
        out_specs=WHOLE,
        compiler_params=PARAMS,
        cost_estimate=SMALL,
    )(after, *in_vmem(own, *parts))


def slot_kernel(after_ref, before_ref, first_ref, out_ref):
    before = before_ref[...].astype(F32)
    both = first_ref[...].astype(F32) + before
    out_ref[...] = jnp.where(lax.axis_index("frame") == 2, both, before).astype(BF16)


def choose_slot(after, before, first):
    return pl.pallas_call(
        slot_kernel,
        out_shape=pltpu.VMEM(before.shape, BF16),
        in_specs=[ANYWHERE] + [WHOLE] * 2,
        out_specs=WHOLE,
        compiler_params=PARAMS,
        cost_estimate=SMALL,
    )(after, *in_vmem(before, first))


def pack_kernel(after, order, *refs):
    out_ref, refs = refs[-1], refs[after:-1]
    rows = refs[0].shape[0]
    for place, ref in zip(order, refs):
        out_ref[place * rows : (place + 1) * rows, :] = ref[...]


def pack(pieces, order, after):
    rows = sum(array.shape[0] for array in pieces)
    pieces = [pieces[place] for place in order]
    return pl.pallas_call(
        functools.partial(pack_kernel, len(after), order),
        out_shape=pltpu.VMEM((rows, HEAD_DIM), BF16),
        in_specs=[ANYWHERE] * len(after) + [WHOLE] * len(pieces),
        out_specs=WHOLE,
        compiler_params=PARAMS,
        cost_estimate=SMALL,
    )(*after, *in_vmem(*pieces))


def local_kernel(coefs, turn, core, *refs):
    inputs, rest = refs[:6], refs[7:]
    outputs = rest[-3:]

    @pl.when(lax.axis_index("core") == core)
    def _():
        local_heads(coefs, turn, *inputs, *outputs)

    if len(rest) > 3:

        @pl.when(lax.axis_index("core") != core)
        def _():
            for ref, out_ref in zip(rest, outputs):
                out_ref[...] = ref[...]


def local_heads(
    coefs, turn, length_ref, back_ref, query_ref, key_ref, value_ref, weight_ref, local_ref, *read_refs
):
    tokens = query_ref.shape[0]
    first = core_heads()[turn]
    heads = local_ref.shape[1] // HEAD_DIM
    key_at = lax.broadcasted_iota(jnp.int32, (tokens, tokens), 0)
    query_at = lax.broadcasted_iota(jnp.int32, (tokens, tokens), 1)
    start = jnp.int32(0)
    floor = jnp.zeros((tokens, tokens), jnp.int32)
    for k in range(length_ref.shape[1]):
        lowest = jnp.maximum(start - back_ref[0, k], 0)
        floor = jnp.where(query_at >= start, lowest, floor)
        start = start + length_ref[0, k]
    hidden = jnp.where((key_at <= query_at) & (key_at >= floor), 0.0, -jnp.inf).astype(F32)
    scale = math.log2(math.e) / math.sqrt(HEAD_DIM)
    ones = jnp.full((HEAD_DIM, HEAD_DIM), 1.0 / HEAD_DIM, BF16)
    half = HEADS // 2
    by_slot = []
    for slot_coefs in coefs(lax.axis_index("frame")):
        total = None
        for level, coef in slot_coefs:
            term = weight_ref[1 + level, pl.ds(first, heads), :] * coef
            total = term if total is None else total + term
        by_slot.append(total)
    pad = -len(by_slot) * heads % HEAD_DIM
    gains = jnp.concatenate(by_slot + [jnp.zeros((pad, tokens), F32)], 0).T

    def scores_of(h):
        at = columns(first + h)
        return lax.dot_general(
            key_ref[:, at], query_ref[:, at], (((1,), (1,)), ((), ())), preferred_element_type=F32
        )

    upcoming = scores_of(0)
    for h in range(heads):
        scores = upcoming * scale + hidden
        if h + 1 < heads:
            upcoming = scores_of(h + 1)
        weights = jnp.exp2(scores - jnp.max(scores, 0, keepdims=True))
        total = jnp.sum(weights, 0, keepdims=True)
        weights = weights * (weight_ref[0, pl.ds(first + h, 1), :] / total)
        at = slice(h * HEAD_DIM, (h + 1) * HEAD_DIM)
        local_ref[:, at] = lax.dot_general(
            weights.astype(BF16),
            value_ref[:, columns(first + h)],
            (((0,), (0,)), ((), ())),
            preferred_element_type=F32,
        )
        query = query_ref[:, columns(first + h)].astype(F32)
        mean = jnp.dot((query * query).astype(BF16), ones, preferred_element_type=F32)
        query = query * lax.rsqrt(mean + EPSILON)
        for slot, read_ref in enumerate(read_refs):
            which = slot * heads + h
            read_ref[:, at] = (query * gains[:, which : which + 1]).astype(BF16)


def local_part(
    coefs, frame_len, window_back, queries, keys, values, weights, turn, core, after, earlier=()
):
    tokens, width = queries.shape
    width //= 2
    return pl.pallas_call(
        functools.partial(local_kernel, coefs, turn, core),
        out_shape=[pltpu.VMEM((tokens, width), F32)] + [pltpu.VMEM((tokens, width), BF16)] * 2,
        in_specs=[SCALARS] * 2 + [WHOLE] * 4 + [ANYWHERE] + [WHOLE] * len(earlier),
        out_specs=[WHOLE] * 3,
        compiler_params=PARAMS,
        cost_estimate=pl.CostEstimate(
            flops=4 * tokens * tokens * width,
            bytes_accessed=14 * tokens * width,
            transcendentals=tokens * width,
        ),
    )(frame_len, window_back, queries, *in_vmem(keys, values), weights, after, *in_vmem(*earlier))


def read_heads(d, chips, base_ref, states):
    count = HEADS // 2 // chips
    first = (lax.axis_index("chip") ^ d) * count
    for h in range(count):
        at = columns(first + h)
        result = base_ref[:, at]
        for read_ref, state_ref, row in states:
            result = result + jnp.dot(
                read_ref[:, at],
                state_ref[row + h * HEAD_DIM : row + (h + 1) * HEAD_DIM, :],
                preferred_element_type=F32,
            )
        yield at, result


def middle_kernel(chips, early, local_ref, x_ref, y_ref, state_ref, out_ref):
    rows = state_ref.shape[0] // (chips + early)
    for d in range(chips):
        states = [(x_ref, state_ref, d * rows)]
        if d < early:
            states.append((y_ref, state_ref, (chips + d) * rows))
        for at, result in read_heads(d, chips, local_ref, states):
            out_ref[:, at] = result


def read_middle(chips, early, local, x, y, states):
    return pl.pallas_call(
        functools.partial(middle_kernel, chips, early),
        out_shape=pltpu.VMEM(local.shape, F32),
        in_specs=[WHOLE] * 4,
        out_specs=WHOLE,
        compiler_params=PARAMS,
        cost_estimate=SMALL,
    )(*in_vmem(local, x, y, states))


def late_kernel(turn, chips, early, base_ref, y_ref, *refs):
    *state_refs, out_ref, held, sems = refs
    rows = base_ref.shape[1] // chips
    half = core_heads()[turn]
    copies = []
    for d in range(chips):
        states = [(y_ref, state_refs[0], (d - early) * rows)] if d >= early else []
        for at, result in read_heads(d, chips, base_ref, states):
            held[:, at] = result.astype(BF16)
        count = HEADS // 2 // chips
        first = (lax.axis_index("chip") ^ d) * count
        copies.append(
            pltpu.make_async_copy(
                held.at[:, columns(first, count)], out_ref.at[:, columns(half + first, count)], sems.at[d]
            )
        )
        copies[-1].start()
    for copy in copies:
        copy.wait()


def aliased_kernel(turn, chips, early, out_before_ref, *refs):
    late_kernel(turn, chips, early, *refs)


def write_late(turn, chips, early, base, y, states, out=None):
    tokens, width = base.shape
    before = [] if out is None else [out]
    kernel = late_kernel if out is None else aliased_kernel
    return pl.pallas_call(
        functools.partial(kernel, turn, chips, early),
        out_shape=jax.ShapeDtypeStruct((tokens, 2 * width), BF16),
        in_specs=[ANYWHERE] * len(before) + [WHOLE] * (2 + len(states)),
        out_specs=ANYWHERE,
        input_output_aliases={0: 0} if before else {},
        scratch_shapes=[pltpu.VMEM((tokens, width), BF16), pltpu.SemaphoreType.DMA((chips,))],
        compiler_params=PARAMS,
        cost_estimate=SMALL if before else LARGE,
    )(*before, *in_vmem(base, y, *states))


def swap(array, axis, mask, size):
    return lax.ppermute(array, axis, [(n, n ^ mask) for n in range(size)])


def body(sizes, queries, keys, values, level_weight, frame_len, window_back):
    frames, outer, chips = sizes
    low, high = (
        1.0 / math.sqrt(HEAD_DIM * 2**level * queries.shape[0] * outer * chips * 2) for level in (0, 1)
    )

    def coefs(f):
        x_low = jnp.where(f % 2 == 1, low, 0.0)
        x_high = jnp.where(f == 2, high, 0.0)
        return [[(0, x_low), (1, x_high)], [(1, jnp.where(f == 3, high, 0.0))]]

    early = 1

    outgoing, keys, values = outgoing_state(keys, values)
    incoming = swap(outgoing, "core", 1, 2)
    mine = own_state(keys, values)
    local = functools.partial(
        local_part, coefs, frame_len, window_back, queries, keys, values, level_weight
    )
    first = [local(turn, 0, mine) for turn in range(2)]
    own, *sends = chip_pieces([array for part in first for array in part[:1]], mine, incoming, chips)
    got = [swap(sends[d - 1], "chip", d, chips) for d in reversed(range(1, chips))]
    local_0, x_0, y_0 = local(0, 1, own, first[0])
    state = sum_pieces(local_0, own, got, F32 if outer > 1 else BF16)
    if outer > 1:
        state = lax.psum(state, "outer").astype(BF16)
    local_1, x_1, y_1 = local(1, 1, state, first[1])
    shifted = lax.ppermute(state, "frame", [(f, (f + 1) % frames) for f in range(frames)])
    slot = choose_slot(local_1, shifted, swap(state, "frame", 2, frames))

    x = [slot] + [swap(slot, "chip", d, chips) for d in range(1, chips)]
    y = [swap(slot, "frame", 1, frames)]
    y += [swap(piece, "frame", 1, frames) for piece in x[1:]]
    places = [0, *range(chips + early - 1, 2, -1), *range(1, min(3, chips + early))]
    own_states = pack(x + y[:early], places, [local_1])
    other_states = swap(own_states, "core", 1, 2)
    base_0 = read_middle(chips, early, local_0, x_0, y_0, own_states)
    base_1 = read_middle(chips, early, local_1, x_1, y_1, other_states)
    late = y[early:]
    late_own = [pack(late, list(range(len(late))), [])] if late else []
    late_other = [swap(piece, "core", 1, 2) for piece in late_own]
    out = write_late(0, chips, early, base_0, y_0, late_own)
    return write_late(1, chips, early, base_1, y_1, late_other, out)


def solution(mesh):
    frames, space = mesh.shape["frame"], mesh.shape["space"]
    chips = 1
    while HEADS % (chips * 4) == 0 and space % (chips * 4) == 0 and chips < 4:
        chips *= 2
    sizes = (frames, space // (2 * chips), chips)
    names = ("frame", "outer", "chip", "core")
    fine = Mesh(mesh.devices.reshape(sizes + (2,)), names)
    rows = P(names, None)
    return jax.shard_map(
        functools.partial(body, sizes),
        mesh=fine,
        in_specs=(rows, rows, rows, P(None, None, names), rows, rows),
        out_specs=rows,
        check_vma=False,
    )
```

```python
import functools
import math

import jax
import jax.numpy as jnp
from jax import lax
from jax.experimental import pallas as pl
from jax.experimental.pallas import tpu as pltpu
from jax.sharding import Mesh, PartitionSpec as P

HEADS = 24
HEAD_DIM = 128
EPSILON = 1e-06
VMEM_LIMIT = 40 * 1024 * 1024

F32, BF16 = jnp.float32, jnp.bfloat16
WHOLE = pl.BlockSpec(memory_space=pltpu.VMEM)
SCALARS = pl.BlockSpec(memory_space=pltpu.SMEM)
ANYWHERE = pl.BlockSpec(memory_space=pl.ANY)
IN_HBM = pl.BlockSpec(memory_space=pltpu.HBM)
SMALL = pl.CostEstimate(flops=1024, bytes_accessed=1024, transcendentals=0)
LARGE = pl.CostEstimate(flops=2 * 10**10, bytes_accessed=1024, transcendentals=0)
PARAMS = pltpu.CompilerParams(vmem_limit_bytes=VMEM_LIMIT)


def inverse_rms(rows):
    return lax.rsqrt(jnp.mean(rows * rows, -1, keepdims=True) + EPSILON)


def columns(head, count=1):
    return pl.ds(pl.multiple_of(head * HEAD_DIM, HEAD_DIM), count * HEAD_DIM)


def core_heads():
    core = lax.axis_index("core")
    return core * (HEADS // 2), (1 - core) * (HEADS // 2)


def in_vmem(*arrays):
    return [pltpu.with_memory_space_constraint(array, pltpu.VMEM) for array in arrays]


def states_of(first, keys, values, out_ref, ready=lambda h: None):
    for h in range(out_ref.shape[0] // HEAD_DIM):
        ready(h)
        at = columns(first + h)
        key_rows = keys[:, at].astype(F32)
        normal = (key_rows * inverse_rms(key_rows)).astype(BF16)
        state = lax.dot_general(
            normal, values[:, at], (((0,), (0,)), ((), ())), preferred_element_type=F32
        )
        out_ref[h * HEAD_DIM : (h + 1) * HEAD_DIM, :] = state.astype(out_ref.dtype)


def first_kernel(parts, key_ref, value_ref, out_ref, keys, values, sems):
    mine, other = core_heads()
    half = HEADS // 2
    starts = [(other + h, half // parts) for h in range(0, half, half // parts)] + [(mine, half)]
    copies = []
    for n, (first, heads) in enumerate(starts):
        at = columns(first, heads)
        pair = [
            pltpu.make_async_copy(ref.at[:, at], held.at[:, at], sems.at[n, s])
            for s, (ref, held) in enumerate(((key_ref, keys), (value_ref, values)))
        ]
        for copy in pair:
            copy.start()
        copies.append(pair)

    def ready(h):
        if h % (half // parts) == 0:
            for copy in copies[h // (half // parts)]:
                copy.wait()

    states_of(other, keys, values, out_ref, ready)
    for copy in copies[-1]:
        copy.wait()


def outgoing_state(keys, values):
    dim, half = HEAD_DIM, HEADS // 2
    rows, parts = keys.shape[0], 1
    keys, values = (pltpu.with_memory_space_constraint(x, pltpu.HBM) for x in (keys, values))
    return pl.pallas_call(
        functools.partial(first_kernel, parts),
        out_shape=[pltpu.VMEM((half * dim, dim), BF16)] + [pltpu.VMEM(keys.shape, BF16)] * 2,
        in_specs=[IN_HBM, IN_HBM],
        out_specs=[WHOLE] * 3,
        scratch_shapes=[pltpu.SemaphoreType.DMA((parts + 1, 2))],
        compiler_params=PARAMS,
        cost_estimate=pl.CostEstimate(
            flops=2 * half * rows * dim * dim, bytes_accessed=8 * half * rows * dim, transcendentals=0
        ),
    )(keys, values)


def own_kernel(key_ref, value_ref, out_ref):
    states_of(core_heads()[0], key_ref, value_ref, out_ref)


def own_state(keys, values):
    dim, half = HEAD_DIM, HEADS // 2
    rows = keys.shape[0]
    return pl.pallas_call(
        own_kernel,
        out_shape=pltpu.VMEM((half * dim, dim), F32),
        in_specs=[WHOLE, WHOLE],
        out_specs=WHOLE,
        compiler_params=PARAMS,
        cost_estimate=pl.CostEstimate(
            flops=2 * half * rows * dim * dim, bytes_accessed=8 * half * rows * dim, transcendentals=0
        ),
    )(*in_vmem(keys, values))


def piece_kernel(mine_ref, other_ref, own_ref, *piece_refs):
    chip = lax.axis_index("chip")
    rows = own_ref.shape[0]
    for d, ref in enumerate((own_ref,) + piece_refs):
        at = pl.ds(pl.multiple_of((chip ^ d) * rows, rows), rows)
        ref[...] = (mine_ref[at, :] + other_ref[at, :].astype(F32)).astype(ref.dtype)


def chip_pieces(mine, other, chips):
    shape = (mine.shape[0] // chips, HEAD_DIM)
    return pl.pallas_call(
        piece_kernel,
        out_shape=[pltpu.VMEM(shape, F32)] + [pltpu.VMEM(shape, BF16)] * (chips - 1),
        in_specs=[WHOLE, WHOLE],
        out_specs=[WHOLE] * chips,
        compiler_params=PARAMS,
        cost_estimate=SMALL,
    )(*in_vmem(mine, other))


def sum_kernel(after_ref, own_ref, *refs):
    total = own_ref[...]
    for ref in refs[:-1]:
        total = total + ref[...].astype(F32)
    refs[-1][...] = total.astype(refs[-1].dtype)


def sum_pieces(after, own, parts, dtype):
    return pl.pallas_call(
        sum_kernel,
        out_shape=pltpu.VMEM(own.shape, dtype),
        in_specs=[ANYWHERE] + [WHOLE] * (1 + len(parts)),
        out_specs=WHOLE,
        compiler_params=PARAMS,
        cost_estimate=SMALL,
    )(after, *in_vmem(own, *parts))


def slot_kernel(after_ref, before_ref, first_ref, out_ref):
    before = before_ref[...].astype(F32)
    both = first_ref[...].astype(F32) + before
    out_ref[...] = jnp.where(lax.axis_index("frame") == 2, both, before).astype(BF16)


def choose_slot(after, before, first):
    return pl.pallas_call(
        slot_kernel,
        out_shape=pltpu.VMEM(before.shape, BF16),
        in_specs=[ANYWHERE] + [WHOLE] * 2,
        out_specs=WHOLE,
        compiler_params=PARAMS,
        cost_estimate=SMALL,
    )(after, *in_vmem(before, first))


def pack_kernel(after, order, *refs):
    out_ref, refs = refs[-1], refs[after:-1]
    rows = refs[0].shape[0]
    for place, ref in zip(order, refs):
        out_ref[place * rows : (place + 1) * rows, :] = ref[...]


def pack(pieces, order, after):
    rows = sum(array.shape[0] for array in pieces)
    pieces = [pieces[place] for place in order]
    return pl.pallas_call(
        functools.partial(pack_kernel, len(after), order),
        out_shape=pltpu.VMEM((rows, HEAD_DIM), BF16),
        in_specs=[ANYWHERE] * len(after) + [WHOLE] * len(pieces),
        out_specs=WHOLE,
        compiler_params=PARAMS,
        cost_estimate=SMALL,
    )(*after, *in_vmem(*pieces))


def local_kernel(
    coefs, turn, length_ref, back_ref, query_ref, key_ref, value_ref, weight_ref, after_ref, local_ref, *read_refs
):
    tokens = query_ref.shape[0]
    first = core_heads()[turn]
    heads = local_ref.shape[1] // HEAD_DIM
    key_at = lax.broadcasted_iota(jnp.int32, (tokens, tokens), 0)
    query_at = lax.broadcasted_iota(jnp.int32, (tokens, tokens), 1)
    start = jnp.int32(0)
    floor = jnp.zeros((tokens, tokens), jnp.int32)
    for k in range(length_ref.shape[1]):
        lowest = jnp.maximum(start - back_ref[0, k], 0)
        floor = jnp.where(query_at >= start, lowest, floor)
        start = start + length_ref[0, k]
    hidden = jnp.where((key_at <= query_at) & (key_at >= floor), 0.0, -jnp.inf).astype(F32)
    scale = math.log2(math.e) / math.sqrt(HEAD_DIM)
    ones = jnp.full((HEAD_DIM, HEAD_DIM), 1.0 / HEAD_DIM, BF16)
    half = HEADS // 2
    by_slot = []
    for slot_coefs in coefs(lax.axis_index("frame")):
        total = None
        for level, coef in slot_coefs:
            term = weight_ref[1 + level, pl.ds(first, heads), :] * coef
            total = term if total is None else total + term
        by_slot.append(total)
    pad = -len(by_slot) * heads % HEAD_DIM
    gains = jnp.concatenate(by_slot + [jnp.zeros((pad, tokens), F32)], 0).T

    def scores_of(h):
        at = columns(first + h)
        return lax.dot_general(
            key_ref[:, at], query_ref[:, at], (((1,), (1,)), ((), ())), preferred_element_type=F32
        )

    upcoming = scores_of(0)
    for h in range(heads):
        scores = upcoming * scale + hidden
        if h + 1 < heads:
            upcoming = scores_of(h + 1)
        weights = jnp.exp2(scores - jnp.max(scores, 0, keepdims=True))
        total = jnp.sum(weights, 0, keepdims=True)
        weights = weights * (weight_ref[0, pl.ds(first + h, 1), :] / total)
        at = slice(h * HEAD_DIM, (h + 1) * HEAD_DIM)
        local_ref[:, at] = lax.dot_general(
            weights.astype(BF16),
            value_ref[:, columns(first + h)],
            (((0,), (0,)), ((), ())),
            preferred_element_type=F32,
        )
        query = query_ref[:, columns(first + h)].astype(F32)
        mean = jnp.dot((query * query).astype(BF16), ones, preferred_element_type=F32)
        query = query * lax.rsqrt(mean + EPSILON)
        for slot, read_ref in enumerate(read_refs):
            which = slot * heads + h
            read_ref[:, at] = (query * gains[:, which : which + 1]).astype(BF16)


def local_part(coefs, slots, turn, frame_len, window_back, queries, keys, values, weights, after):
    tokens, width = queries.shape
    width //= 2
    return pl.pallas_call(
        functools.partial(local_kernel, coefs, turn),
        out_shape=[pltpu.VMEM((tokens, width), F32)] + [pltpu.VMEM((tokens, width), BF16)] * slots,
        in_specs=[SCALARS] * 2 + [WHOLE] * 4 + [ANYWHERE],
        out_specs=[WHOLE] * (1 + slots),
        compiler_params=PARAMS,
        cost_estimate=pl.CostEstimate(
            flops=4 * tokens * tokens * width,
            bytes_accessed=14 * tokens * width,
            transcendentals=tokens * width,
        ),
    )(frame_len, window_back, queries, *in_vmem(keys, values), weights, after)


def read_heads(d, chips, base_ref, states):
    count = HEADS // 2 // chips
    first = (lax.axis_index("chip") ^ d) * count
    for h in range(count):
        at = columns(first + h)
        result = base_ref[:, at]
        for read_ref, state_ref, row in states:
            result = result + jnp.dot(
                read_ref[:, at],
                state_ref[row + h * HEAD_DIM : row + (h + 1) * HEAD_DIM, :],
                preferred_element_type=F32,
            )
        yield at, result


def middle_kernel(chips, early, local_ref, x_ref, y_ref, state_ref, out_ref):
    rows = state_ref.shape[0] // (chips + early)
    for d in range(chips):
        states = [(x_ref, state_ref, d * rows)]
        if d < early:
            states.append((y_ref, state_ref, (chips + d) * rows))
        for at, result in read_heads(d, chips, local_ref, states):
            out_ref[:, at] = result


def read_middle(cost, chips, early, local, x, y, states):
    return pl.pallas_call(
        functools.partial(middle_kernel, chips, early),
        out_shape=pltpu.VMEM(local.shape, F32),
        in_specs=[WHOLE] * 4,
        out_specs=WHOLE,
        compiler_params=PARAMS,
        cost_estimate=cost,
    )(*in_vmem(local, x, y, states))


def late_kernel(turn, chips, early, base_ref, y_ref, *refs):
    *state_refs, out_ref, held, sems = refs
    rows = base_ref.shape[1] // chips
    half = core_heads()[turn]
    copies = []
    for d in range(chips):
        states = []
        if d >= early:
            ref = state_refs[0] if d < chips - 1 else state_refs[-1]
            states.append((y_ref, ref, (d - early) * rows if d < chips - 1 else 0))
        for at, result in read_heads(d, chips, base_ref, states):
            held[:, at] = result.astype(BF16)
        count = HEADS // 2 // chips
        first = (lax.axis_index("chip") ^ d) * count
        copies.append(
            pltpu.make_async_copy(
                held.at[:, columns(first, count)], out_ref.at[:, columns(half + first, count)], sems.at[d]
            )
        )
        copies[-1].start()
    for copy in copies:
        copy.wait()


def aliased_kernel(turn, chips, early, out_before_ref, *refs):
    late_kernel(turn, chips, early, *refs)


def write_late(turn, chips, early, base, y, states, out=None):
    tokens, width = base.shape
    before = [] if out is None else [out]
    kernel = late_kernel if out is None else aliased_kernel
    return pl.pallas_call(
        functools.partial(kernel, turn, chips, early),
        out_shape=jax.ShapeDtypeStruct((tokens, 2 * width), BF16),
        in_specs=[ANYWHERE] * len(before) + [WHOLE] * (2 + len(states)),
        out_specs=ANYWHERE,
        input_output_aliases={0: 0} if before else {},
        scratch_shapes=[pltpu.VMEM((tokens, width), BF16), pltpu.SemaphoreType.DMA((chips,))],
        compiler_params=PARAMS,
        cost_estimate=SMALL if before else LARGE,
    )(*before, *in_vmem(base, y, *states))


def swap(array, axis, mask, size):
    return lax.ppermute(array, axis, [(n, n ^ mask) for n in range(size)])


def body(sizes, queries, keys, values, level_weight, frame_len, window_back):
    frames, outer, chips = sizes
    low, high = (
        1.0 / math.sqrt(HEAD_DIM * 2**level * queries.shape[0] * outer * chips * 2) for level in (0, 1)
    )

    def coefs(f):
        x_low = jnp.where(f % 2 == 1, low, 0.0)
        x_high = jnp.where(f == 2, high, 0.0)
        return [[(0, x_low), (1, x_high)], [(1, jnp.where(f == 3, high, 0.0))]]

    local = functools.partial(local_part, coefs, 2)
    rest = (frame_len, window_back, queries)
    early = 1

    order = [*range(2, chips), *range(1, min(2, chips))]

    outgoing, keys, values = outgoing_state(keys, values)
    incoming = swap(outgoing, "core", 1, 2)
    mine = own_state(keys, values)
    own, *sends = chip_pieces(mine, incoming, chips)
    got = [swap(sends[d - 1], "chip", d, chips) for d in order]
    local_0, x_0, y_0 = local(0, *rest, keys, values, level_weight, own)
    state = sum_pieces(local_0, own, got, F32 if outer > 1 else BF16)
    if outer > 1:
        state = lax.psum(state, "outer").astype(BF16)
    local_1, x_1, y_1 = local(1, *rest, keys, values, level_weight, state)
    shifted = lax.ppermute(state, "frame", [(f, (f + 1) % frames) for f in range(frames)])
    slot = choose_slot(local_1, shifted, swap(state, "frame", 2, frames))

    x = [slot] + [swap(slot, "chip", d, chips) for d in range(1, chips)]
    y = [swap(slot, "frame", 1, frames)]
    y += [swap(piece, "frame", 1, frames) for piece in x[1:]]
    places = [0, *range(chips + early - 1, 2, -1), *range(1, min(3, chips + early))]
    own_states = pack(x + y[:early], places, [local_1])
    other_states = swap(own_states, "core", 1, 2)
    base_0 = read_middle(SMALL, chips, early, local_0, x_0, y_0, own_states)
    base_1 = read_middle(LARGE, chips, early, local_1, x_1, y_1, other_states)
    late_own = [pack(y[early:-1], list(range(chips - 1 - early)), [])] if chips - 1 > early else []
    late_other = [swap(piece, "core", 1, 2) for piece in late_own]
    if chips > early:
        last = y[-1]
        late_own.append(last)
        late_other.append(swap(last, "core", 1, 2))
    out = write_late(0, chips, early, base_0, y_0, late_own)
    return write_late(1, chips, early, base_1, y_1, late_other, out)


def solution(mesh):
    frames, space = mesh.shape["frame"], mesh.shape["space"]
    chips = 1
    while HEADS % (chips * 4) == 0 and space % (chips * 4) == 0 and chips < 4:
        chips *= 2
    sizes = (frames, space // (2 * chips), chips)
    names = ("frame", "outer", "chip", "core")
    fine = Mesh(mesh.devices.reshape(sizes + (2,)), names)
    rows = P(names, None)
    return jax.shard_map(
        functools.partial(body, sizes),
        mesh=fine,
        in_specs=(rows, rows, rows, P(None, None, names), rows, rows),
        out_specs=rows,
        check_vma=False,
    )
```

```python
import functools
import math

import jax
import jax.numpy as jnp
from jax import lax
from jax.experimental import pallas as pl
from jax.experimental.pallas import tpu as pltpu
from jax.sharding import Mesh, PartitionSpec as P

HEADS = 24
HEAD_DIM = 128
EPSILON = 1e-06
VMEM_LIMIT = 40 * 1024 * 1024

F32, BF16 = jnp.float32, jnp.bfloat16
WHOLE = pl.BlockSpec(memory_space=pltpu.VMEM)
SCALARS = pl.BlockSpec(memory_space=pltpu.SMEM)
ANYWHERE = pl.BlockSpec(memory_space=pl.ANY)
IN_HBM = pl.BlockSpec(memory_space=pltpu.HBM)
SMALL = pl.CostEstimate(flops=1024, bytes_accessed=1024, transcendentals=0)
LARGE = pl.CostEstimate(flops=2 * 10**10, bytes_accessed=1024, transcendentals=0)
PARAMS = pltpu.CompilerParams(vmem_limit_bytes=VMEM_LIMIT)


def inverse_rms(rows):
    return lax.rsqrt(jnp.mean(rows * rows, -1, keepdims=True) + EPSILON)


def columns(head, count=1):
    return pl.ds(pl.multiple_of(head * HEAD_DIM, HEAD_DIM), count * HEAD_DIM)


def core_heads():
    core = lax.axis_index("core")
    return core * (HEADS // 2), (1 - core) * (HEADS // 2)


def in_vmem(*arrays):
    return [pltpu.with_memory_space_constraint(array, pltpu.VMEM) for array in arrays]


def states_of(first, keys, values, out_ref, ready=lambda h: None):
    for h in range(out_ref.shape[0] // HEAD_DIM):
        ready(h)
        at = columns(first + h)
        key_rows = keys[:, at].astype(F32)
        normal = (key_rows * inverse_rms(key_rows)).astype(BF16)
        state = lax.dot_general(
            normal, values[:, at], (((0,), (0,)), ((), ())), preferred_element_type=F32
        )
        out_ref[h * HEAD_DIM : (h + 1) * HEAD_DIM, :] = state.astype(out_ref.dtype)


def first_kernel(parts, key_ref, value_ref, out_ref, keys, values, sems):
    mine, other = core_heads()
    half = HEADS // 2
    starts = [(other + h, half // parts) for h in range(0, half, half // parts)] + [(mine, half)]
    copies = []
    for n, (first, heads) in enumerate(starts):
        at = columns(first, heads)
        pair = [
            pltpu.make_async_copy(ref.at[:, at], held.at[:, at], sems.at[n, s])
            for s, (ref, held) in enumerate(((key_ref, keys), (value_ref, values)))
        ]
        for copy in pair:
            copy.start()
        copies.append(pair)

    def ready(h):
        if h % (half // parts) == 0:
            for copy in copies[h // (half // parts)]:
                copy.wait()

    states_of(other, keys, values, out_ref, ready)
    for copy in copies[-1]:
        copy.wait()


def outgoing_state(keys, values):
    dim, half = HEAD_DIM, HEADS // 2
    rows, parts = keys.shape[0], 1
    keys, values = (pltpu.with_memory_space_constraint(x, pltpu.HBM) for x in (keys, values))
    return pl.pallas_call(
        functools.partial(first_kernel, parts),
        out_shape=[pltpu.VMEM((half * dim, dim), BF16)] + [pltpu.VMEM(keys.shape, BF16)] * 2,
        in_specs=[IN_HBM, IN_HBM],
        out_specs=[WHOLE] * 3,
        scratch_shapes=[pltpu.SemaphoreType.DMA((parts + 1, 2))],
        compiler_params=PARAMS,
        cost_estimate=pl.CostEstimate(
            flops=2 * half * rows * dim * dim, bytes_accessed=8 * half * rows * dim, transcendentals=0
        ),
    )(keys, values)


def own_kernel(key_ref, value_ref, out_ref):
    states_of(core_heads()[0], key_ref, value_ref, out_ref)


def own_state(keys, values):
    dim, half = HEAD_DIM, HEADS // 2
    rows = keys.shape[0]
    return pl.pallas_call(
        own_kernel,
        out_shape=pltpu.VMEM((half * dim, dim), F32),
        in_specs=[WHOLE, WHOLE],
        out_specs=WHOLE,
        compiler_params=PARAMS,
        cost_estimate=pl.CostEstimate(
            flops=2 * half * rows * dim * dim, bytes_accessed=8 * half * rows * dim, transcendentals=0
        ),
    )(*in_vmem(keys, values))


def piece_kernel(mine_ref, other_ref, own_ref, *piece_refs):
    chip = lax.axis_index("chip")
    rows = own_ref.shape[0]
    for d, ref in enumerate((own_ref,) + piece_refs):
        at = pl.ds(pl.multiple_of((chip ^ d) * rows, rows), rows)
        ref[...] = (mine_ref[at, :] + other_ref[at, :].astype(F32)).astype(ref.dtype)


def chip_pieces(mine, other, chips):
    shape = (mine.shape[0] // chips, HEAD_DIM)
    return pl.pallas_call(
        piece_kernel,
        out_shape=[pltpu.VMEM(shape, F32)] + [pltpu.VMEM(shape, BF16)] * (chips - 1),
        in_specs=[WHOLE, WHOLE],
        out_specs=[WHOLE] * chips,
        compiler_params=PARAMS,
        cost_estimate=SMALL,
    )(*in_vmem(mine, other))


def sum_kernel(after_ref, own_ref, *refs):
    total = own_ref[...]
    for ref in refs[:-1]:
        total = total + ref[...].astype(F32)
    refs[-1][...] = total.astype(refs[-1].dtype)


def sum_pieces(after, own, parts, dtype):
    return pl.pallas_call(
        sum_kernel,
        out_shape=pltpu.VMEM(own.shape, dtype),
        in_specs=[ANYWHERE] + [WHOLE] * (1 + len(parts)),
        out_specs=WHOLE,
        compiler_params=PARAMS,
        cost_estimate=SMALL,
    )(after, *in_vmem(own, *parts))


def slot_kernel(after_ref, before_ref, first_ref, out_ref):
    before = before_ref[...].astype(F32)
    both = first_ref[...].astype(F32) + before
    out_ref[...] = jnp.where(lax.axis_index("frame") == 2, both, before).astype(BF16)


def choose_slot(after, before, first):
    return pl.pallas_call(
        slot_kernel,
        out_shape=pltpu.VMEM(before.shape, BF16),
        in_specs=[ANYWHERE] + [WHOLE] * 2,
        out_specs=WHOLE,
        compiler_params=PARAMS,
        cost_estimate=SMALL,
    )(after, *in_vmem(before, first))


def pack_kernel(after, order, *refs):
    out_ref, refs = refs[-1], refs[after:-1]
    rows = refs[0].shape[0]
    for place, ref in zip(order, refs):
        out_ref[place * rows : (place + 1) * rows, :] = ref[...]


def pack(pieces, order, after):
    rows = sum(array.shape[0] for array in pieces)
    pieces = [pieces[place] for place in order]
    return pl.pallas_call(
        functools.partial(pack_kernel, len(after), order),
        out_shape=pltpu.VMEM((rows, HEAD_DIM), BF16),
        in_specs=[ANYWHERE] * len(after) + [WHOLE] * len(pieces),
        out_specs=WHOLE,
        compiler_params=PARAMS,
        cost_estimate=SMALL,
    )(*after, *in_vmem(*pieces))


def local_kernel(
    coefs, turn, length_ref, back_ref, query_ref, key_ref, value_ref, weight_ref, after_ref, local_ref, *read_refs
):
    tokens = query_ref.shape[0]
    first = core_heads()[turn]
    heads = local_ref.shape[1] // HEAD_DIM
    key_at = lax.broadcasted_iota(jnp.int32, (tokens, tokens), 0)
    query_at = lax.broadcasted_iota(jnp.int32, (tokens, tokens), 1)
    start = jnp.int32(0)
    floor = jnp.zeros((tokens, tokens), jnp.int32)
    for k in range(length_ref.shape[1]):
        lowest = jnp.maximum(start - back_ref[0, k], 0)
        floor = jnp.where(query_at >= start, lowest, floor)
        start = start + length_ref[0, k]
    hidden = jnp.where((key_at <= query_at) & (key_at >= floor), 0.0, -jnp.inf).astype(F32)
    scale = math.log2(math.e) / math.sqrt(HEAD_DIM)
    ones = jnp.full((HEAD_DIM, HEAD_DIM), 1.0 / HEAD_DIM, BF16)
    half = HEADS // 2
    by_slot = []
    for slot_coefs in coefs(lax.axis_index("frame")):
        total = None
        for level, coef in slot_coefs:
            term = weight_ref[1 + level, pl.ds(first, heads), :] * coef
            total = term if total is None else total + term
        by_slot.append(total)
    pad = -len(by_slot) * heads % HEAD_DIM
    gains = jnp.concatenate(by_slot + [jnp.zeros((pad, tokens), F32)], 0).T

    def scores_of(h):
        at = columns(first + h)
        return lax.dot_general(
            key_ref[:, at], query_ref[:, at], (((1,), (1,)), ((), ())), preferred_element_type=F32
        )

    upcoming = scores_of(0)
    for h in range(heads):
        scores = upcoming * scale + hidden
        if h + 1 < heads:
            upcoming = scores_of(h + 1)
        weights = jnp.exp2(scores - jnp.max(scores, 0, keepdims=True))
        total = jnp.sum(weights, 0, keepdims=True)
        weights = weights * (weight_ref[0, pl.ds(first + h, 1), :] / total)
        at = slice(h * HEAD_DIM, (h + 1) * HEAD_DIM)
        local_ref[:, at] = lax.dot_general(
            weights.astype(BF16),
            value_ref[:, columns(first + h)],
            (((0,), (0,)), ((), ())),
            preferred_element_type=F32,
        )
        query = query_ref[:, columns(first + h)].astype(F32)
        mean = jnp.dot((query * query).astype(BF16), ones, preferred_element_type=F32)
        query = query * lax.rsqrt(mean + EPSILON)
        for slot, read_ref in enumerate(read_refs):
            which = slot * heads + h
            read_ref[:, at] = (query * gains[:, which : which + 1]).astype(BF16)


def local_part(coefs, slots, turn, frame_len, window_back, queries, keys, values, weights, after):
    tokens, width = queries.shape
    width //= 2
    return pl.pallas_call(
        functools.partial(local_kernel, coefs, turn),
        out_shape=[pltpu.VMEM((tokens, width), F32)] + [pltpu.VMEM((tokens, width), BF16)] * slots,
        in_specs=[SCALARS] * 2 + [WHOLE] * 4 + [ANYWHERE],
        out_specs=[WHOLE] * (1 + slots),
        compiler_params=PARAMS,
        cost_estimate=pl.CostEstimate(
            flops=4 * tokens * tokens * width,
            bytes_accessed=14 * tokens * width,
            transcendentals=tokens * width,
        ),
    )(frame_len, window_back, queries, *in_vmem(keys, values), weights, after)


def read_heads(d, chips, base_ref, states):
    count = HEADS // 2 // chips
    first = (lax.axis_index("chip") ^ d) * count
    for h in range(count):
        at = columns(first + h)
        result = base_ref[:, at]
        for read_ref, state_ref, row in states:
            result = result + jnp.dot(
                read_ref[:, at],
                state_ref[row + h * HEAD_DIM : row + (h + 1) * HEAD_DIM, :],
                preferred_element_type=F32,
            )
        yield at, result


def middle_kernel(chips, early, local_ref, x_ref, y_ref, state_ref, out_ref):
    rows = state_ref.shape[0] // (chips + early)
    for d in range(chips):
        states = [(x_ref, state_ref, d * rows)]
        if d < early:
            states.append((y_ref, state_ref, (chips + d) * rows))
        for at, result in read_heads(d, chips, local_ref, states):
            out_ref[:, at] = result


def read_middle(cost, chips, early, local, x, y, states):
    return pl.pallas_call(
        functools.partial(middle_kernel, chips, early),
        out_shape=pltpu.VMEM(local.shape, F32),
        in_specs=[WHOLE] * 4,
        out_specs=WHOLE,
        compiler_params=PARAMS,
        cost_estimate=cost,
    )(*in_vmem(local, x, y, states))


def late_kernel(turn, chips, early, base_ref, y_ref, *refs):
    *state_refs, out_ref, held, sems = refs
    rows = base_ref.shape[1] // chips
    half = core_heads()[turn]
    copies = []
    for d in range(chips):
        states = []
        if d >= early:
            ref = state_refs[0] if d < chips - 1 else state_refs[-1]
            states.append((y_ref, ref, (d - early) * rows if d < chips - 1 else 0))
        for at, result in read_heads(d, chips, base_ref, states):
            held[:, at] = result.astype(BF16)
        count = HEADS // 2 // chips
        first = (lax.axis_index("chip") ^ d) * count
        copies.append(
            pltpu.make_async_copy(
                held.at[:, columns(first, count)], out_ref.at[:, columns(half + first, count)], sems.at[d]
            )
        )
        copies[-1].start()
    for copy in copies:
        copy.wait()


def aliased_kernel(turn, chips, early, out_before_ref, *refs):
    late_kernel(turn, chips, early, *refs)


def write_late(turn, chips, early, base, y, states, out=None):
    tokens, width = base.shape
    before = [] if out is None else [out]
    kernel = late_kernel if out is None else aliased_kernel
    return pl.pallas_call(
        functools.partial(kernel, turn, chips, early),
        out_shape=jax.ShapeDtypeStruct((tokens, 2 * width), BF16),
        in_specs=[ANYWHERE] * len(before) + [WHOLE] * (2 + len(states)),
        out_specs=ANYWHERE,
        input_output_aliases={0: 0} if before else {},
        scratch_shapes=[pltpu.VMEM((tokens, width), BF16), pltpu.SemaphoreType.DMA((chips,))],
        compiler_params=PARAMS,
        cost_estimate=SMALL if before else LARGE,
    )(*before, *in_vmem(base, y, *states))


def swap(array, axis, mask, size):
    return lax.ppermute(array, axis, [(n, n ^ mask) for n in range(size)])


def body(sizes, queries, keys, values, level_weight, frame_len, window_back):
    frames, outer, chips = sizes
    low, high = (
        1.0 / math.sqrt(HEAD_DIM * 2**level * queries.shape[0] * outer * chips * 2) for level in (0, 1)
    )

    def coefs(f):
        x_low = jnp.where(f % 2 == 1, low, 0.0)
        x_high = jnp.where(f == 2, high, 0.0)
        return [[(0, x_low), (1, x_high)], [(1, jnp.where(f == 3, high, 0.0))]]

    local = functools.partial(local_part, coefs, 2)
    rest = (frame_len, window_back, queries)
    early = 1

    order = [*reversed(range(1, chips))]

    outgoing, keys, values = outgoing_state(keys, values)
    incoming = swap(outgoing, "core", 1, 2)
    mine = own_state(keys, values)
    own, *sends = chip_pieces(mine, incoming, chips)
    got = [swap(sends[d - 1], "chip", d, chips) for d in order]
    local_0, x_0, y_0 = local(0, *rest, keys, values, level_weight, own)
    state = sum_pieces(local_0, own, got, F32 if outer > 1 else BF16)
    if outer > 1:
        state = lax.psum(state, "outer").astype(BF16)
    local_1, x_1, y_1 = local(1, *rest, keys, values, level_weight, state)
    shifted = lax.ppermute(state, "frame", [(f, (f + 1) % frames) for f in range(frames)])
    slot = choose_slot(local_1, shifted, swap(state, "frame", 2, frames))

    x = [slot] + [swap(slot, "chip", d, chips) for d in range(1, chips)]
    y = [swap(slot, "frame", 1, frames)]
    y += [swap(piece, "frame", 1, frames) for piece in x[1:]]
    places = [0, *range(chips + early - 1, 2, -1), *range(1, min(3, chips + early))]
    own_states = pack(x + y[:early], places, [local_1])
    other_states = swap(own_states, "core", 1, 2)
    base_0 = read_middle(SMALL, chips, early, local_0, x_0, y_0, own_states)
    base_1 = read_middle(LARGE, chips, early, local_1, x_1, y_1, other_states)
    late_own = [pack(y[early:-1], list(range(chips - 1 - early)), [])] if chips - 1 > early else []
    late_other = [swap(piece, "core", 1, 2) for piece in late_own]
    if chips > early:
        last = y[-1]
        late_own.append(last)
        late_other.append(swap(last, "core", 1, 2))
    out = write_late(0, chips, early, base_0, y_0, late_own)
    return write_late(1, chips, early, base_1, y_1, late_other, out)


def solution(mesh):
    frames, space = mesh.shape["frame"], mesh.shape["space"]
    chips = 1
    while HEADS % (chips * 4) == 0 and space % (chips * 4) == 0 and chips < 4:
        chips *= 2
    sizes = (frames, space // (2 * chips), chips)
    names = ("frame", "outer", "chip", "core")
    fine = Mesh(mesh.devices.reshape(sizes + (2,)), names)
    rows = P(names, None)
    return jax.shard_map(
        functools.partial(body, sizes),
        mesh=fine,
        in_specs=(rows, rows, rows, P(None, None, names), rows, rows),
        out_specs=rows,
        check_vma=False,
    )
```
